32 devices in a mesh: row: 8 (over z, core), seq: 4 (over y, x).
Axes of the slice: x: 2, y: 2, z: 4, core: 2. Of those that a mesh axis runs over, the one named last changes fastest.
Arguments:
- tokens_in: bfloat16 [24, 1024, 768], P('row', 'seq'), may hold values from -6 to 6
- lengths: int32 [24, 8], P('row'), may hold values from 1 to 1017, as said below
- ln1_gain: float32 [768], replicated, may hold values from 0.1 to 1.9
- ln1_bias: float32 [768], replicated, may hold values from -1.75 to 1.75
- qkv_weight: bfloat16 [768, 2304], replicated, may hold values from -0.21875 to 0.21875
- qv_bias: float32 [1536], replicated, may hold values from -3 to 3
- proj_weight: bfloat16 [768, 768], replicated, may hold values from -3.5 to 3.5
- proj_bias: float32 [768], replicated, may hold values from -3 to 3
- ln2_gain: float32 [768], replicated, may hold values from 0.1 to 1.9
- ln2_bias: float32 [768], replicated, may hold values from -1.75 to 1.75
- fc_weight: bfloat16 [768, 3072], replicated, may hold values from -0.21875 to 0.21875
- fc_bias: float32 [3072], replicated, may hold values from -3 to 3
- out_weight: bfloat16 [3072, 768], replicated, may hold values from -0.4375 to 0.4375
- out_bias: float32 [768], replicated, may hold values from -3 to 3
- cotangent: bfloat16 [24, 1024, 768], P('row', 'seq'), may hold values from -6 to 6
Outputs:
- layer_out: bfloat16 [24, 1024, 768], P('row', 'seq')
- input_grad: float32 [24, 1024, 768], P('row', 'seq')
- ln1_gain_grad: float32 [768], replicated
- ln1_bias_grad: float32 [768], replicated
- qkv_weight_grad: float32 [768, 2304], replicated
- qv_bias_grad: float32 [1536], replicated
- proj_weight_grad: float32 [768, 768], replicated
- proj_bias_grad: float32 [768], replicated
- ln2_gain_grad: float32 [768], replicated
- ln2_bias_grad: float32 [768], replicated
- fc_weight_grad: float32 [768, 3072], replicated
- fc_bias_grad: float32 [3072], replicated
- out_weight_grad: float32 [3072, 768], replicated
- out_bias_grad: float32 [768], replicated
The draws below stay inside these ranges and needn't reach their ends.
Inputs may be any that keep to these rules, and one draw needn't show every extreme that they name: Each row's 8 lengths are positive, sum to at most 1024 and to at least 95 percent of it; the rest of the row is padding.
All inputs are finite; a program needn't handle non-finite values.
Results may differ from the reference program's by a relative error of at most 0.04.
Values may be sent and summed in bfloat16 or wider, within the bound.
A program may use at most 448 MiB of HBM per device.

```python
import jax
import jax.numpy as jnp
from jax import lax

D = 768
HEADS = 12
HEAD = 64
FF = 3072
SPAN = 256
DOCS = 8
SEQ_LEN = 1024
ROWS = 24


def draw_lengths(key, part):
    key = jax.random.fold_in(key, 7)
    key_short, key_big, key_pad = jax.random.split(key, 3)
    short = jax.random.randint(key_short, (ROWS, DOCS), 1, SPAN // (2 * DOCS) + 1)
    big_index = jax.random.randint(key_big, (ROWS, 1), 0, DOCS)
    padding = jax.random.randint(key_pad, (ROWS, 1), 0, min(SEQ_LEN // 20, SPAN // 2 - 1) + 1)
    first_row = jnp.arange(ROWS)[:, None] == 0
    short = jnp.where(first_row, 1, short)
    padding = jnp.where(first_row, 0, padding)
    column = jnp.arange(DOCS)[None, :]
    others = jnp.sum(jnp.where(column == big_index, 0, short), axis=1, keepdims=True)
    giant = SEQ_LEN - padding - others
    return jnp.where(column == big_index, giant, short).astype(jnp.int32)


def block_scale(own_key, shape, cuts, smallest, largest):
    level = 1.0
    for dim, shards_of in cuts:
        draws = jax.random.uniform(jax.random.fold_in(jax.random.fold_in(own_key, 6), dim), (shards_of,), jnp.float32, smallest / len(cuts), largest / len(cuts))
        level = level * jnp.repeat(jnp.exp(draws), shape[dim] // shards_of).reshape((-1,) + (1,) * (len(shape) - 1 - dim))
    return level


def scatter_about(rng, shape, scale, reach, pieces=(), kind=jnp.bfloat16):
    factor_of = block_scale(rng, shape, pieces, -0.22, 0.18) if pieces else 1.0
    drawn = jax.random.normal(rng, shape, jnp.float32) * scale * factor_of
    return jnp.minimum(jnp.maximum(drawn, -reach), reach).astype(kind)


def setup_inputs(seed: int = 0) -> dict:
    seeds = jax.random.split(jax.random.key(seed), 16)
    tokens_in = scatter_about(seeds[0], (ROWS, SEQ_LEN, D), 1.0, 6.0, ((0, 8), (1, 4)))
    lengths = draw_lengths(jax.random.fold_in(seeds[15], 71), 0)
    ln1_gain = jnp.clip(1.0 + 0.18 * jax.random.normal(seeds[2], (D,), jnp.float32), 0.1, 1.9)
    ln1_bias = scatter_about(seeds[3], (D,), 0.3, 1.75, (), jnp.float32)
    qkv_weight = scatter_about(seeds[4], (D, 3 * D), D ** -0.5, 0.21875)
    qv_bias = scatter_about(seeds[5], (2 * D,), 0.5, 3.0, (), jnp.float32)
    proj_weight = scatter_about(seeds[6], (D, D), (max(D // 256, 1)) ** -0.5, 3.5)
    proj_bias = scatter_about(seeds[7], (D,), 0.5, 3.0, (), jnp.float32)
    ln2_gain = jnp.clip(1.0 + 0.18 * jax.random.normal(seeds[8], (D,), jnp.float32), 0.1, 1.9)
    ln2_bias = scatter_about(seeds[9], (D,), 0.3, 1.75, (), jnp.float32)
    fc_weight = scatter_about(seeds[10], (D, FF), D ** -0.5, 0.21875)
    fc_bias = scatter_about(seeds[11], (FF,), 0.5, 3.0, (), jnp.float32)
    out_weight = scatter_about(seeds[12], (FF, D), (FF // 16) ** -0.5, 0.4375)
    out_bias = scatter_about(seeds[13], (D,), 0.5, 3.0, (), jnp.float32)
    cotangent = scatter_about(seeds[14], (ROWS, SEQ_LEN, D), 1.0, 6.0, ((0, 8), (1, 4)))
    return {"tokens_in": tokens_in, "lengths": lengths, "ln1_gain": ln1_gain, "ln1_bias": ln1_bias, "qkv_weight": qkv_weight, "qv_bias": qv_bias, "proj_weight": proj_weight, "proj_bias": proj_bias, "ln2_gain": ln2_gain, "ln2_bias": ln2_bias, "fc_weight": fc_weight, "fc_bias": fc_bias, "out_weight": out_weight, "out_bias": out_bias, "cotangent": cotangent}


branch_scale = 12.0 ** (-0.5)
masked_value = -1e+30
norm_eps = 1e-05
highest = lax.Precision.HIGHEST

@jax.custom_vjp
def low(v):
    return lax.optimization_barrier(v.astype(jnp.bfloat16)).astype(jnp.float32)

@jax.custom_vjp
def low_back(v):
    return v

def low_keep(v):
    return (low(v), None)

def low_pass(kept, grad):
    return (grad,)

def back_keep(v):
    return (v, None)

def back_low(kept, grad):
    return (low(grad),)
low.defvjp(low_keep, low_pass)
low_back.defvjp(back_keep, back_low)

def layer_norm(values, gain, shift):
    center = values - lax.optimization_barrier(jnp.mean(values, axis=-1, keepdims=True))
    spread = lax.optimization_barrier(jnp.mean(center * center, axis=-1, keepdims=True))
    return center * lax.rsqrt(spread + norm_eps) * gain + shift

def attend_row(queries, keys, values, segments):
    row_len = queries.shape[0]
    block = min(512, row_len)
    positions = jnp.arange(row_len, dtype=jnp.int32)
    query_heads = queries.reshape(row_len, HEADS, HEAD).transpose(1, 0, 2)
    key_heads = keys.reshape(row_len, HEADS, HEAD).transpose(1, 0, 2)
    value_heads = values.reshape(row_len, HEADS, HEAD).transpose(1, 0, 2)

    def one_block(block_idx):
        start = (block_idx * block).astype(jnp.int32)
        query_block = lax.dynamic_slice_in_dim(query_heads, start, block, 1)
        query_pos = start + jnp.arange(block, dtype=jnp.int32)
        query_seg = lax.dynamic_slice_in_dim(segments, start, block, 0)
        scores = jnp.einsum('hqd,hkd->hqk', query_block, key_heads, precision=highest) * HEAD ** (-0.5)
        scores = low_back(scores)
        allowed = (positions[None, :] <= query_pos[:, None]) & (segments[None, :] == query_seg[:, None])
        scores = jnp.where(allowed[None], scores, masked_value)
        probs = jax.nn.softmax(scores, axis=-1)
        return jnp.einsum('hqk,hkd->hqd', low(probs), value_heads, precision=highest)
    blocks = lax.map(jax.checkpoint(one_block), jnp.arange(row_len // block, dtype=jnp.int32))
    return blocks.transpose(0, 2, 1, 3).reshape(row_len, HEADS * HEAD)

def layer_forward(inputs, ln1_gain, ln1_bias, qkv_weight, qv_bias, proj_weight, proj_bias, ln2_gain, ln2_bias, fc_weight, fc_bias, out_weight, out_bias, segments, keep_mask):
    model_width = inputs.shape[-1]
    normed = low(layer_norm(inputs, ln1_gain, ln1_bias))
    bias_full = jnp.concatenate([qv_bias[:model_width], jnp.zeros((model_width,), qv_bias.dtype), qv_bias[model_width:]])
    projected = jnp.einsum('rtd,de->rte', normed, qkv_weight, precision=highest) + bias_full
    projected = low_back(low(projected))
    queries = projected[..., :model_width]
    keys = projected[..., model_width:2 * model_width]
    values = projected[..., 2 * model_width:]
    mixed = lax.map(lambda group: attend_row(group[0], group[1], group[2], group[3]), (queries, keys, values, segments))
    mixed = low_back(low(mixed))
    attended = low_back(jnp.einsum('rtd,de->rte', mixed, proj_weight, precision=highest) + proj_bias)
    middle = inputs + branch_scale * attended
    normed_two = low(layer_norm(middle, ln2_gain, ln2_bias))
    hidden_pre = low_back(jnp.einsum('rtd,df->rtf', normed_two, fc_weight, precision=highest) + fc_bias)
    hidden = low(jax.nn.gelu(hidden_pre, approximate=True))
    branch_out = low_back(jnp.einsum('rtf,fd->rtd', hidden, out_weight, precision=highest) + out_bias)
    return (middle + branch_scale * branch_out) * keep_mask

def reference(tokens_in, lengths, ln1_gain, ln1_bias, qkv_weight, qv_bias, proj_weight, proj_bias, ln2_gain, ln2_bias, fc_weight, fc_bias, out_weight, out_bias, cotangent):
    positions = jnp.arange(SEQ_LEN, dtype=jnp.int32)
    ends = jnp.cumsum(lengths, axis=1).astype(jnp.int32)
    segments = lax.optimization_barrier(jnp.sum((positions[None, :, None] >= ends[:, None, :]).astype(jnp.int32), axis=2)).astype(jnp.int32)
    keep_mask = (segments < DOCS).astype(jnp.float32)[..., None]
    weights = (ln1_gain, ln1_bias, qkv_weight, qv_bias, proj_weight, proj_bias, ln2_gain, ln2_bias, fc_weight, fc_bias, out_weight, out_bias)
    weights = tuple((item.astype(jnp.float32) for item in weights))

    def wrapped(inputs, *params):
        return layer_forward(inputs, *params, segments, keep_mask)
    result, pull = jax.vjp(wrapped, tokens_in.astype(jnp.float32), *weights)
    grads = pull(cotangent.astype(jnp.float32))
    return (result.astype(jnp.bfloat16), grads[0], grads[1], grads[2], grads[3], grads[4], grads[5], grads[6], grads[7], grads[8], grads[9], grads[10], grads[11], grads[12])
```

```python
import functools

import jax
import jax.numpy as jnp
from jax import lax
from jax.experimental import pallas as pl
from jax.experimental.pallas import tpu as pltpu
from jax.sharding import PartitionSpec as P

HEAD = 64
branch_scale = 12.0 ** (-0.5)
masked_value = -1e30
norm_eps = 1e-05
F32, BF16 = jnp.float32, jnp.bfloat16
VMEM_LIMIT = 60 * 1024 * 1024


MESH = pl.DeviceIdType.MESH


class Place:
    def __init__(self):
        row, seq = lax.axis_index("row"), lax.axis_index("seq")
        self.row, self.seq = row, seq
        self.core, self.z = lax.rem(row, 2), lax.div(row, 2)
        self.x, self.y = lax.rem(seq, 2), lax.div(seq, 2)
        self.sibling = (row + 1 - 2 * self.core, seq)
        self.across_x = (row, seq + 1 - 2 * self.x)
        self.across_y = (row, seq + 2 - 4 * self.y)
        step_x, step_y = 1 - 2 * self.x, 2 - 4 * self.y
        self.first_bit = self.x + self.core * (self.y - self.x)
        self.second_bit = self.y + self.core * (self.x - self.y)
        self.first = (row, seq + step_x + self.core * (step_y - step_x))
        self.second = (row, seq + step_y + self.core * (step_x - step_y))

        own = seq + self.core * (3 - 2 * seq)
        self.active = own < 3
        self.my_row = jnp.minimum(own, 2)

    def in_plane(self, hop):
        across_x, across_y = hop % 2, hop // 2
        x = self.x + across_x * (1 - 2 * self.x)
        y = self.y + across_y * (1 - 2 * self.y)
        seq = 2 * y + x
        return (self.row, seq), seq + self.core * (3 - 2 * seq)

    def greet_plane(self):
        barrier = pltpu.get_barrier_semaphore()
        for hop in (1, 2, 3):
            pl.semaphore_signal(barrier, inc=1, device_id=self.in_plane(hop)[0], device_id_type=MESH)
        pl.semaphore_wait(barrier, 3)

    def along_z(self, hop):
        return (2 * lax.rem(self.z + hop, 4) + self.core, self.seq)

    def greet(self):
        barrier = pltpu.get_barrier_semaphore()
        others = [self.sibling, self.across_x, self.across_y] + [self.along_z(hop) for hop in (1, 2, 3)]
        for other in others:
            pl.semaphore_signal(barrier, inc=1, device_id=other, device_id_type=MESH)
        pl.semaphore_wait(barrier, len(others))


def send(source, target, send_sem, recv_sem, device):
    return pltpu.make_async_remote_copy(
        src_ref=source, dst_ref=target, send_sem=send_sem, recv_sem=recv_sem,
        device_id=device, device_id_type=MESH,
    )


class Reducer:
    def __init__(self, place, work, recv0, recv1, recv2, recv3, part, out, send_sem, recv_sem, copy_sem):
        self.place, self.work, self.out, self.part = place, work, out, part
        self.recv = (recv0, recv1, recv2, recv3)
        self.send_sem, self.recv_sem, self.copy_sem = send_sem, recv_sem, copy_sem
        rows = work.shape[2]
        self.size = (rows // 2, rows // 4, rows // 8, rows // 16)
        half, quarter, eighth, piece = self.size
        self.own0 = place.core * half
        self.own1 = self.own0 + place.first_bit * quarter
        self.own2 = self.own1 + place.second_bit * eighth
        self.away0 = (1 - place.core) * half
        self.away1 = self.own0 + (1 - place.first_bit) * quarter
        self.away2 = self.own1 + (1 - place.second_bit) * eighth

    def rows(self, start, size):
        return pl.ds(pl.multiple_of(start, self.size[3]), size)

    def piece(self, z):
        return lax.div(z, 2), self.rows(self.own2 + lax.rem(z, 2) * self.size[3], self.size[3])

    def copies(self, phase, u):
        place, work, out, size = self.place, self.work, self.out, self.size
        sems = lambda slot: (self.send_sem.at[u, slot], self.recv_sem.at[u, slot])
        if phase == 0:
            return [send(work.at[u, :, self.rows(self.away0, size[0])], self.recv[0].at[u], *sems(0), place.sibling)]
        if phase == 1:
            return [send(work.at[u, :, self.rows(self.away1, size[1])], self.recv[1].at[u], *sems(1), place.first)]
        if phase == 2:
            return [send(work.at[u, :, self.rows(self.away2, size[2])], self.recv[2].at[u], *sems(2), place.second)]
        if phase == 3:
            made = []
            for hop in (1, 2, 3):
                panel, rows = self.piece(lax.rem(place.z + hop, 4))
                made.append(send(work.at[u, panel, rows], self.recv[3].at[u, hop - 1], *sems(2 + hop), place.along_z(hop)))
            return made
        if phase == 4:
            panel, rows = self.piece(place.z)
            return [
                send(self.part.at[u], out.at[u, panel, rows], *sems(5 + hop), place.along_z(hop)) for hop in (1, 2, 3)
            ]
        start, count, other = {
            5: (self.own2, size[2], place.second),
            6: (self.own1, size[1], place.first),
            7: (self.own0, size[0], place.sibling),
        }[phase]
        rows = self.rows(start, count)
        return [send(out.at[u, :, rows], out.at[u, :, rows], *sems(4 + phase), other)]

    def local(self, u):
        panel, rows = self.piece(self.place.z)
        return pltpu.make_async_copy(self.part.at[u], self.out.at[u, panel, rows], self.copy_sem.at[u])

    def start(self, phase, u):
        for copy in self.copies(phase, u):
            copy.start()
        if phase == 4:
            self.local(u).start()

    def wait(self, phase, u):
        for copy in self.copies(phase, u):
            copy.wait()
        if phase == 4:
            self.local(u).wait()

    def add(self, target, source, u, start, count):
        step = self.size[3]

        def one(i, carry):
            here = self.rows(start + i * step, step)
            there = pl.ds(pl.multiple_of(i * step, step), step)
            for panel in range(2):
                total = target[u, panel, here, :].astype(F32) + source[u, panel, there, :].astype(F32)
                target[u, panel, here, :] = total.astype(BF16)
            return carry

        lax.fori_loop(0, count // step, one, 0)

    def step(self, phase, u):
        if phase > 0:
            self.wait(phase - 1, u)
        if phase == 1:
            self.add(self.work, self.recv[0], u, self.own0, self.size[0])
        elif phase == 2:
            self.add(self.work, self.recv[1], u, self.own1, self.size[1])
        elif phase == 3:
            self.add(self.work, self.recv[2], u, self.own2, self.size[2])
        elif phase == 4:
            panel, rows = self.piece(self.place.z)
            total = self.work[u, panel, rows, :].astype(F32)
            for hop in range(3):
                total = total + self.recv[3][u, hop].astype(F32)
            self.part[u] = total.astype(BF16)
        if phase < 8:
            self.start(phase, u)


class SmallReducer:
    def __init__(self, place, sums, recv, line, send_sem, recv_sem):
        self.place, self.sums, self.recv, self.line = place, sums, recv, line
        self.send_sem, self.recv_sem = send_sem, recv_sem

    def copies(self, phase):
        place = self.place
        if phase < 3:
            other = (place.sibling, place.across_x, place.across_y)[phase]
            return [send(self.sums.at[phase], self.recv.at[phase], self.send_sem.at[phase], self.recv_sem.at[phase], other)]
        return [
            send(self.sums.at[3], self.line.at[place.z], self.send_sem.at[2 + hop], self.recv_sem.at[2 + hop], place.along_z(hop))
            for hop in (1, 2, 3)
        ]

    def step(self, phase):
        if phase > 0:
            for copy in self.copies(phase - 1):
                copy.wait()
        if 0 < phase < 4:
            self.sums[phase] = self.sums[phase - 1] + self.recv[phase - 1]
        if phase < 4:
            for copy in self.copies(phase):
                copy.start()
        if phase == 3:
            self.line[self.place.z] = self.sums[3]

    def total(self):
        return (self.line[0] + self.line[1]) + (self.line[2] + self.line[3])


def dot_nn(left, right):
    return lax.dot_general(left, right, (((1,), (0,)), ((), ())), preferred_element_type=F32)


def dot_nt(left, right):
    return lax.dot_general(left, right, (((1,), (1,)), ((), ())), preferred_element_type=F32)


def dot_tn(left, right):
    return lax.dot_general(left, right, (((0,), (0,)), ((), ())), preferred_element_type=F32)


def row_mean(values):
    return jnp.mean(values, axis=-1, keepdims=True)


def normalise(values):
    center = values - row_mean(values)
    inverse = lax.rsqrt(row_mean(center * center) + norm_eps)
    return center * inverse, inverse


def fill_bias(lens_ref, row, bias_ref, block):
    tokens = bias_ref.shape[0]
    ends, total = [], jnp.int32(0)
    for j in range(lens_ref.shape[1]):
        total = total + lens_ref[row, j]
        ends.append(total)
    query_pos = lax.broadcasted_iota(jnp.int32, (1, tokens), 1)
    query_seg = jnp.zeros((1, tokens), jnp.int32)
    for end in ends:
        query_seg = query_seg + (query_pos >= end).astype(jnp.int32)

    def one(i, carry):
        start = pl.multiple_of(i * block, block)
        key_pos = start + lax.broadcasted_iota(jnp.int32, (block, 1), 0)
        key_seg = jnp.zeros((block, 1), jnp.int32)
        for end in ends:
            key_seg = key_seg + (key_pos >= end).astype(jnp.int32)
        allowed = (key_pos <= query_pos) & (key_seg == query_seg)
        bias_ref[pl.ds(start, block), :] = jnp.where(allowed, 0.0, masked_value)
        return carry

    lax.fori_loop(0, tokens // block, one, 0)


def keep_column(lens_ref, row, start, block):
    total = jnp.int32(0)
    for j in range(lens_ref.shape[1]):
        total = total + lens_ref[row, j]
    pos = start + lax.broadcasted_iota(jnp.int32, (block, 1), 0)
    return (pos < total).astype(F32)


def head_row(h, value):
    lane = lax.broadcasted_iota(jnp.int32, (1, 2 * HEAD), 1)
    low = h % 2 * HEAD
    return jnp.where((lane >= low) & (lane < low + HEAD), value, 0.0).astype(BF16)


def front_kernel(
    lens_ref, tokens_ref, cot_in_ref, gain_ref, shift_ref, wq_ref, wk_ref, wv_ref, bq_ref, bv_ref,
    q_ref, k_ref, v_ref, o_ref, lse_ref, x_ref, cot_ref,
    arrived, normed, bias, value_t, out_t, send_sem, recv_sem, copy_sem,
):
    tokens, width = x_ref.shape
    lanes = wq_ref.shape[1]
    block = tokens_ref.shape[1]
    blocks = tokens // block
    place = Place()
    mine = pl.ds(place.seq, 1)
    sources, targets = (tokens_ref, cot_in_ref), (arrived, cot_ref)

    def outgoing(which, hop):
        other, row = place.in_plane(hop)
        return row, send(
            sources[which].at[jnp.minimum(row, 2)], targets[which].at[place.seq],
            send_sem.at[which, hop - 1], recv_sem.at[which, hop - 1], other,
        )

    def local(which):
        return pltpu.make_async_copy(
            sources[which].at[place.my_row], targets[which].at[place.seq], copy_sem.at[which]
        )

    def start(which):
        for hop in (1, 2, 3):
            row, copy = outgoing(which, hop)
            pl.when(row < 3)(copy.start)
        pl.when(place.active)(local(which).start)

    def finish(which):
        for hop in (1, 2, 3):
            row, copy = outgoing(which, hop)
            pl.when(row < 3)(copy.wait_send)
            pl.when(place.active)(copy.wait_recv)
        pl.when(place.active)(local(which).wait)

    @pl.when(pl.program_id(0) == 0)
    def _():
        place.greet_plane()
        start(0)
        start(1)
        fill_bias(lens_ref, place.my_row, bias, block)

        @pl.when(jnp.logical_not(place.active))
        def _():
            arrived[...] = jnp.zeros_like(arrived)

        finish(0)

        def one(i, carry):
            rows = pl.ds(pl.multiple_of(i * block, block), block)
            x = arrived[i]
            x_ref[rows, :] = x
            unit, _ = normalise(x.astype(F32))
            normed[rows, :] = (unit * gain_ref[...] + shift_ref[...]).astype(BF16)
            return carry

        lax.fori_loop(0, blocks, one, 0)

    def project(i, carry):
        rows = pl.ds(pl.multiple_of(i * block, block), block)
        h1 = normed[rows, :]
        q_ref[rows, :] = (dot_nn(h1, wq_ref[...]) + bq_ref[...]).astype(BF16)
        k_ref[rows, :] = dot_nn(h1, wk_ref[...]).astype(BF16)
        values = dot_nn(h1, wv_ref[...]) + bv_ref[...]
        v_ref[rows, :] = values.astype(BF16)
        value_t[:, rows] = values.T.astype(BF16)
        return carry

    lax.fori_loop(0, blocks, project, 0)

    for i in range(blocks):
        rows = slice(i * block, (i + 1) * block)
        count = (i + 1) * block
        for h in range(lanes // HEAD):
            pair = slice(h // 2 * 2 * HEAD, (h // 2 + 1) * 2 * HEAD)
            own = slice(h * HEAD, (h + 1) * HEAD)
            queries = q_ref[rows, pair] * head_row(h, HEAD ** (-0.5))
            scores = dot_nt(k_ref[:count, pair], queries) + bias[:count, rows]
            top = jnp.max(scores, axis=0, keepdims=True)
            probs = jnp.exp(scores - top)
            total = jnp.sum(probs, axis=0, keepdims=True)
            mixed = dot_nn(value_t[own, :count], probs.astype(BF16))
            out_t[own, :] = mixed * (1.0 / total)
            lse_ref[0, h : h + 1, rows] = top + jnp.log(total)
        o_ref[rows, :] = out_t[...].T.astype(BF16)

    @pl.when(pl.program_id(0) == pl.num_programs(0) - 1)
    def _():
        finish(1)

        @pl.when(jnp.logical_not(place.active))
        def _():
            copy = pltpu.make_async_copy(arrived, cot_ref, copy_sem.at[1])
            copy.start()
            copy.wait()


def front(lens, tokens_in, cotangent, gain, shift, qkv_weight, qv_bias):
    rows, span, width = tokens_in.shape
    spans = lax.axis_size("seq")
    tokens = spans * span
    lanes = min(256, width)
    groups = width // lanes
    heads = max(8, lanes // HEAD)
    whole = lambda shape: pl.BlockSpec(shape, lambda g: (0,) * len(shape))
    columns = lambda shape, first: pl.BlockSpec(shape, lambda g: (0, first + g))
    act = jax.ShapeDtypeStruct((tokens, width), BF16)
    sem = lambda *shape: pltpu.SemaphoreType.DMA(shape)
    return pl.pallas_call(
        front_kernel,
        grid=(groups,),
        out_shape=(
            act, act, act, act, jax.ShapeDtypeStruct((groups, heads, tokens), F32), act,
            jax.ShapeDtypeStruct((spans, span, width), BF16),
        ),
        in_specs=[
            pl.BlockSpec(memory_space=pltpu.SMEM),
            pl.BlockSpec(memory_space=pl.ANY),
            pl.BlockSpec(memory_space=pl.ANY),
            whole((1, width)),
            whole((1, width)),
            columns((width, lanes), 0),
            columns((width, lanes), groups),
            columns((width, lanes), 2 * groups),
            columns((1, lanes), 0),
            columns((1, lanes), groups),
        ],
        out_specs=[columns((tokens, lanes), 0)] * 4
        + [
            pl.BlockSpec((1, heads, tokens), lambda g: (g, 0, 0)),
            whole((tokens, width)),
            pl.BlockSpec(memory_space=pl.ANY),
        ],
        scratch_shapes=[
            pltpu.VMEM((spans, span, width), BF16),
            pltpu.VMEM((tokens, width), BF16),
            pltpu.VMEM((tokens, tokens), F32),
            pltpu.VMEM((lanes, tokens), BF16),
            pltpu.VMEM((lanes, span), F32),
            sem(2, 3), sem(2, 3), sem(2),
        ],
        compiler_params=pltpu.CompilerParams(
            collective_id=1, has_side_effects=True, vmem_limit_bytes=VMEM_LIMIT
        ),
        name="front",
    )(lens, tokens_in, cotangent, gain, shift, qkv_weight, qkv_weight, qkv_weight, qv_bias, qv_bias)


def feed_kernel(
    lens_ref, o_ref, x_ref, cot_ref, wp_ref, bp_ref, gain_ref, shift_ref,
    wf_ref, bf_ref, wo_ref, bo_ref,
    lo_ref, dy_ref, do_ref, gp_ref, gf_ref, go_ref, gbf_ref, small_ref,
    middle, normed, normed_t, cot_low, out_acc, back_acc, hidden, back_low,
):
    tokens, width = x_ref.shape
    step, last = pl.program_id(0), pl.num_programs(0) - 1
    block = min(256, tokens)
    blocks = tokens // block

    def each(body):
        def run(i, carry):
            start = pl.multiple_of(i * block, block)
            body(start, pl.ds(start, block))
            return carry

        lax.fori_loop(0, blocks, run, 0)

    @pl.when(step == 0)
    def _():
        small_ref[...] = jnp.zeros_like(small_ref)

        def begin(start, rows):
            attn = dot_nn(o_ref[rows, :], wp_ref[...]) + bp_ref[...]
            mid = x_ref[rows, :].astype(F32) + branch_scale * attn
            middle[rows, :] = mid
            unit, _ = normalise(mid)
            h2 = unit * gain_ref[...] + shift_ref[...]
            normed[rows, :] = h2.astype(BF16)
            normed_t[:, rows] = h2.T.astype(BF16)
            keep = keep_column(lens_ref, Place().my_row, start, block)
            low = (branch_scale * (keep * cot_ref[rows, :].astype(F32))).astype(BF16)
            cot_low[rows, :] = low
            small_ref[0:1, :] += jnp.sum(low.astype(F32), axis=0, keepdims=True)

        each(begin)

    gbf_ref[...] = jnp.zeros_like(gbf_ref)

    def chunk(start, rows):
        pre = dot_nn(normed[rows, :], wf_ref[...]) + bf_ref[...]
        back = dot_nt(cot_low[rows, :], wo_ref[...])
        square = pre * pre
        root = (2.0 / jnp.pi) ** 0.5
        bend = jnp.tanh(pre * (root + (root * 0.044715) * square))
        half = 0.5 * pre
        hid = (half + half * bend).astype(BF16)
        slope = (0.5 + 0.5 * bend) + half * (1.0 - bend * bend) * (root + (3.0 * root * 0.044715) * square)
        grad = (back * slope).astype(BF16)
        hidden[rows, :] = hid
        back_low[rows, :] = grad
        gbf_ref[0:1, :] += jnp.sum(grad.astype(F32), axis=0, keepdims=True)
        added = dot_nn(hid, wo_ref[...])
        backed = dot_nt(grad, wf_ref[...])

        @pl.when(step == 0)
        def _():
            out_acc[rows, :] = added
            back_acc[rows, :] = backed

        @pl.when(step > 0)
        def _():
            out_acc[rows, :] += added
            back_acc[rows, :] += backed

    each(chunk)
    go_ref[0] = dot_tn(hidden[...], cot_low[...]).astype(BF16)
    gf_ref[0] = dot_nn(normed_t[...], back_low[...]).astype(BF16)

    @pl.when(step == last)
    def _():
        def end(start, rows):
            keep = keep_column(lens_ref, Place().my_row, start, block)
            mid = middle[rows, :]
            lo_ref[rows, :] = (
                keep * (mid + branch_scale * (out_acc[rows, :] + bo_ref[...]))
            ).astype(BF16)
            unit, inverse = normalise(mid)
            back = back_acc[rows, :]
            small_ref[1:2, :] += jnp.sum(back * unit, axis=0, keepdims=True)
            small_ref[2:3, :] += jnp.sum(back, axis=0, keepdims=True)
            scaled = back * gain_ref[...]
            grad = keep * cot_ref[rows, :].astype(F32) + inverse * (
                scaled - row_mean(scaled) - unit * row_mean(scaled * unit)
            )
            dy_ref[rows, :] = grad
            low = (branch_scale * grad).astype(BF16)
            hidden[rows, :] = low
            small_ref[3:4, :] += jnp.sum(low.astype(F32), axis=0, keepdims=True)
            do_ref[rows, :] = dot_nt(low, wp_ref[...]).astype(BF16)

        each(end)
        gp_ref[...] = dot_tn(o_ref[...], hidden[...]).astype(BF16)


def feed(lens, o, x, cot, proj_weight, proj_bias, gain, shift, fc_weight, fc_bias, out_weight, out_bias):
    tokens, width = x.shape
    steps = fc_weight.shape[1] // width
    whole = lambda shape: pl.BlockSpec(shape, lambda f: (0,) * len(shape))
    act, vec, mat = whole((tokens, width)), whole((1, width)), whole((width, width))
    panel = pl.BlockSpec((1, width, width), lambda f: (f, 0, 0))
    shape = jax.ShapeDtypeStruct
    return pl.pallas_call(
        feed_kernel,
        grid=(steps,),
        out_shape=(
            shape((tokens, width), BF16),
            shape((tokens, width), F32),
            shape((tokens, width), BF16),
            shape((width, width), BF16),
            shape((steps, width, width), BF16),
            shape((steps, width, width), BF16),
            shape((8, steps * width), F32),
            shape((8, width), F32),
        ),
        in_specs=[
            pl.BlockSpec(memory_space=pltpu.SMEM),
            act, act, act, mat, vec, vec, vec,
            pl.BlockSpec((width, width), lambda f: (0, f)),
            pl.BlockSpec((1, width), lambda f: (0, f)),
            pl.BlockSpec((width, width), lambda f: (f, 0)),
            vec,
        ],
        out_specs=[
            act, act, act, mat, panel, panel,
            pl.BlockSpec((8, width), lambda f: (0, f)),
            whole((8, width)),
        ],
        scratch_shapes=[
            pltpu.VMEM((tokens, width), F32),
            pltpu.VMEM((tokens, width), BF16),
            pltpu.VMEM((width, tokens), BF16),
            pltpu.VMEM((tokens, width), BF16),
            pltpu.VMEM((tokens, width), F32),
            pltpu.VMEM((tokens, width), F32),
            pltpu.VMEM((tokens, width), BF16),
            pltpu.VMEM((tokens, width), BF16),
        ],
        compiler_params=pltpu.CompilerParams(vmem_limit_bytes=VMEM_LIMIT),
        name="feed",
    )(lens, o, x, cot, proj_weight, proj_bias, gain, shift, fc_weight, fc_bias, out_weight, out_bias)


def back_kernel(
    lens_ref, x_ref, dy_ref, gain_ref, shift_ref, q_ref, k_ref, v_ref, o_ref, do_ref, lse_ref,
    wq_ref, wk_ref, wv_ref,
    dx_ref, gq_ref, gk_ref, gv_ref, gb_ref, small_ref,
    bias, normed_t, back_acc, key_t, grad_q_t, grad_q, grad_k, grad_v,
):
    tokens, width = x_ref.shape
    lanes = wq_ref.shape[1]
    step, last = pl.program_id(0), pl.num_programs(0) - 1
    block = min(256, tokens)
    blocks = tokens // block

    def each(body):
        def run(i, carry):
            start = pl.multiple_of(i * block, block)
            body(start, pl.ds(start, block))
            return carry

        lax.fori_loop(0, blocks, run, 0)

    @pl.when(step == 0)
    def _():
        fill_bias(lens_ref, Place().my_row, bias, block)
        small_ref[...] = jnp.zeros_like(small_ref)

        def begin(start, rows):
            unit, _ = normalise(x_ref[rows, :].astype(F32))
            h1 = unit * gain_ref[...] + shift_ref[...]
            normed_t[:, rows] = h1.T.astype(BF16)

        each(begin)

    gb_ref[...] = jnp.zeros_like(gb_ref)
    grad_k[...] = jnp.zeros_like(grad_k)
    grad_v[...] = jnp.zeros_like(grad_v)
    key_t[...] = k_ref[...].astype(F32).T.astype(BF16)
    head_id = lax.broadcasted_iota(jnp.int32, (8, lanes), 0)
    lane_id = lax.broadcasted_iota(jnp.int32, (8, lanes), 1)
    member = ((lane_id >= head_id * HEAD) & (lane_id < (head_id + 1) * HEAD)).astype(F32)

    for i in range(blocks):
        rows = slice(i * block, (i + 1) * block)
        count = (i + 1) * block
        product = do_ref[rows, :].astype(F32) * o_ref[rows, :].astype(F32)
        delta = lax.dot_general(
            member, product, (((1,), (1,)), ((), ())),
            precision=lax.Precision.HIGHEST, preferred_element_type=F32,
        )
        for h in range(lanes // HEAD):
            pair = slice(h // 2 * 2 * HEAD, (h // 2 + 1) * 2 * HEAD)
            own = slice(h * HEAD, (h + 1) * HEAD)
            queries = q_ref[rows, pair] * head_row(h, HEAD ** (-0.5))
            grads = do_ref[rows, pair] * head_row(h, 1.0)
            scores = dot_nt(k_ref[:count, pair], queries) + bias[:count, rows]
            probs = jnp.exp(scores - lse_ref[0, h : h + 1, rows])
            grad_probs = dot_nt(v_ref[:count, pair], grads)
            grad_scores = (probs * (grad_probs - delta[h : h + 1, :])).astype(BF16)
            grad_v[:count, pair] += dot_nn(probs.astype(BF16), grads)
            grad_k[:count, pair] += dot_nn(grad_scores, queries)
            grad_q_t[own, rows] = dot_nn(key_t[own, :count], grad_scores)

    def finish(start, rows):
        dq = (grad_q_t[:, rows].T * HEAD ** (-0.5)).astype(BF16)
        grad_q[rows, :] = dq
        dk = grad_k[rows, :].astype(BF16)
        dv = grad_v[rows, :].astype(BF16)
        gb_ref[0:1, :] += jnp.sum(dq.astype(F32), axis=0, keepdims=True)
        gb_ref[1:2, :] += jnp.sum(dv.astype(F32), axis=0, keepdims=True)
        added = dot_nt(dq, wq_ref[...]) + dot_nt(dk, wk_ref[...]) + dot_nt(dv, wv_ref[...])

        @pl.when(step == 0)
        def _():
            back_acc[rows, :] = added

        @pl.when(step > 0)
        def _():
            back_acc[rows, :] += added

    each(finish)
    gq_ref[...] = dot_nn(normed_t[...], grad_q[...]).astype(BF16)
    gk_ref[...] = dot_nn(normed_t[...], grad_k[...].astype(BF16)).astype(BF16)
    gv_ref[...] = dot_nn(normed_t[...], grad_v[...].astype(BF16)).astype(BF16)

    @pl.when(step == last)
    def _():
        def end(start, rows):
            unit, inverse = normalise(x_ref[rows, :].astype(F32))
            back = back_acc[rows, :]
            small_ref[0:1, :] += jnp.sum(back * unit, axis=0, keepdims=True)
            small_ref[1:2, :] += jnp.sum(back, axis=0, keepdims=True)
            scaled = back * gain_ref[...]
            grad = dy_ref[rows, :] + inverse * (
                scaled - row_mean(scaled) - unit * row_mean(scaled * unit)
            )
            dx_ref[rows, :] = grad.astype(dx_ref.dtype)

        each(end)


def back(lens, x, dy, gain, shift, q, k, v, o, do, lse, qkv_weight):
    tokens, width = x.shape
    lanes = min(256, width)
    groups = width // lanes
    heads = lse.shape[1]
    whole = lambda shape: pl.BlockSpec(shape, lambda g: (0,) * len(shape))
    columns = lambda shape, first: pl.BlockSpec(shape, lambda g: (0, first + g))
    act, vec = whole((tokens, width)), whole((1, width))
    shape = jax.ShapeDtypeStruct
    mat = shape((width, width), BF16)
    return pl.pallas_call(
        back_kernel,
        grid=(groups,),
        out_shape=(shape((tokens, width), BF16), mat, mat, mat, shape((8, width), F32), shape((8, width), F32)),
        in_specs=[pl.BlockSpec(memory_space=pltpu.SMEM), act, act, vec, vec]
        + [columns((tokens, lanes), 0)] * 5
        + [
            pl.BlockSpec((1, heads, tokens), lambda g: (g, 0, 0)),
            columns((width, lanes), 0),
            columns((width, lanes), groups),
            columns((width, lanes), 2 * groups),
        ],
        out_specs=[act]
        + [columns((width, lanes), 0)] * 3
        + [columns((8, lanes), 0), whole((8, width))],
        scratch_shapes=[
            pltpu.VMEM((tokens, tokens), F32),
            pltpu.VMEM((width, tokens), BF16),
            pltpu.VMEM((tokens, width), F32),
            pltpu.VMEM((lanes, tokens), BF16),
            pltpu.VMEM((lanes, tokens), F32),
            pltpu.VMEM((tokens, lanes), BF16),
            pltpu.VMEM((tokens, lanes), F32),
            pltpu.VMEM((tokens, lanes), F32),
        ],
        compiler_params=pltpu.CompilerParams(vmem_limit_bytes=VMEM_LIMIT),
        name="back",
    )(lens, x, dy, gain, shift, q, k, v, o, do, lse, qkv_weight, qkv_weight, qkv_weight)


def reduce_kernel(
    go_ref, gf_ref, gq_ref, gk_ref, gv_ref, gp_ref, small_ref,
    out_ref, small_out,
    work, recv0, recv1, recv2, recv3, part, sums, small_recv, line,
    send_sem, recv_sem, copy_sem, load_sem, small_send, small_recv_sem,
):
    place = Place()
    units = work.shape[0]
    feed_units = units - 2
    loads = [(go_ref.at[f], (f, 0)) for f in range(feed_units)]
    loads += [(gf_ref.at[f], (f, 1)) for f in range(feed_units)]
    loads += [(gq_ref, (feed_units, 0)), (gk_ref, (feed_units, 1)), (gv_ref, (feed_units + 1, 0)), (gp_ref, (feed_units + 1, 1))]
    copies = [pltpu.make_async_copy(source, work.at[u, p], load_sem.at[u, p]) for source, (u, p) in loads]
    for copy in copies:
        copy.start()
    sums[0] = small_ref[...]
    place.greet()
    small = SmallReducer(place, sums, small_recv, line, small_send, small_recv_sem)
    main = Reducer(place, work, recv0, recv1, recv2, recv3, part, out_ref, send_sem, recv_sem, copy_sem)
    for copy in copies:
        copy.wait()
    small.step(0)

    def tick(t, carry):
        for phase in range(8, -1, -1):
            u = t - phase

            @pl.when((u >= 0) & (u < units))
            def _():
                main.step(phase, u)

        return carry

    lax.fori_loop(0, units + 8, tick, 0)
    for phase in range(1, 5):
        small.step(phase)
    small_out[...] = small.total()


def all_reduce(go, gf, gq, gk, gv, gp, small):
    units, width = go.shape[0] + 2, gp.shape[0]
    vmem = lambda *shape: pltpu.VMEM(shape, BF16)
    sem = lambda *shape: pltpu.SemaphoreType.DMA(shape)
    return pl.pallas_call(
        reduce_kernel,
        out_shape=(
            jax.ShapeDtypeStruct((units, 2, width, width), BF16),
            jax.ShapeDtypeStruct(small.shape, F32),
        ),
        in_specs=[pl.BlockSpec(memory_space=pl.ANY)] * 6 + [pl.BlockSpec(memory_space=pltpu.VMEM)],
        out_specs=[pl.BlockSpec(memory_space=pl.ANY), pl.BlockSpec(memory_space=pltpu.VMEM)],
        scratch_shapes=[
            vmem(units, 2, width, width),
            vmem(units, 2, width // 2, width),
            vmem(units, 2, width // 4, width),
            vmem(units, 2, width // 8, width),
            vmem(units, 3, width // 16, width),
            vmem(units, width // 16, width),
            pltpu.VMEM((4,) + small.shape, F32),
            pltpu.VMEM((3,) + small.shape, F32),
            pltpu.VMEM((4,) + small.shape, F32),
            sem(units, 12), sem(units, 12), sem(units), sem(units, 2), sem(6), sem(6),
        ],
        compiler_params=pltpu.CompilerParams(
            collective_id=0, has_side_effects=True, vmem_limit_bytes=VMEM_LIMIT
        ),
        name="all_reduce",
    )(go, gf, gq, gk, gv, gp, small)


def spread_kernel(lo_ref, dx_ref, lo_out, dx_out, send_sem, recv_sem, copy_sem):
    place = Place()
    place.greet_plane()
    sources, targets = (dx_ref, lo_ref), (dx_out, lo_out)

    def outgoing(which, hop):
        other, row = place.in_plane(hop)
        return row, send(
            sources[which].at[other[1]], targets[which].at[place.my_row],
            send_sem.at[which, hop - 1], recv_sem.at[which, hop - 1], other,
        )

    def local(which):
        return pltpu.make_async_copy(
            sources[which].at[place.seq], targets[which].at[place.my_row], copy_sem.at[which]
        )

    for which in (0, 1):
        for hop in (1, 2, 3):
            row, copy = outgoing(which, hop)
            pl.when(place.active)(copy.start)
        pl.when(place.active)(local(which).start)
    for which in (0, 1):
        for hop in (1, 2, 3):
            row, copy = outgoing(which, hop)
            pl.when(place.active)(copy.wait_send)
            pl.when(row < 3)(copy.wait_recv)
        pl.when(place.active)(local(which).wait)


def spread(lo, dx, rows):
    spans, span, width = lo.shape
    out = jax.ShapeDtypeStruct((rows, span, width), BF16)
    sem = lambda *shape: pltpu.SemaphoreType.DMA(shape)
    return pl.pallas_call(
        spread_kernel,
        out_shape=(out, out),
        in_specs=[pl.BlockSpec(memory_space=pl.ANY)] * 2,
        out_specs=[pl.BlockSpec(memory_space=pl.ANY)] * 2,
        scratch_shapes=[sem(2, 3), sem(2, 3), sem(2)],
        compiler_params=pltpu.CompilerParams(collective_id=2, has_side_effects=True),
        name="spread",
    )(lo, dx)


def by_rows(
    tokens_in, lengths, ln1_gain, ln1_bias, qkv_weight, qv_bias, proj_weight, proj_bias,
    ln2_gain, ln2_bias, fc_weight, fc_bias, out_weight, out_bias, cotangent,
):
    rows, span, width = tokens_in.shape
    flat = lambda array: array.reshape(1, -1)
    q, k, v, o, lse, x, cot = front(
        lengths, tokens_in, cotangent, flat(ln1_gain), flat(ln1_bias), qkv_weight, flat(qv_bias)
    )
    lo, dy, do, gp, gf, go, gbf, small2 = feed(
        lengths, o, x, cot.reshape(x.shape), proj_weight, flat(proj_bias), flat(ln2_gain), flat(ln2_bias),
        fc_weight, flat(fc_bias), out_weight, flat(out_bias),
    )
    dx, gq, gk, gv, gb, small1 = back(
        lengths, x, dy, flat(ln1_gain), flat(ln1_bias), q, k, v, o, do, lse, qkv_weight
    )
    small = jnp.concatenate(
        [small1[0:2], gb[0:2], small2[0:4], gbf[0].reshape(-1, width), jnp.zeros((4, width), F32)]
    )
    whole, small = all_reduce(go, gf, gq, gk, gv, gp, small)
    layer_out, input_grad = spread(
        lo.reshape(-1, span, width), dx.reshape(-1, span, width), rows
    )
    whole = whole.astype(F32)
    steps = go.shape[0]
    return (
        layer_out,
        input_grad.astype(F32),
        small[0],
        small[1],
        jnp.concatenate([whole[steps, 0], whole[steps, 1], whole[steps + 1, 0]], axis=1),
        small[2:4].reshape(-1),
        whole[steps + 1, 1],
        small[7],
        small[5],
        small[6],
        whole[:steps, 1].transpose(1, 0, 2).reshape(width, -1),
        small[8 : 8 + steps].reshape(-1),
        whole[:steps, 0].reshape(-1, width),
        small[4],
    )


def layer_norm(values, gain, shift):
    center = values - jnp.mean(values, axis=-1, keepdims=True)
    spread = jnp.mean(center * center, axis=-1, keepdims=True)
    return center * lax.rsqrt(spread + norm_eps) * gain + shift


def gelu_tanh(values):
    return jax.nn.gelu(values, approximate=True)


def left_dot(left, right):
    return lax.dot_general(
        left, right, (((0,), (0,)), ((), ())), preferred_element_type=jnp.float32
    )


def right_dot(left, right):
    return lax.dot_general(
        left, right, (((1,), (1,)), ((), ())), preferred_element_type=jnp.float32
    )


def allowed_mask(query_pos, query_seg, key_pos, key_seg):
    return (key_pos[None, None, :] <= query_pos[None, :, None]) & (
        key_seg[:, None, :] == query_seg[:, :, None]
    )


def local(
    tokens_in,
    lengths,
    ln1_gain,
    ln1_bias,
    qkv_weight,
    qv_bias,
    proj_weight,
    proj_bias,
    ln2_gain,
    ln2_bias,
    fc_weight,
    fc_bias,
    out_weight,
    out_bias,
    cotangent,
):
    row_count, span_len, model_width = tokens_in.shape
    head_count = model_width // HEAD
    scale = HEAD ** (-0.5)
    seq_parts = lax.axis_size("seq")
    row_len = span_len * seq_parts
    first_pos = lax.axis_index("seq") * span_len
    doc_count = lengths.shape[1]
    positions = jnp.arange(row_len, dtype=jnp.int32)
    ends = jnp.cumsum(lengths, axis=1)
    segments = jnp.sum((positions[None, :, None] >= ends[:, None, :]).astype(jnp.int32), axis=2)
    my_segs = lax.dynamic_slice_in_dim(segments, first_pos, span_len, 1)
    my_pos = first_pos + jnp.arange(span_len, dtype=jnp.int32)
    token_count = row_count * span_len
    keep_flat = (my_segs < doc_count).astype(jnp.float32).reshape(token_count, 1)
    inputs = tokens_in.astype(jnp.float32).reshape(token_count, model_width)
    normed = layer_norm(inputs, ln1_gain, ln1_bias)
    normed_low = normed.astype(jnp.bfloat16)
    bias_full = jnp.concatenate(
        [qv_bias[:model_width], jnp.zeros((model_width,), jnp.float32), qv_bias[model_width:]]
    )
    projected = (
        jnp.dot(normed_low, qkv_weight, preferred_element_type=jnp.float32) + bias_full
    ).astype(jnp.bfloat16)
    projected = projected.reshape(row_count, span_len, 3 * model_width)
    queries = projected[..., :model_width]
    keys = projected[..., model_width : 2 * model_width]
    values = projected[..., 2 * model_width :]
    query_heads = queries.reshape(row_count, span_len, head_count, HEAD)
    key_heads = keys.reshape(row_count, span_len, head_count, HEAD)
    value_heads = values.reshape(row_count, span_len, head_count, HEAD)
    last_pos = first_pos + span_len - 1
    start_state = (
        jnp.full((row_count, head_count, span_len), masked_value, jnp.float32),
        jnp.zeros((row_count, head_count, span_len), jnp.float32),
        jnp.zeros((row_count, span_len, model_width), jnp.float32),
    )
    key_piece = lax.all_gather(keys, "seq", axis=1, tiled=True)
    value_piece = lax.all_gather(values, "seq", axis=1, tiled=True)
    count = key_piece.shape[1]

    def forward_update(state):
        top, total, accum = state
        piece_keys = key_piece.reshape(row_count, count, head_count, HEAD)
        piece_values = value_piece.reshape(row_count, count, head_count, HEAD)
        scores = (
            jnp.einsum(
                "rqhd,rkhd->rhqk", query_heads, piece_keys, preferred_element_type=jnp.float32
            )
            * scale
        )
        key_pos = jnp.arange(count, dtype=jnp.int32)
        allowed = allowed_mask(my_pos, my_segs, key_pos, segments)[:, None]
        scores = jnp.where(allowed, scores, masked_value)
        new_top = jnp.maximum(top, jnp.max(scores, axis=-1))
        weights = jnp.where(allowed, jnp.exp(scores - new_top[..., None]), 0.0)
        total = jnp.sum(weights, axis=-1)
        added = jnp.einsum(
            "rhqk,rkhd->rqhd",
            weights.astype(jnp.bfloat16),
            piece_values,
            preferred_element_type=jnp.float32,
        )
        accum = added.reshape(row_count, span_len, model_width)
        return (new_top, total, accum)

    top, total, accum = lax.cond(
        jnp.int32(0) > last_pos, lambda state: state, forward_update, start_state
    )
    log_total = top + jnp.log(total)
    attended_heads = (
        accum.reshape(row_count, span_len, head_count, HEAD) / total.transpose(0, 2, 1)[..., None]
    )
    attended = attended_heads.reshape(token_count, model_width)
    attended_low = attended.astype(jnp.bfloat16)
    attn_out = jnp.dot(attended_low, proj_weight, preferred_element_type=jnp.float32) + proj_bias
    middle = inputs + branch_scale * attn_out
    normed_two = layer_norm(middle, ln2_gain, ln2_bias)
    normed_two_low = normed_two.astype(jnp.bfloat16)
    hidden_pre = jnp.dot(normed_two_low, fc_weight, preferred_element_type=jnp.float32) + fc_bias
    hidden_low = gelu_tanh(hidden_pre).astype(jnp.bfloat16)
    branch_out = jnp.dot(hidden_low, out_weight, preferred_element_type=jnp.float32) + out_bias
    layer_out = (
        ((middle + branch_scale * branch_out) * keep_flat)
        .astype(jnp.bfloat16)
        .reshape(row_count, span_len, model_width)
    )
    grad_final = keep_flat * cotangent.astype(jnp.float32).reshape(token_count, model_width)
    grad_branch = (branch_scale * grad_final).astype(jnp.bfloat16)
    grad_out_weight = left_dot(hidden_low, grad_branch)
    grad_out_bias = jnp.sum(grad_branch.astype(jnp.float32), axis=0)
    grad_hidden = right_dot(grad_branch, out_weight)
    gelu_value, gelu_pull = jax.vjp(gelu_tanh, hidden_pre)
    grad_pre = gelu_pull(grad_hidden)[0].astype(jnp.bfloat16)
    grad_fc_weight = left_dot(normed_two_low, grad_pre)
    grad_fc_bias = jnp.sum(grad_pre.astype(jnp.float32), axis=0)
    grad_normed_two = right_dot(grad_pre, fc_weight)
    norm_value, norm_pull = jax.vjp(layer_norm, middle, ln2_gain, ln2_bias)
    grad_mid_norm, grad_ln2_gain, grad_ln2_bias = norm_pull(grad_normed_two)
    grad_middle = grad_final + grad_mid_norm
    grad_attn = (branch_scale * grad_middle).astype(jnp.bfloat16)
    grad_proj_weight = left_dot(attended_low, grad_attn)
    grad_proj_bias = jnp.sum(grad_attn.astype(jnp.float32), axis=0)
    grad_attended = (
        right_dot(grad_attn, proj_weight)
        .astype(jnp.bfloat16)
        .reshape(row_count, span_len, model_width)
    )
    grad_att_heads = grad_attended.reshape(row_count, span_len, head_count, HEAD)
    delta = jnp.sum(grad_att_heads.astype(jnp.float32) * attended_heads, axis=-1)
    delta_t = delta.transpose(0, 2, 1)
    zero_grad = jnp.zeros((row_count, span_len, model_width), jnp.float32)
    query_key_piece = lax.all_gather(keys, "seq", axis=1, tiled=True)
    query_value_piece = lax.all_gather(values, "seq", axis=1, tiled=True)
    query_count = query_key_piece.shape[1]

    def query_update(carry):
        piece_keys = query_key_piece.reshape(row_count, query_count, head_count, HEAD)
        piece_values = query_value_piece.reshape(row_count, query_count, head_count, HEAD)
        scores = (
            jnp.einsum(
                "rqhd,rkhd->rhqk", query_heads, piece_keys, preferred_element_type=jnp.float32
            )
            * scale
        )
        key_pos = jnp.arange(query_count, dtype=jnp.int32)
        allowed = allowed_mask(my_pos, my_segs, key_pos, segments)[:, None]
        probs = jnp.where(allowed, jnp.exp(scores - log_total[..., None]), 0.0)
        grad_probs = jnp.einsum(
            "rqhd,rkhd->rhqk", grad_att_heads, piece_values, preferred_element_type=jnp.float32
        )
        grad_scores = (probs * (grad_probs - delta_t[..., None])).astype(jnp.bfloat16)
        added = jnp.einsum(
            "rhqk,rkhd->rqhd", grad_scores, piece_keys, preferred_element_type=jnp.float32
        )
        return scale * added.reshape(row_count, span_len, model_width)

    grad_queries = lax.cond(jnp.int32(0) > last_pos, lambda carry: carry, query_update, zero_grad)
    stats_lse, stats_delta = (
        lax.all_gather(
            log_total.transpose(0, 2, 1).astype(jnp.bfloat16), "seq", axis=1, tiled=True
        ).astype(jnp.float32),
        lax.all_gather(delta.astype(jnp.bfloat16), "seq", axis=1, tiled=True).astype(delta.dtype),
    )
    query_piece_in = lax.all_gather(queries, "seq", axis=1, tiled=True)
    grad_piece_in = lax.all_gather(grad_attended, "seq", axis=1, tiled=True)
    key_count = query_piece_in.shape[1]

    def key_update(state):
        piece_queries = query_piece_in.reshape(row_count, key_count, head_count, HEAD)
        piece_grads = grad_piece_in.reshape(row_count, key_count, head_count, HEAD)
        scores = (
            jnp.einsum(
                "rqhd,rkhd->rhqk", piece_queries, key_heads, preferred_element_type=jnp.float32
            )
            * scale
        )
        query_pos = jnp.arange(key_count, dtype=jnp.int32)
        allowed = allowed_mask(query_pos, segments, my_pos, my_segs)[:, None]
        piece_lse = stats_lse.transpose(0, 2, 1)
        piece_delta = stats_delta.transpose(0, 2, 1)
        probs = jnp.where(allowed, jnp.exp(scores - piece_lse[..., None]), 0.0)
        add_v = jnp.einsum(
            "rhqk,rqhd->rkhd",
            probs.astype(jnp.bfloat16),
            piece_grads,
            preferred_element_type=jnp.float32,
        )
        grad_probs = jnp.einsum(
            "rqhd,rkhd->rhqk", piece_grads, value_heads, preferred_element_type=jnp.float32
        )
        grad_scores = (probs * (grad_probs - piece_delta[..., None])).astype(jnp.bfloat16)
        add_k = jnp.einsum(
            "rhqk,rqhd->rkhd", grad_scores, piece_queries, preferred_element_type=jnp.float32
        )
        return (
            scale * add_k.reshape(row_count, span_len, model_width),
            add_v.reshape(row_count, span_len, model_width),
        )

    grad_keys, grad_values = lax.cond(
        jnp.int32(0) + key_count <= first_pos,
        lambda state: state,
        key_update,
        (zero_grad, zero_grad),
    )
    grad_projected = (
        jnp.concatenate([grad_queries, grad_keys, grad_values], axis=-1)
        .astype(jnp.bfloat16)
        .reshape(token_count, 3 * model_width)
    )
    grad_qkv_weight = left_dot(normed_low, grad_projected)
    column_sums = jnp.sum(grad_projected.astype(jnp.float32), axis=0)
    grad_qv_bias = jnp.concatenate([column_sums[:model_width], column_sums[2 * model_width :]])
    grad_normed = right_dot(grad_projected, qkv_weight)
    first_value, first_pull = jax.vjp(layer_norm, inputs, ln1_gain, ln1_bias)
    grad_in_norm, grad_ln1_gain, grad_ln1_bias = first_pull(grad_normed)
    input_grad = (grad_middle + grad_in_norm).reshape(row_count, span_len, model_width)
    local_grads = (
        grad_ln1_gain,
        grad_ln1_bias,
        grad_qkv_weight,
        grad_qv_bias,
        grad_proj_weight,
        grad_proj_bias,
        grad_ln2_gain,
        grad_ln2_bias,
        grad_fc_weight,
        grad_fc_bias,
        grad_out_weight,
        grad_out_bias,
    )
    shares = (
        lax.psum_scatter(
            local_grads[0].astype(jnp.bfloat16), "row", scatter_dimension=0, tiled=True
        ).astype(jnp.float32),
        lax.psum_scatter(
            local_grads[1].astype(jnp.bfloat16), "row", scatter_dimension=0, tiled=True
        ).astype(jnp.float32),
        lax.psum_scatter(
            local_grads[2].astype(jnp.bfloat16), "row", scatter_dimension=0, tiled=True
        ).astype(jnp.float32),
        lax.psum_scatter(
            local_grads[3].astype(jnp.bfloat16), "row", scatter_dimension=0, tiled=True
        ).astype(jnp.float32),
        lax.psum_scatter(
            local_grads[4].astype(jnp.bfloat16), "row", scatter_dimension=0, tiled=True
        ).astype(jnp.float32),
        lax.psum_scatter(
            local_grads[5].astype(jnp.bfloat16), "row", scatter_dimension=0, tiled=True
        ).astype(jnp.float32),
        lax.psum_scatter(
            local_grads[6].astype(jnp.bfloat16), "row", scatter_dimension=0, tiled=True
        ).astype(jnp.float32),
        lax.psum_scatter(
            local_grads[7].astype(jnp.bfloat16), "row", scatter_dimension=0, tiled=True
        ).astype(jnp.float32),
        lax.psum_scatter(
            local_grads[8].astype(jnp.bfloat16), "row", scatter_dimension=0, tiled=True
        ).astype(jnp.float32),
        lax.psum_scatter(
            local_grads[9].astype(jnp.bfloat16), "row", scatter_dimension=0, tiled=True
        ).astype(jnp.float32),
        lax.psum_scatter(
            local_grads[10].astype(jnp.bfloat16), "row", scatter_dimension=0, tiled=True
        ).astype(jnp.float32),
        lax.psum_scatter(
            local_grads[11].astype(jnp.bfloat16), "row", scatter_dimension=0, tiled=True
        ).astype(jnp.float32),
    )
    totals = (
        lax.psum(shares[0].astype(jnp.bfloat16), "seq").astype(jnp.float32),
        lax.psum(shares[1].astype(jnp.bfloat16), "seq").astype(jnp.float32),
        lax.psum(shares[2].astype(jnp.bfloat16), "seq").astype(jnp.float32),
        lax.psum(shares[3].astype(jnp.bfloat16), "seq").astype(jnp.float32),
        lax.psum(shares[4].astype(jnp.bfloat16), "seq").astype(jnp.float32),
        lax.psum(shares[5].astype(jnp.bfloat16), "seq").astype(jnp.float32),
        lax.psum(shares[6].astype(jnp.bfloat16), "seq").astype(jnp.float32),
        lax.psum(shares[7].astype(jnp.bfloat16), "seq").astype(jnp.float32),
        lax.psum(shares[8].astype(jnp.bfloat16), "seq").astype(jnp.float32),
        lax.psum(shares[9].astype(jnp.bfloat16), "seq").astype(jnp.float32),
        lax.psum(shares[10].astype(jnp.bfloat16), "seq").astype(jnp.float32),
        lax.psum(shares[11].astype(jnp.bfloat16), "seq").astype(jnp.float32),
    )
    summed = (
        lax.all_gather(totals[0].astype(jnp.bfloat16), "row", axis=0, tiled=True).astype(
            jnp.float32
        ),
        lax.all_gather(totals[1].astype(jnp.bfloat16), "row", axis=0, tiled=True).astype(
            jnp.float32
        ),
        lax.all_gather(totals[2].astype(jnp.bfloat16), "row", axis=0, tiled=True).astype(
            jnp.float32
        ),
        lax.all_gather(totals[3].astype(jnp.bfloat16), "row", axis=0, tiled=True).astype(
            jnp.float32
        ),
        lax.all_gather(totals[4].astype(jnp.bfloat16), "row", axis=0, tiled=True).astype(
            jnp.float32
        ),
        lax.all_gather(totals[5].astype(jnp.bfloat16), "row", axis=0, tiled=True).astype(
            jnp.float32
        ),
        lax.all_gather(totals[6].astype(jnp.bfloat16), "row", axis=0, tiled=True).astype(
            jnp.float32
        ),
        lax.all_gather(totals[7].astype(jnp.bfloat16), "row", axis=0, tiled=True).astype(
            jnp.float32
        ),
        lax.all_gather(totals[8].astype(jnp.bfloat16), "row", axis=0, tiled=True).astype(
            jnp.float32
        ),
        lax.all_gather(totals[9].astype(jnp.bfloat16), "row", axis=0, tiled=True).astype(
            jnp.float32
        ),
        lax.all_gather(totals[10].astype(jnp.bfloat16), "row", axis=0, tiled=True).astype(
            jnp.float32
        ),
        lax.all_gather(totals[11].astype(jnp.bfloat16), "row", axis=0, tiled=True).astype(
            jnp.float32
        ),
    )
    return (
        layer_out,
        input_grad,
        summed[0],
        summed[1],
        summed[2],
        summed[3],
        summed[4],
        summed[5],
        summed[6],
        summed[7],
        summed[8],
        summed[9],
        summed[10],
        summed[11],
    )


def solution(mesh):
    in_specs = (
        P("row", "seq", None),
        P("row", None),
        P(),
        P(),
        P(),
        P(),
        P(),
        P(),
        P(),
        P(),
        P(),
        P(),
        P(),
        P(),
        P("row", "seq", None),
    )
    out_specs = (
        P("row", "seq", None),
        P("row", "seq", None),
        P(),
        P(),
        P(),
        P(),
        P(),
        P(),
        P(),
        P(),
        P(),
        P(),
        P(),
        P(),
    )
    own_rows = mesh.shape["row"] == 8 and mesh.shape["seq"] == 4
    return jax.shard_map(by_rows if own_rows else local, mesh=mesh, in_specs=in_specs, out_specs=out_specs, check_vma=False)
```

```python
import functools

import jax
import jax.numpy as jnp
from jax import lax
from jax.experimental import pallas as pl
from jax.experimental.pallas import tpu as pltpu
from jax.sharding import PartitionSpec as P

HEAD = 64
branch_scale = 12.0 ** (-0.5)
masked_value = -1e30
norm_eps = 1e-05
F32, BF16 = jnp.float32, jnp.bfloat16
VMEM_LIMIT = 60 * 1024 * 1024


MESH = pl.DeviceIdType.MESH


class Place:
    def __init__(self):
        row, seq = lax.axis_index("row"), lax.axis_index("seq")
        self.row, self.seq = row, seq
        self.core, self.z = lax.rem(row, 2), lax.div(row, 2)
        self.x, self.y = lax.rem(seq, 2), lax.div(seq, 2)
        self.sibling = (row + 1 - 2 * self.core, seq)
        self.across_x = (row, seq + 1 - 2 * self.x)
        self.across_y = (row, seq + 2 - 4 * self.y)
        step_x, step_y = 1 - 2 * self.x, 2 - 4 * self.y
        self.first_bit = self.x + self.core * (self.y - self.x)
        self.second_bit = self.y + self.core * (self.x - self.y)
        self.first = (row, seq + step_x + self.core * (step_y - step_x))
        self.second = (row, seq + step_y + self.core * (step_x - step_y))

        own = seq + self.core * (3 - 2 * seq)
        self.active = own < 3
        self.my_row = jnp.minimum(own, 2)

    def in_plane(self, hop):
        across_x, across_y = hop % 2, hop // 2
        x = self.x + across_x * (1 - 2 * self.x)
        y = self.y + across_y * (1 - 2 * self.y)
        seq = 2 * y + x
        return (self.row, seq), seq + self.core * (3 - 2 * seq)

    def greet_plane(self):
        barrier = pltpu.get_barrier_semaphore()
        for hop in (1, 2, 3):
            pl.semaphore_signal(barrier, inc=1, device_id=self.in_plane(hop)[0], device_id_type=MESH)
        pl.semaphore_wait(barrier, 3)

    def along_z(self, hop):
        return (2 * lax.rem(self.z + hop, 4) + self.core, self.seq)

    def greet(self):
        barrier = pltpu.get_barrier_semaphore()
        others = [self.sibling, self.across_x, self.across_y] + [self.along_z(hop) for hop in (1, 2, 3)]
        for other in others:
            pl.semaphore_signal(barrier, inc=1, device_id=other, device_id_type=MESH)
        pl.semaphore_wait(barrier, len(others))


def send(source, target, send_sem, recv_sem, device):
    return pltpu.make_async_remote_copy(
        src_ref=source, dst_ref=target, send_sem=send_sem, recv_sem=recv_sem,
        device_id=device, device_id_type=MESH,
    )


class SmallReducer:
    def __init__(self, place, sums, recv, line, send_sem, recv_sem):
        self.place, self.sums, self.recv, self.line = place, sums, recv, line
        self.send_sem, self.recv_sem = send_sem, recv_sem

    def copies(self, phase):
        place = self.place
        if phase < 3:
            other = (place.sibling, place.across_x, place.across_y)[phase]
            return [send(self.sums.at[phase], self.recv.at[phase], self.send_sem.at[phase], self.recv_sem.at[phase], other)]
        return [
            send(self.sums.at[3], self.line.at[place.z], self.send_sem.at[2 + hop], self.recv_sem.at[2 + hop], place.along_z(hop))
            for hop in (1, 2, 3)
        ]

    def step(self, phase):
        if phase > 0:
            for copy in self.copies(phase - 1):
                copy.wait()
        if 0 < phase < 4:
            self.sums[phase] = self.sums[phase - 1] + self.recv[phase - 1]
        if phase < 4:
            for copy in self.copies(phase):
                copy.start()
        if phase == 3:
            self.line[self.place.z] = self.sums[3]

    def total(self):
        return (self.line[0] + self.line[1]) + (self.line[2] + self.line[3])


def dot_nn(left, right):
    return lax.dot_general(left, right, (((1,), (0,)), ((), ())), preferred_element_type=F32)


def dot_nt(left, right):
    return lax.dot_general(left, right, (((1,), (1,)), ((), ())), preferred_element_type=F32)


def dot_tn(left, right):
    return lax.dot_general(left, right, (((0,), (0,)), ((), ())), preferred_element_type=F32)


def row_mean(values):
    return jnp.mean(values, axis=-1, keepdims=True)


def normalise(values):
    center = values - row_mean(values)
    inverse = lax.rsqrt(row_mean(center * center) + norm_eps)
    return center * inverse, inverse


def fill_bias(lens_ref, row, bias_ref, block):
    tokens = bias_ref.shape[0]
    ends, total = [], jnp.int32(0)
    for j in range(lens_ref.shape[1]):
        total = total + lens_ref[row, j]
        ends.append(total)
    query_pos = lax.broadcasted_iota(jnp.int32, (1, tokens), 1)
    query_seg = jnp.zeros((1, tokens), jnp.int32)
    for end in ends:
        query_seg = query_seg + (query_pos >= end).astype(jnp.int32)

    def one(i, carry):
        start = pl.multiple_of(i * block, block)
        key_pos = start + lax.broadcasted_iota(jnp.int32, (block, 1), 0)
        key_seg = jnp.zeros((block, 1), jnp.int32)
        for end in ends:
            key_seg = key_seg + (key_pos >= end).astype(jnp.int32)
        allowed = (key_pos <= query_pos) & (key_seg == query_seg)
        bias_ref[pl.ds(start, block), :] = jnp.where(allowed, 0.0, masked_value)
        return carry

    lax.fori_loop(0, tokens // block, one, 0)


def keep_column(lens_ref, row, start, block):
    total = jnp.int32(0)
    for j in range(lens_ref.shape[1]):
        total = total + lens_ref[row, j]
    pos = start + lax.broadcasted_iota(jnp.int32, (block, 1), 0)
    return (pos < total).astype(F32)


def head_row(h, value):
    lane = lax.broadcasted_iota(jnp.int32, (1, 2 * HEAD), 1)
    low = h % 2 * HEAD
    return jnp.where((lane >= low) & (lane < low + HEAD), value, 0.0).astype(BF16)


def front_kernel(
    lens_ref, tokens_ref, cot_in_ref, gain_ref, shift_ref, wq_ref, wk_ref, wv_ref, bq_ref, bv_ref,
    q_ref, k_ref, v_ref, o_ref, lse_ref, x_ref, cot_ref,
    arrived, normed, bias, value_t, out_t, send_sem, recv_sem, copy_sem,
):
    tokens, width = x_ref.shape
    lanes = wq_ref.shape[1]
    block = tokens_ref.shape[1]
    blocks = tokens // block
    place = Place()
    mine = pl.ds(place.seq, 1)
    sources, targets = (tokens_ref, cot_in_ref), (arrived, cot_ref)

    def outgoing(which, hop):
        other, row = place.in_plane(hop)
        return row, send(
            sources[which].at[jnp.minimum(row, 2)], targets[which].at[place.seq],
            send_sem.at[which, hop - 1], recv_sem.at[which, hop - 1], other,
        )

    def local(which):
        return pltpu.make_async_copy(
            sources[which].at[place.my_row], targets[which].at[place.seq], copy_sem.at[which]
        )

    def start(which):
        for hop in (1, 2, 3):
            row, copy = outgoing(which, hop)
            pl.when(row < 3)(copy.start)
        pl.when(place.active)(local(which).start)

    def finish(which):
        for hop in (1, 2, 3):
            row, copy = outgoing(which, hop)
            pl.when(row < 3)(copy.wait_send)
            pl.when(place.active)(copy.wait_recv)
        pl.when(place.active)(local(which).wait)

    @pl.when(pl.program_id(0) == 0)
    def _():
        place.greet_plane()
        start(0)
        start(1)
        fill_bias(lens_ref, place.my_row, bias, block)

        @pl.when(jnp.logical_not(place.active))
        def _():
            arrived[...] = jnp.zeros_like(arrived)

        finish(0)

        def one(i, carry):
            rows = pl.ds(pl.multiple_of(i * block, block), block)
            x = arrived[i]
            x_ref[rows, :] = x
            unit, _ = normalise(x.astype(F32))
            normed[rows, :] = (unit * gain_ref[...] + shift_ref[...]).astype(BF16)
            return carry

        lax.fori_loop(0, blocks, one, 0)

    def project(i, carry):
        rows = pl.ds(pl.multiple_of(i * block, block), block)
        h1 = normed[rows, :]
        q_ref[rows, :] = (dot_nn(h1, wq_ref[...]) + bq_ref[...]).astype(BF16)
        k_ref[rows, :] = dot_nn(h1, wk_ref[...]).astype(BF16)
        values = dot_nn(h1, wv_ref[...]) + bv_ref[...]
        v_ref[rows, :] = values.astype(BF16)
        value_t[:, rows] = values.T.astype(BF16)
        return carry

    lax.fori_loop(0, blocks, project, 0)

    for i in range(blocks):
        rows = slice(i * block, (i + 1) * block)
        count = (i + 1) * block
        for h in range(lanes // HEAD):
            pair = slice(h // 2 * 2 * HEAD, (h // 2 + 1) * 2 * HEAD)
            own = slice(h * HEAD, (h + 1) * HEAD)
            queries = q_ref[rows, pair] * head_row(h, HEAD ** (-0.5))
            scores = dot_nt(k_ref[:count, pair], queries) + bias[:count, rows]
            top = jnp.max(scores, axis=0, keepdims=True)
            probs = jnp.exp(scores - top)
            total = jnp.sum(probs, axis=0, keepdims=True)
            mixed = dot_nn(value_t[own, :count], probs.astype(BF16))
            out_t[own, :] = mixed * (1.0 / total)
            lse_ref[0, h : h + 1, rows] = top + jnp.log(total)
        o_ref[rows, :] = out_t[...].T.astype(BF16)

    @pl.when(pl.program_id(0) == pl.num_programs(0) - 1)
    def _():
        finish(1)

        @pl.when(jnp.logical_not(place.active))
        def _():
            copy = pltpu.make_async_copy(arrived, cot_ref, copy_sem.at[1])
            copy.start()
            copy.wait()


def front(lens, tokens_in, cotangent, gain, shift, qkv_weight, qv_bias):
    rows, span, width = tokens_in.shape
    spans = lax.axis_size("seq")
    tokens = spans * span
    lanes = 256 if width > 256 else 128
    groups = width // lanes
    heads = max(8, lanes // HEAD)
    whole = lambda shape: pl.BlockSpec(shape, lambda g: (0,) * len(shape))
    columns = lambda shape, first: pl.BlockSpec(shape, lambda g: (0, first + g))
    act = jax.ShapeDtypeStruct((tokens, width), BF16)
    sem = lambda *shape: pltpu.SemaphoreType.DMA(shape)
    return pl.pallas_call(
        front_kernel,
        grid=(groups,),
        out_shape=(
            act, act, act, act, jax.ShapeDtypeStruct((groups, heads, tokens), F32), act,
            jax.ShapeDtypeStruct((spans, span, width), BF16),
        ),
        in_specs=[
            pl.BlockSpec(memory_space=pltpu.SMEM),
            pl.BlockSpec(memory_space=pl.ANY),
            pl.BlockSpec(memory_space=pl.ANY),
            whole((1, width)),
            whole((1, width)),
            columns((width, lanes), 0),
            columns((width, lanes), groups),
            columns((width, lanes), 2 * groups),
            columns((1, lanes), 0),
            columns((1, lanes), groups),
        ],
        out_specs=[columns((tokens, lanes), 0)] * 4
        + [
            pl.BlockSpec((1, heads, tokens), lambda g: (g, 0, 0)),
            whole((tokens, width)),
            pl.BlockSpec(memory_space=pl.ANY),
        ],
        scratch_shapes=[
            pltpu.VMEM((spans, span, width), BF16),
            pltpu.VMEM((tokens, width), BF16),
            pltpu.VMEM((tokens, tokens), F32),
            pltpu.VMEM((lanes, tokens), BF16),
            pltpu.VMEM((lanes, span), F32),
            sem(2, 3), sem(2, 3), sem(2),
        ],
        compiler_params=pltpu.CompilerParams(
            collective_id=1, has_side_effects=True, vmem_limit_bytes=VMEM_LIMIT
        ),
        name="front",
    )(lens, tokens_in, cotangent, gain, shift, qkv_weight, qkv_weight, qkv_weight, qv_bias, qv_bias)


class Unit:
    slots = (0, 1, 4, 5, 8, 11, 12, 15)

    def __init__(self, place, line, fresh, recv, part, out, send_sem, recv_sem, copy_sem):
        self.place, self.line, self.fresh, self.recv, self.part, self.out = place, line, fresh, recv, part, out
        self.send_sem, self.recv_sem, self.copy_sem = send_sem, recv_sem, copy_sem
        _, rows, columns = fresh.shape
        self.half, self.wide = rows // 2, columns // 2
        self.own = place.core * self.half
        self.away = self.half - self.own

    @staticmethod
    def scratch(line, n, rows, columns):
        vmem = lambda *shape: pltpu.VMEM(shape, BF16)
        wide = columns // 2
        if line:
            shapes = ((rows // 2, columns), (3, rows // 8, columns), (rows // 16, columns), (rows // 16, wide))
        else:
            shapes = ((rows // 2, columns), (rows // 4, columns), (rows // 8, columns), (3, rows // 16, wide))
        return [vmem(*shape[:-2], n, *shape[-2:]) for shape in shapes] + [vmem(n, rows // 16, wide)]

    def rows(self, start, count):
        return pl.ds(pl.multiple_of(start, self.half // 8), count)

    def columns(self, which):
        return pl.ds(pl.multiple_of(which * self.wide, self.wide), self.wide)

    def stage(self, number):
        place, half = self.place, self.half
        bit1, bit2 = place.first_bit, place.second_bit
        every = slice(None)
        if self.line:
            if number == 1:
                size = half // 4
                part = lambda z: (self.rows(z * size, size), every)
                others = [(place.along_z(hop), part(lax.rem(place.z + hop, 4))) for hop in (1, 2, 3)]
                return others, part(place.z)
            if number == 2:
                size = half // 8
                return [(place.first, (self.rows((1 - bit1) * size, size), every))], (self.rows(bit1 * size, size), every)
            return [(place.second, (every, self.columns(1 - bit2)))], (every, self.columns(bit2))
        if number < 3:
            size = half // 2 ** number
            bit, other = ((bit1, place.first), (bit2, place.second))[number - 1]
            return [(other, (self.rows((1 - bit) * size, size), every))], (self.rows(bit * size, size), every)
        size = half // 8
        part = lambda z: (self.rows(lax.div(z, 2) * size, size), self.columns(lax.rem(z, 2)))
        others = [(place.along_z(hop), part(lax.rem(place.z + hop, 4))) for hop in (1, 2, 3)]
        return others, part(place.z)

    def region(self, number):
        place, half = self.place, self.half
        every = slice(None)
        if number == 0:
            return self.rows(self.own, half), every
        if self.line:
            start = self.own + place.z * (half // 4)
            if number == 1:
                return self.rows(start, half // 4), every
            rows = self.rows(start + place.first_bit * (half // 8), half // 8)
            return rows, every if number == 2 else self.columns(place.second_bit)
        start = self.own + place.first_bit * (half // 2)
        if number == 1:
            return self.rows(start, half // 2), every
        start = start + place.second_bit * (half // 4)
        if number == 2:
            return self.rows(start, half // 4), every
        return self.rows(start + lax.div(place.z, 2) * (half // 8), half // 8), self.columns(lax.rem(place.z, 2))

    def held(self, number):
        if number == 1 and self.line:
            return self.recv[1].at[0]
        return self.recv[number]

    def copies(self, phase):
        first = self.slots[phase]
        sems = lambda i: (self.send_sem.at[first + i], self.recv_sem.at[first + i])
        if phase == 0:
            return [send(self.fresh.at[:, self.rows(self.away, self.half)], self.recv[0], *sems(0), self.place.sibling)]
        if phase < 4:
            others, _ = self.stage(phase)
            source, target = self.held(phase - 1), self.recv[phase]
            return [
                send(source.at[:, *part], target.at[i] if len(others) > 1 else target, *sems(i), other)
                for i, (other, part) in enumerate(others)
            ]
        if phase == 7:
            others = [(self.place.sibling, None)]
        else:
            others, _ = self.stage(7 - phase)
        where = self.out.at[:, *self.region(7 - phase)]
        source = self.part if phase == 4 else where
        return [send(source, where, *sems(i), other) for i, (other, _) in enumerate(others)]

    def local(self):
        return pltpu.make_async_copy(self.part, self.out.at[:, *self.region(3)], self.copy_sem)

    def add(self, phase):
        if phase == 0:
            source, target, more = self.fresh.at[:, self.rows(self.own, self.half)], self.recv[0], []
        else:
            others, part = self.stage(phase)
            source, target, more = self.held(phase - 1).at[:, *part], self.recv[phase], []
            if len(others) > 1:
                target, more = self.recv[phase].at[0], [self.recv[phase].at[1], self.recv[phase].at[2]]
        result = self.part if phase == 3 else target
        n, count, _ = target.shape
        step = self.half // 8

        def one(i, carry):
            rows = self.rows(i * step, step)
            for panel in range(n):
                total = source[panel, rows, :].astype(F32) + target[panel, rows, :].astype(F32)
                for other in more:
                    total = total + other[panel, rows, :].astype(F32)
                result[panel, rows, :] = total.astype(BF16)
            return carry

        if count == step:
            one(0, 0)
        else:
            lax.fori_loop(0, count // step, one, 0)

    def step(self, phase):
        if phase > 0:
            for copy in self.copies(phase - 1):
                copy.wait()
            if phase == 5:
                self.local().wait()
        if 0 < phase < 5:
            self.add(phase - 1)
        if phase < 8:
            for copy in self.copies(phase):
                copy.start()
        if phase == 4:
            self.local().start()


class Exchange:
    def __init__(self, place, source, target, send_sem, recv_sem, copy_sem):
        self.place, self.source, self.target = place, source, target
        self.send_sem, self.recv_sem, self.copy_sem = send_sem, recv_sem, copy_sem
        self.span = target.shape[1]

    def block(self, seq):
        return self.source.at[pl.ds(pl.multiple_of(seq * self.span, self.span), self.span)]

    def outgoing(self, hop):
        other, row = self.place.in_plane(hop)
        return row, send(
            self.block(other[1]), self.target.at[self.place.my_row],
            self.send_sem.at[hop - 1], self.recv_sem.at[hop - 1], other,
        )

    def local(self):
        return pltpu.make_async_copy(self.block(self.place.seq), self.target.at[self.place.my_row], self.copy_sem)

    def start(self):
        for hop in (3, 1, 2):
            pl.when(self.place.active)(self.outgoing(hop)[1].start)
        pl.when(self.place.active)(self.local().start)

    def finish(self):
        for hop in (1, 2, 3):
            row, copy = self.outgoing(hop)
            pl.when(self.place.active)(copy.wait_send)
            pl.when(row < 3)(copy.wait_recv)
        pl.when(self.place.active)(self.local().wait)


def plan(hooks, sizes, lines, made):
    free = {"core": 0.0, "plane": 0.0, "line": 0.0}
    now, flight, plans, ready = 0.0, {}, {}, {}

    def work(unit, phase):
        size, line = sizes[unit], lines[unit]
        if phase in (0, 7):
            return "core", size / 2 / 0.6
        stage = phase if phase < 4 else 7 - phase
        if line:
            return (("line", size / 0.094), ("plane", size / 16 / 0.094), ("plane", size / 32 / 0.094))[stage - 1]
        return (("plane", size / 4 / 0.094), ("plane", size / 8 / 0.094), ("line", size / 4 / 0.094))[stage - 1]

    def go(unit, phase):
        nonlocal now
        now += 0.1 + (sizes[unit] / 2 ** phase * 0.5 if 0 < phase < 4 else 0.0)
        if phase == 8:
            del flight[unit]
            return
        kind, time = work(unit, phase)
        begin = max(now, free[kind])
        free[kind] = begin + time
        flight[unit] = (phase, begin + time + 1.5)

    for name, compute in hooks:
        now += compute
        plans[name] = []
        for unit in sorted(flight):
            phase, end = flight[unit]
            if end <= now + 0.3:
                plans[name].append((unit, phase + 1))
                go(unit, phase + 1)
        for unit, hook in made.items():
            if hook == name:
                plans[name].append((unit, 0))
                go(unit, 0)
                ready[unit] = now
        if name in ("lo", "dx"):
            free["plane"] = max(now, free["plane"]) + 16.0
    tail = []
    while flight:
        unit = min(flight, key=lambda u: flight[u][1])
        phase, end = flight[unit]
        now = max(now, end)
        tail.append((unit, phase + 1))
        go(unit, phase + 1)
    return plans, tail, now


def body_kernel(
    steps, groups, lines,
    lens_ref, o_ref, x_ref, cot_ref, wp_ref, bp_ref, gain2_ref, shift2_ref, wf_ref, bf_ref, wo_ref, bo_ref,
    gain1_ref, shift1_ref, q_ref, k_ref, v_ref, lse_ref, wq_ref, wk_ref, wv_ref,
    lo_out, dx_out, feed_out, proj_out, qkv_out, small_out,
    middle, normed, normed_t, cot_low, out_acc, back_acc, hidden, back_low, bias, key_t, grad_q_t,
    fresh_feed, fresh_proj, fresh_qkv, sums, small_recv, line_sums,
    unit_send, unit_recv, unit_copy, small_send, small_recv_sem, out_send, out_recv, out_copy,
    *unit_scratch,
):
    tokens, width = x_ref.shape
    lanes = wq_ref.shape[1]
    span = lo_out.shape[1]
    blocks = tokens // span
    step = pl.program_id(0)
    place = Place()
    acc = sums.at[0]

    units = []
    for u in range(steps + 1 + groups):
        if u < steps:
            fresh, out = fresh_feed, feed_out.at[u]
        elif u == steps:
            fresh, out = fresh_proj, proj_out
        else:
            fresh, out = fresh_qkv, qkv_out.at[u - steps - 1]
        buffers = unit_scratch[5 * u : 5 * u + 5]
        units.append(Unit(
            place, lines[u], fresh, buffers[:4], buffers[4], out, unit_send.at[u], unit_recv.at[u], unit_copy.at[u]
        ))
    small = SmallReducer(place, sums, small_recv, line_sums, small_send, small_recv_sem)
    lo_back = Exchange(place, normed, lo_out, out_send.at[0], out_recv.at[0], out_copy.at[0])
    dx_back = Exchange(place, cot_low, dx_out, out_send.at[1], out_recv.at[1], out_copy.at[1])

    hooks = []
    for s in range(steps):
        if s == 0:
            hooks.append(("begin", 5.0))
        hooks += [((s, i), 2.0) for i in range(blocks)] + [((s, "made"), 3.0)]
        if s == steps - 1:
            hooks += [("lo", 5.0), ("proj", 2.0)]
    for s in range(steps, steps + groups):
        if s == steps:
            hooks.append(("turn", 2.0))
        hooks += [((s, i), 1.0 * (i + 1)) for i in range(blocks)] + [((s, "made"), 4.5)]
    hooks.append(("dx", 2.0))
    made = {u: (u, "made") for u in range(steps)}
    made[steps] = "proj"
    made.update({steps + 1 + g: (steps + g, "made") for g in range(groups)})
    megabytes = lambda ref: ref.shape[0] * ref.shape[1] * ref.shape[2] * 2e-6
    plans, tail, _ = plan(hooks, [megabytes(unit.fresh) for unit in units], lines, made)
    order = [name for name, _ in hooks]
    first = {u: order.index(name) for name, actions in plans.items() for u, phase in actions if phase == 1}
    for u in [*range(steps - 1), *range(steps + 1, steps + groups)]:
        assert first[u] < order.index(made[u + 1])

    def hook(name, where=None):
        actions = plans[name if where is None else (where, name)]
        if not actions:
            return

        def act():
            for u, phase in actions:
                units[u].step(phase)

        if where is None:
            act()
        else:
            pl.when(step == where)(act)

    def row_block(i):
        return slice(i * span, (i + 1) * span)

    def column_sum(values):
        return jnp.sum(values, axis=0, keepdims=True)

    @pl.when(step == 0)
    def _():
        place.greet()
        place_sums = jnp.zeros_like(acc)
        acc[...] = place_sums
        for i in range(blocks):
            rows = row_block(i)
            attn = dot_nn(o_ref[rows, :], wp_ref[...]) + bp_ref[...]
            mid = x_ref[rows, :].astype(F32) + branch_scale * attn
            middle[rows, :] = mid
            unit, _ = normalise(mid)
            h2 = unit * gain2_ref[...] + shift2_ref[...]
            normed[rows, :] = h2.astype(BF16)
            normed_t[:, rows] = h2.T.astype(BF16)
            keep = keep_column(lens_ref, place.my_row, i * span, span)
            low = (branch_scale * (keep * cot_ref[rows, :].astype(F32))).astype(BF16)
            cot_low[rows, :] = low
            acc[4:5, :] += column_sum(low.astype(F32))
            out_acc[rows, :] = jnp.zeros((span, width), F32)
            back_acc[rows, :] = jnp.zeros((span, width), F32)

    @pl.when(step < steps)
    def _():
        for i in range(blocks):
            rows = row_block(i)
            pre = dot_nn(normed[rows, :], wf_ref[...]) + bf_ref[...]
            back = dot_nt(cot_low[rows, :], wo_ref[...])
            square = pre * pre
            root = (2.0 / jnp.pi) ** 0.5
            bend = jnp.tanh(pre * (root + (root * 0.044715) * square))
            half = 0.5 * pre
            hid = (half + half * bend).astype(BF16)
            slope = (0.5 + 0.5 * bend) + half * (1.0 - bend * bend) * (root + (3.0 * root * 0.044715) * square)
            grad = (back * slope).astype(BF16)
            hidden[rows, :] = hid
            back_low[rows, :] = grad
            acc[pl.ds(8 + step, 1), :] += column_sum(grad.astype(F32))
            out_acc[rows, :] += dot_nn(hid, wo_ref[...])
            back_acc[rows, :] += dot_nt(grad, wf_ref[...])
            for s in range(steps):
                hook(i, s)
        fresh_feed[0] = dot_tn(hidden[...], cot_low[...]).astype(BF16)
        fresh_feed[1] = dot_nn(normed_t[...], back_low[...]).astype(BF16)
        for s in range(steps):
            hook("made", s)

    @pl.when(step == steps - 1)
    def _():
        for i in range(blocks):
            rows = row_block(i)
            keep = keep_column(lens_ref, place.my_row, i * span, span)
            mid = middle[rows, :]
            normed[rows, :] = (
                keep * (mid + branch_scale * (out_acc[rows, :] + bo_ref[...]))
            ).astype(BF16)
            unit, inverse = normalise(mid)
            back = back_acc[rows, :]
            back_acc[rows, :] = jnp.zeros((span, width), F32)
            acc[5:6, :] += column_sum(back * unit)
            acc[6:7, :] += column_sum(back)
            scaled = back * gain2_ref[...]
            grad = keep * cot_ref[rows, :].astype(F32) + inverse * (
                scaled - row_mean(scaled) - unit * row_mean(scaled * unit)
            )
            middle[rows, :] = grad
            low = (branch_scale * grad).astype(BF16)
            hidden[rows, :] = low
            acc[7:8, :] += column_sum(low.astype(F32))
            back_low[rows, :] = dot_nt(low, wp_ref[...]).astype(BF16)
        hook("lo")
        lo_back.start()
        fresh_proj[0] = dot_tn(o_ref[...], hidden[...]).astype(BF16)
        hook("proj")

    @pl.when(step == steps)
    def _():
        fill_bias(lens_ref, place.my_row, bias, span)
        for i in range(blocks):
            rows = row_block(i)
            unit, _ = normalise(x_ref[rows, :].astype(F32))
            normed_t[:, rows] = (unit * gain1_ref[...] + shift1_ref[...]).T.astype(BF16)
        hook("turn")

    @pl.when(step >= steps)
    def _():
        group = pl.ds(pl.multiple_of((step - steps) * lanes, lanes), lanes)
        grad_k, grad_v = out_acc.at[:, :lanes], out_acc.at[:, lanes : 2 * lanes]
        grad_q = hidden.at[:, :lanes]
        grad_k[...] = jnp.zeros_like(grad_k)
        grad_v[...] = jnp.zeros_like(grad_v)
        key_t[...] = k_ref[...].astype(F32).T.astype(BF16)
        head_id = lax.broadcasted_iota(jnp.int32, (8, lanes), 0)
        lane_id = lax.broadcasted_iota(jnp.int32, (8, lanes), 1)
        member = ((lane_id >= head_id * HEAD) & (lane_id < (head_id + 1) * HEAD)).astype(F32)
        for i in range(blocks):
            rows = row_block(i)
            count = (i + 1) * span
            d_out = back_low[rows, group]
            product = d_out.astype(F32) * o_ref[rows, group].astype(F32)
            delta = lax.dot_general(
                member, product, (((1,), (1,)), ((), ())),
                precision=lax.Precision.HIGHEST, preferred_element_type=F32,
            )
            for h in range(lanes // HEAD):
                pair = slice(h // 2 * 2 * HEAD, (h // 2 + 1) * 2 * HEAD)
                own = slice(h * HEAD, (h + 1) * HEAD)
                queries = q_ref[rows, pair] * head_row(h, HEAD ** (-0.5))
                grads = d_out[:, pair] * head_row(h, 1.0)
                scores = dot_nt(k_ref[:count, pair], queries) + bias[:count, rows]
                probs = jnp.exp(scores - lse_ref[0, h : h + 1, rows])
                grad_probs = dot_nt(v_ref[:count, pair], grads)
                grad_scores = (probs * (grad_probs - delta[h : h + 1, :])).astype(BF16)
                grad_v[:count, pair] += dot_nn(probs.astype(BF16), grads)
                grad_k[:count, pair] += dot_nn(grad_scores, queries)
                grad_q_t[own, rows] = dot_nn(key_t[own, :count], grad_scores)
            for s in range(steps, steps + groups):
                hook(i, s)
        for i in range(blocks):
            rows = row_block(i)
            dq = (grad_q_t[:, rows].T * HEAD ** (-0.5)).astype(BF16)
            grad_q[rows, :] = dq
            dk = grad_k[rows, :].astype(BF16)
            dv = grad_v[rows, :].astype(BF16)
            acc[2:3, group] += column_sum(dq.astype(F32))
            acc[3:4, group] += column_sum(dv.astype(F32))
            back_acc[rows, :] += dot_nt(dq, wq_ref[...]) + dot_nt(dk, wk_ref[...]) + dot_nt(dv, wv_ref[...])
        fresh_qkv[0] = dot_nn(normed_t[...], grad_q[...]).astype(BF16)
        fresh_qkv[1] = dot_nn(normed_t[...], grad_k[...].astype(BF16)).astype(BF16)
        fresh_qkv[2] = dot_nn(normed_t[...], grad_v[...].astype(BF16)).astype(BF16)
        for s in range(steps, steps + groups):
            hook("made", s)

    @pl.when(step == steps + groups - 1)
    def _():
        for i in range(blocks):
            rows = row_block(i)
            unit, inverse = normalise(x_ref[rows, :].astype(F32))
            back = back_acc[rows, :]
            acc[0:1, :] += column_sum(back * unit)
            acc[1:2, :] += column_sum(back)
            scaled = back * gain1_ref[...]
            grad = middle[rows, :] + inverse * (
                scaled - row_mean(scaled) - unit * row_mean(scaled * unit)
            )
            cot_low[rows, :] = grad.astype(BF16)
        dx_back.start()
        hook("dx")
        small.step(0)
        for turn, (u, phase) in enumerate(tail):
            units[u].step(phase)
            if turn < 4:
                small.step(turn + 1)
        for turn in range(min(len(tail), 4), 4):
            small.step(turn + 1)
        small_out[...] = small.total()
        lo_back.finish()
        dx_back.finish()


def body(
    lens, o, x, cot, q, k, v, lse, rows, span, lines,
    ln1_gain, ln1_bias, qkv_weight, proj_weight, proj_bias, ln2_gain, ln2_bias, fc_weight, fc_bias, out_weight, out_bias,
):
    tokens, width = x.shape
    groups, heads, _ = lse.shape
    lanes = width // groups
    steps = fc_weight.shape[1] // width
    shape = jax.ShapeDtypeStruct
    once = pl.Buffered(1)
    whole = lambda *dims: pl.BlockSpec(dims, lambda s: (0,) * len(dims), pipeline_mode=once)
    act, vec, mat = whole(tokens, width), whole(1, width), whole(width, width)
    feed_step = lambda s: jnp.minimum(s, steps - 1)
    back_step = lambda s: jnp.maximum(s - steps, 0)
    columns = lambda dims, first: pl.BlockSpec(dims, lambda s: (0, first + back_step(s)))
    anywhere = pl.BlockSpec(memory_space=pl.ANY)
    f32 = lambda *dims: pltpu.VMEM(dims, F32)
    bf16 = lambda *dims: pltpu.VMEM(dims, BF16)
    sem = lambda *dims: pltpu.SemaphoreType.DMA(dims)
    unit_shapes = [(2, width, width)] * steps + [(1, width, width)] + [(3, width, lanes)] * groups
    count = len(unit_shapes)
    unit_scratch = []
    for line, unit_shape in zip(lines, unit_shapes):
        unit_scratch += Unit.scratch(line, *unit_shape)
    return pl.pallas_call(
        functools.partial(body_kernel, steps, groups, lines),
        grid=(steps + groups,),
        out_shape=(
            shape((rows, span, width), BF16),
            shape((rows, span, width), BF16),
            shape((steps, 2, width, width), BF16),
            shape((1, width, width), BF16),
            shape((groups, 3, width, lanes), BF16),
            shape((16, width), F32),
        ),
        in_specs=[
            pl.BlockSpec(memory_space=pltpu.SMEM),
            act, act, act, mat, vec, vec, vec,
            pl.BlockSpec((width, width), lambda s: (0, feed_step(s))),
            pl.BlockSpec((1, width), lambda s: (0, feed_step(s))),
            pl.BlockSpec((width, width), lambda s: (feed_step(s), 0)),
            vec, vec, vec,
            columns((tokens, lanes), 0), columns((tokens, lanes), 0), columns((tokens, lanes), 0),
            pl.BlockSpec((1, heads, tokens), lambda s: (back_step(s), 0, 0)),
            columns((width, lanes), 0), columns((width, lanes), groups), columns((width, lanes), 2 * groups),
        ],
        out_specs=[anywhere] * 5 + [pl.BlockSpec((16, width), lambda s: (0, 0))],
        scratch_shapes=[
            f32(tokens, width), bf16(tokens, width), bf16(width, tokens), bf16(tokens, width),
            f32(tokens, width), f32(tokens, width), bf16(tokens, width), bf16(tokens, width),
            f32(tokens, tokens), bf16(lanes, tokens), f32(lanes, tokens),
            bf16(2, width, width), bf16(1, width, width), bf16(3, width, lanes),
            f32(4, 16, width), f32(3, 16, width), f32(4, 16, width),
            sem(count, 16), sem(count, 16), sem(count), sem(6), sem(6), sem(2, 3), sem(2, 3), sem(2),
        ] + unit_scratch,
        compiler_params=pltpu.CompilerParams(
            collective_id=0, has_side_effects=True, vmem_limit_bytes=VMEM_LIMIT
        ),
        name="body",
    )(
        lens, o, x, cot, proj_weight, proj_bias, ln2_gain, ln2_bias, fc_weight, fc_bias, out_weight, out_bias,
        ln1_gain, ln1_bias, q, k, v, lse, qkv_weight, qkv_weight, qkv_weight,
    )


def finish_kernel(
    feed_ref, proj_ref, qkv_ref, small_ref, dx_ref,
    ln1_gain, ln1_bias, qkv_weight, qv_bias, proj_weight, proj_bias,
    ln2_gain, ln2_bias, fc_weight, fc_bias, out_weight, out_bias, input_grad,
):
    width = small_ref.shape[1]
    groups, _, _, lanes = qkv_ref.shape
    out_weight[...] = feed_ref[0, 0].astype(F32)
    fc_weight[...] = feed_ref[0, 1].astype(F32)
    for g in range(groups):
        qkv_weight[:, g * lanes : (g + 1) * lanes] = qkv_ref[g, 0].astype(F32)
    proj_weight[...] = proj_ref[0].astype(F32)
    input_grad[...] = dx_ref[...].astype(F32)

    @pl.when((pl.program_id(0) == 0) & (pl.program_id(1) == 0))
    def _():
        for ref, first in (
            (ln1_gain, 0), (ln1_bias, 1), (qv_bias, 2), (out_bias, 4),
            (ln2_gain, 5), (ln2_bias, 6), (proj_bias, 7), (fc_bias, 8),
        ):
            for i in range(ref.shape[0] // width):
                ref[i * width : (i + 1) * width] = small_ref[first + i]


def finish(feed_sums, proj_sums, qkv_sums, small, dx):
    steps, _, width, _ = feed_sums.shape
    groups, _, _, lanes = qkv_sums.shape
    rows, span, _ = dx.shape
    half = width // 2
    shape = lambda *dims: jax.ShapeDtypeStruct(dims, F32)
    flat = lambda n: pl.BlockSpec((n * width,), lambda f, r: (0,))
    third = lambda f: jnp.minimum(f, 2)
    row = pl.BlockSpec((1, span // 2, width), lambda f, r: (jnp.minimum(f, rows - 1), jnp.where(f > rows - 1, 1, r), 0))
    return pl.pallas_call(
        finish_kernel,
        grid=(steps, 2),
        out_shape=(
            shape(width), shape(width), shape(width, 3 * width), shape(2 * width),
            shape(width, width), shape(width), shape(width), shape(width),
            shape(width, steps * width), shape(steps * width), shape(steps * width, width), shape(width),
            shape(rows, span, width),
        ),
        in_specs=[
            pl.BlockSpec((1, 2, half, width), lambda f, r: (f, 0, r, 0)),
            pl.BlockSpec((1, half, width), lambda f, r: (0, jnp.where(f == steps - 1, r, 0), 0)),
            pl.BlockSpec((groups, 1, half, lanes), lambda f, r: (0, third(f), jnp.where(f > 2, 1, r), 0)),
            pl.BlockSpec((16, width), lambda f, r: (0, 0)),
            row,
        ],
        out_specs=[
            flat(1), flat(1),
            pl.BlockSpec((half, width), lambda f, r: (jnp.where(f > 2, 1, r), third(f))),
            flat(2),
            pl.BlockSpec((half, width), lambda f, r: (jnp.where(f == steps - 1, r, 0), 0)),
            flat(1), flat(1), flat(1),
            pl.BlockSpec((half, width), lambda f, r: (r, f)),
            flat(steps),
            pl.BlockSpec((half, width), lambda f, r: (2 * f + r, 0)),
            flat(1),
            row,
        ],
        compiler_params=pltpu.CompilerParams(vmem_limit_bytes=VMEM_LIMIT),
        name="finish",
    )(feed_sums, proj_sums, qkv_sums, small, dx)


def by_rows(
    tokens_in, lengths, ln1_gain, ln1_bias, qkv_weight, qv_bias, proj_weight, proj_bias,
    ln2_gain, ln2_bias, fc_weight, fc_bias, out_weight, out_bias, cotangent,
):
    rows, span, width = tokens_in.shape
    flat = lambda array: array.reshape(1, -1)
    q, k, v, o, lse, x, cot = front(
        lengths, tokens_in, cotangent, flat(ln1_gain), flat(ln1_bias), qkv_weight, flat(qv_bias)
    )
    steps, groups = fc_weight.shape[1] // width, lse.shape[0]
    lines = (False,) * (steps + 1 + groups)
    layer_out, dx, feed_sums, proj_sums, qkv_sums, small = body(
        lengths, o, x, cot.reshape(x.shape), q, k, v, lse, rows, span, lines,
        flat(ln1_gain), flat(ln1_bias), qkv_weight, proj_weight, flat(proj_bias), flat(ln2_gain), flat(ln2_bias),
        fc_weight, flat(fc_bias), out_weight, flat(out_bias),
    )
    *grads, input_grad = finish(feed_sums, proj_sums, qkv_sums, small, dx)
    return (layer_out, input_grad, *grads)


def layer_norm(values, gain, shift):
    center = values - jnp.mean(values, axis=-1, keepdims=True)
    spread = jnp.mean(center * center, axis=-1, keepdims=True)
    return center * lax.rsqrt(spread + norm_eps) * gain + shift


def gelu_tanh(values):
    return jax.nn.gelu(values, approximate=True)


def left_dot(left, right):
    return lax.dot_general(
        left, right, (((0,), (0,)), ((), ())), preferred_element_type=jnp.float32
    )


def right_dot(left, right):
    return lax.dot_general(
        left, right, (((1,), (1,)), ((), ())), preferred_element_type=jnp.float32
    )


def allowed_mask(query_pos, query_seg, key_pos, key_seg):
    return (key_pos[None, None, :] <= query_pos[None, :, None]) & (
        key_seg[:, None, :] == query_seg[:, :, None]
    )


def local(
    tokens_in,
    lengths,
    ln1_gain,
    ln1_bias,
    qkv_weight,
    qv_bias,
    proj_weight,
    proj_bias,
    ln2_gain,
    ln2_bias,
    fc_weight,
    fc_bias,
    out_weight,
    out_bias,
    cotangent,
):
    row_count, span_len, model_width = tokens_in.shape
    head_count = model_width // HEAD
    scale = HEAD ** (-0.5)
    seq_parts = lax.axis_size("seq")
    row_len = span_len * seq_parts
    first_pos = lax.axis_index("seq") * span_len
    doc_count = lengths.shape[1]
    positions = jnp.arange(row_len, dtype=jnp.int32)
    ends = jnp.cumsum(lengths, axis=1)
    segments = jnp.sum((positions[None, :, None] >= ends[:, None, :]).astype(jnp.int32), axis=2)
    my_segs = lax.dynamic_slice_in_dim(segments, first_pos, span_len, 1)
    my_pos = first_pos + jnp.arange(span_len, dtype=jnp.int32)
    token_count = row_count * span_len
    keep_flat = (my_segs < doc_count).astype(jnp.float32).reshape(token_count, 1)
    inputs = tokens_in.astype(jnp.float32).reshape(token_count, model_width)
    normed = layer_norm(inputs, ln1_gain, ln1_bias)
    normed_low = normed.astype(jnp.bfloat16)
    bias_full = jnp.concatenate(
        [qv_bias[:model_width], jnp.zeros((model_width,), jnp.float32), qv_bias[model_width:]]
    )
    projected = (
        jnp.dot(normed_low, qkv_weight, preferred_element_type=jnp.float32) + bias_full
    ).astype(jnp.bfloat16)
    projected = projected.reshape(row_count, span_len, 3 * model_width)
    queries = projected[..., :model_width]
    keys = projected[..., model_width : 2 * model_width]
    values = projected[..., 2 * model_width :]
    query_heads = queries.reshape(row_count, span_len, head_count, HEAD)
    key_heads = keys.reshape(row_count, span_len, head_count, HEAD)
    value_heads = values.reshape(row_count, span_len, head_count, HEAD)
    last_pos = first_pos + span_len - 1
    start_state = (
        jnp.full((row_count, head_count, span_len), masked_value, jnp.float32),
        jnp.zeros((row_count, head_count, span_len), jnp.float32),
        jnp.zeros((row_count, span_len, model_width), jnp.float32),
    )
    key_piece = lax.all_gather(keys, "seq", axis=1, tiled=True)
    value_piece = lax.all_gather(values, "seq", axis=1, tiled=True)
    count = key_piece.shape[1]

    def forward_update(state):
        top, total, accum = state
        piece_keys = key_piece.reshape(row_count, count, head_count, HEAD)
        piece_values = value_piece.reshape(row_count, count, head_count, HEAD)
        scores = (
            jnp.einsum(
                "rqhd,rkhd->rhqk", query_heads, piece_keys, preferred_element_type=jnp.float32
            )
            * scale
        )
        key_pos = jnp.arange(count, dtype=jnp.int32)
        allowed = allowed_mask(my_pos, my_segs, key_pos, segments)[:, None]
        scores = jnp.where(allowed, scores, masked_value)
        new_top = jnp.maximum(top, jnp.max(scores, axis=-1))
        weights = jnp.where(allowed, jnp.exp(scores - new_top[..., None]), 0.0)
        total = jnp.sum(weights, axis=-1)
        added = jnp.einsum(
            "rhqk,rkhd->rqhd",
            weights.astype(jnp.bfloat16),
            piece_values,
            preferred_element_type=jnp.float32,
        )
        accum = added.reshape(row_count, span_len, model_width)
        return (new_top, total, accum)

    top, total, accum = lax.cond(
        jnp.int32(0) > last_pos, lambda state: state, forward_update, start_state
    )
    log_total = top + jnp.log(total)
    attended_heads = (
        accum.reshape(row_count, span_len, head_count, HEAD) / total.transpose(0, 2, 1)[..., None]
    )
    attended = attended_heads.reshape(token_count, model_width)
    attended_low = attended.astype(jnp.bfloat16)
    attn_out = jnp.dot(attended_low, proj_weight, preferred_element_type=jnp.float32) + proj_bias
    middle = inputs + branch_scale * attn_out
    normed_two = layer_norm(middle, ln2_gain, ln2_bias)
    normed_two_low = normed_two.astype(jnp.bfloat16)
    hidden_pre = jnp.dot(normed_two_low, fc_weight, preferred_element_type=jnp.float32) + fc_bias
    hidden_low = gelu_tanh(hidden_pre).astype(jnp.bfloat16)
    branch_out = jnp.dot(hidden_low, out_weight, preferred_element_type=jnp.float32) + out_bias
    layer_out = (
        ((middle + branch_scale * branch_out) * keep_flat)
        .astype(jnp.bfloat16)
        .reshape(row_count, span_len, model_width)
    )
    grad_final = keep_flat * cotangent.astype(jnp.float32).reshape(token_count, model_width)
    grad_branch = (branch_scale * grad_final).astype(jnp.bfloat16)
    grad_out_weight = left_dot(hidden_low, grad_branch)
    grad_out_bias = jnp.sum(grad_branch.astype(jnp.float32), axis=0)
    grad_hidden = right_dot(grad_branch, out_weight)
    gelu_value, gelu_pull = jax.vjp(gelu_tanh, hidden_pre)
    grad_pre = gelu_pull(grad_hidden)[0].astype(jnp.bfloat16)
    grad_fc_weight = left_dot(normed_two_low, grad_pre)
    grad_fc_bias = jnp.sum(grad_pre.astype(jnp.float32), axis=0)
    grad_normed_two = right_dot(grad_pre, fc_weight)
    norm_value, norm_pull = jax.vjp(layer_norm, middle, ln2_gain, ln2_bias)
    grad_mid_norm, grad_ln2_gain, grad_ln2_bias = norm_pull(grad_normed_two)
    grad_middle = grad_final + grad_mid_norm
    grad_attn = (branch_scale * grad_middle).astype(jnp.bfloat16)
    grad_proj_weight = left_dot(attended_low, grad_attn)
    grad_proj_bias = jnp.sum(grad_attn.astype(jnp.float32), axis=0)
    grad_attended = (
        right_dot(grad_attn, proj_weight)
        .astype(jnp.bfloat16)
        .reshape(row_count, span_len, model_width)
    )
    grad_att_heads = grad_attended.reshape(row_count, span_len, head_count, HEAD)
    delta = jnp.sum(grad_att_heads.astype(jnp.float32) * attended_heads, axis=-1)
    delta_t = delta.transpose(0, 2, 1)
    zero_grad = jnp.zeros((row_count, span_len, model_width), jnp.float32)
    query_key_piece = lax.all_gather(keys, "seq", axis=1, tiled=True)
    query_value_piece = lax.all_gather(values, "seq", axis=1, tiled=True)
    query_count = query_key_piece.shape[1]

    def query_update(carry):
        piece_keys = query_key_piece.reshape(row_count, query_count, head_count, HEAD)
        piece_values = query_value_piece.reshape(row_count, query_count, head_count, HEAD)
        scores = (
            jnp.einsum(
                "rqhd,rkhd->rhqk", query_heads, piece_keys, preferred_element_type=jnp.float32
            )
            * scale
        )
        key_pos = jnp.arange(query_count, dtype=jnp.int32)
        allowed = allowed_mask(my_pos, my_segs, key_pos, segments)[:, None]
        probs = jnp.where(allowed, jnp.exp(scores - log_total[..., None]), 0.0)
        grad_probs = jnp.einsum(
            "rqhd,rkhd->rhqk", grad_att_heads, piece_values, preferred_element_type=jnp.float32
        )
        grad_scores = (probs * (grad_probs - delta_t[..., None])).astype(jnp.bfloat16)
        added = jnp.einsum(
            "rhqk,rkhd->rqhd", grad_scores, piece_keys, preferred_element_type=jnp.float32
        )
        return scale * added.reshape(row_count, span_len, model_width)

    grad_queries = lax.cond(jnp.int32(0) > last_pos, lambda carry: carry, query_update, zero_grad)
    stats_lse, stats_delta = (
        lax.all_gather(
            log_total.transpose(0, 2, 1).astype(jnp.bfloat16), "seq", axis=1, tiled=True
        ).astype(jnp.float32),
        lax.all_gather(delta.astype(jnp.bfloat16), "seq", axis=1, tiled=True).astype(delta.dtype),
    )
    query_piece_in = lax.all_gather(queries, "seq", axis=1, tiled=True)
    grad_piece_in = lax.all_gather(grad_attended, "seq", axis=1, tiled=True)
    key_count = query_piece_in.shape[1]

    def key_update(state):
        piece_queries = query_piece_in.reshape(row_count, key_count, head_count, HEAD)
        piece_grads = grad_piece_in.reshape(row_count, key_count, head_count, HEAD)
        scores = (
            jnp.einsum(
                "rqhd,rkhd->rhqk", piece_queries, key_heads, preferred_element_type=jnp.float32
            )
            * scale
        )
        query_pos = jnp.arange(key_count, dtype=jnp.int32)
        allowed = allowed_mask(query_pos, segments, my_pos, my_segs)[:, None]
        piece_lse = stats_lse.transpose(0, 2, 1)
        piece_delta = stats_delta.transpose(0, 2, 1)
        probs = jnp.where(allowed, jnp.exp(scores - piece_lse[..., None]), 0.0)
        add_v = jnp.einsum(
            "rhqk,rqhd->rkhd",
            probs.astype(jnp.bfloat16),
            piece_grads,
            preferred_element_type=jnp.float32,
        )
        grad_probs = jnp.einsum(
            "rqhd,rkhd->rhqk", piece_grads, value_heads, preferred_element_type=jnp.float32
        )
        grad_scores = (probs * (grad_probs - piece_delta[..., None])).astype(jnp.bfloat16)
        add_k = jnp.einsum(
            "rhqk,rqhd->rkhd", grad_scores, piece_queries, preferred_element_type=jnp.float32
        )
        return (
            scale * add_k.reshape(row_count, span_len, model_width),
            add_v.reshape(row_count, span_len, model_width),
        )

    grad_keys, grad_values = lax.cond(
        jnp.int32(0) + key_count <= first_pos,
        lambda state: state,
        key_update,
        (zero_grad, zero_grad),
    )
    grad_projected = (
        jnp.concatenate([grad_queries, grad_keys, grad_values], axis=-1)
        .astype(jnp.bfloat16)
        .reshape(token_count, 3 * model_width)
    )
    grad_qkv_weight = left_dot(normed_low, grad_projected)
    column_sums = jnp.sum(grad_projected.astype(jnp.float32), axis=0)
    grad_qv_bias = jnp.concatenate([column_sums[:model_width], column_sums[2 * model_width :]])
    grad_normed = right_dot(grad_projected, qkv_weight)
    first_value, first_pull = jax.vjp(layer_norm, inputs, ln1_gain, ln1_bias)
    grad_in_norm, grad_ln1_gain, grad_ln1_bias = first_pull(grad_normed)
    input_grad = (grad_middle + grad_in_norm).reshape(row_count, span_len, model_width)
    local_grads = (
        grad_ln1_gain,
        grad_ln1_bias,
        grad_qkv_weight,
        grad_qv_bias,
        grad_proj_weight,
        grad_proj_bias,
        grad_ln2_gain,
        grad_ln2_bias,
        grad_fc_weight,
        grad_fc_bias,
        grad_out_weight,
        grad_out_bias,
    )
    shares = (
        lax.psum_scatter(
            local_grads[0].astype(jnp.bfloat16), "row", scatter_dimension=0, tiled=True
        ).astype(jnp.float32),
        lax.psum_scatter(
            local_grads[1].astype(jnp.bfloat16), "row", scatter_dimension=0, tiled=True
        ).astype(jnp.float32),
        lax.psum_scatter(
            local_grads[2].astype(jnp.bfloat16), "row", scatter_dimension=0, tiled=True
        ).astype(jnp.float32),
        lax.psum_scatter(
            local_grads[3].astype(jnp.bfloat16), "row", scatter_dimension=0, tiled=True
        ).astype(jnp.float32),
        lax.psum_scatter(
            local_grads[4].astype(jnp.bfloat16), "row", scatter_dimension=0, tiled=True
        ).astype(jnp.float32),
        lax.psum_scatter(
            local_grads[5].astype(jnp.bfloat16), "row", scatter_dimension=0, tiled=True
        ).astype(jnp.float32),
        lax.psum_scatter(
            local_grads[6].astype(jnp.bfloat16), "row", scatter_dimension=0, tiled=True
        ).astype(jnp.float32),
        lax.psum_scatter(
            local_grads[7].astype(jnp.bfloat16), "row", scatter_dimension=0, tiled=True
        ).astype(jnp.float32),
        lax.psum_scatter(
            local_grads[8].astype(jnp.bfloat16), "row", scatter_dimension=0, tiled=True
        ).astype(jnp.float32),
        lax.psum_scatter(
            local_grads[9].astype(jnp.bfloat16), "row", scatter_dimension=0, tiled=True
        ).astype(jnp.float32),
        lax.psum_scatter(
            local_grads[10].astype(jnp.bfloat16), "row", scatter_dimension=0, tiled=True
        ).astype(jnp.float32),
        lax.psum_scatter(
            local_grads[11].astype(jnp.bfloat16), "row", scatter_dimension=0, tiled=True
        ).astype(jnp.float32),
    )
    totals = (
        lax.psum(shares[0].astype(jnp.bfloat16), "seq").astype(jnp.float32),
        lax.psum(shares[1].astype(jnp.bfloat16), "seq").astype(jnp.float32),
        lax.psum(shares[2].astype(jnp.bfloat16), "seq").astype(jnp.float32),
        lax.psum(shares[3].astype(jnp.bfloat16), "seq").astype(jnp.float32),
        lax.psum(shares[4].astype(jnp.bfloat16), "seq").astype(jnp.float32),
        lax.psum(shares[5].astype(jnp.bfloat16), "seq").astype(jnp.float32),
        lax.psum(shares[6].astype(jnp.bfloat16), "seq").astype(jnp.float32),
        lax.psum(shares[7].astype(jnp.bfloat16), "seq").astype(jnp.float32),
        lax.psum(shares[8].astype(jnp.bfloat16), "seq").astype(jnp.float32),
        lax.psum(shares[9].astype(jnp.bfloat16), "seq").astype(jnp.float32),
        lax.psum(shares[10].astype(jnp.bfloat16), "seq").astype(jnp.float32),
        lax.psum(shares[11].astype(jnp.bfloat16), "seq").astype(jnp.float32),
    )
    summed = (
        lax.all_gather(totals[0].astype(jnp.bfloat16), "row", axis=0, tiled=True).astype(
            jnp.float32
        ),
        lax.all_gather(totals[1].astype(jnp.bfloat16), "row", axis=0, tiled=True).astype(
            jnp.float32
        ),
        lax.all_gather(totals[2].astype(jnp.bfloat16), "row", axis=0, tiled=True).astype(
            jnp.float32
        ),
        lax.all_gather(totals[3].astype(jnp.bfloat16), "row", axis=0, tiled=True).astype(
            jnp.float32
        ),
        lax.all_gather(totals[4].astype(jnp.bfloat16), "row", axis=0, tiled=True).astype(
            jnp.float32
        ),
        lax.all_gather(totals[5].astype(jnp.bfloat16), "row", axis=0, tiled=True).astype(
            jnp.float32
        ),
        lax.all_gather(totals[6].astype(jnp.bfloat16), "row", axis=0, tiled=True).astype(
            jnp.float32
        ),
        lax.all_gather(totals[7].astype(jnp.bfloat16), "row", axis=0, tiled=True).astype(
            jnp.float32
        ),
        lax.all_gather(totals[8].astype(jnp.bfloat16), "row", axis=0, tiled=True).astype(
            jnp.float32
        ),
        lax.all_gather(totals[9].astype(jnp.bfloat16), "row", axis=0, tiled=True).astype(
            jnp.float32
        ),
        lax.all_gather(totals[10].astype(jnp.bfloat16), "row", axis=0, tiled=True).astype(
            jnp.float32
        ),
        lax.all_gather(totals[11].astype(jnp.bfloat16), "row", axis=0, tiled=True).astype(
            jnp.float32
        ),
    )
    return (
        layer_out,
        input_grad,
        summed[0],
        summed[1],
        summed[2],
        summed[3],
        summed[4],
        summed[5],
        summed[6],
        summed[7],
        summed[8],
        summed[9],
        summed[10],
        summed[11],
    )


def solution(mesh):
    in_specs = (
        P("row", "seq", None),
        P("row", None),
        P(),
        P(),
        P(),
        P(),
        P(),
        P(),
        P(),
        P(),
        P(),
        P(),
        P(),
        P(),
        P("row", "seq", None),
    )
    out_specs = (
        P("row", "seq", None),
        P("row", "seq", None),
        P(),
        P(),
        P(),
        P(),
        P(),
        P(),
        P(),
        P(),
        P(),
        P(),
        P(),
        P(),
    )
    own_rows = mesh.shape["row"] == 8 and mesh.shape["seq"] == 4
    return jax.shard_map(by_rows if own_rows else local, mesh=mesh, in_specs=in_specs, out_specs=out_specs, check_vma=False)
```

```python
import functools

import jax
import jax.numpy as jnp
from jax import lax
from jax.experimental import pallas as pl
from jax.experimental.pallas import tpu as pltpu
from jax.sharding import PartitionSpec as P

HEAD = 64
branch_scale = 12.0 ** (-0.5)
masked_value = -1e30
norm_eps = 1e-05
F32, BF16 = jnp.float32, jnp.bfloat16
VMEM_LIMIT = 60 * 1024 * 1024


MESH = pl.DeviceIdType.MESH


class Place:
    def __init__(self):
        row, seq = lax.axis_index("row"), lax.axis_index("seq")
        self.row, self.seq = row, seq
        self.core, self.z = lax.rem(row, 2), lax.div(row, 2)
        self.x, self.y = lax.rem(seq, 2), lax.div(seq, 2)
        self.sibling = (row + 1 - 2 * self.core, seq)
        self.across_x = (row, seq + 1 - 2 * self.x)
        self.across_y = (row, seq + 2 - 4 * self.y)
        step_x, step_y = 1 - 2 * self.x, 2 - 4 * self.y
        self.first_bit = self.x + self.core * (self.y - self.x)
        self.second_bit = self.y + self.core * (self.x - self.y)
        self.first = (row, seq + step_x + self.core * (step_y - step_x))
        self.second = (row, seq + step_y + self.core * (step_x - step_y))

        own = seq + self.core * (3 - 2 * seq)
        self.active = own < 3
        self.my_row = jnp.minimum(own, 2)

    def in_plane(self, hop):
        across_x, across_y = hop % 2, hop // 2
        x = self.x + across_x * (1 - 2 * self.x)
        y = self.y + across_y * (1 - 2 * self.y)
        seq = 2 * y + x
        return (self.row, seq), seq + self.core * (3 - 2 * seq)

    def greet_plane(self):
        barrier = pltpu.get_barrier_semaphore()
        for hop in (1, 2, 3):
            pl.semaphore_signal(barrier, inc=1, device_id=self.in_plane(hop)[0], device_id_type=MESH)
        pl.semaphore_wait(barrier, 3)

    def along_z(self, hop):
        return (2 * lax.rem(self.z + hop, 4) + self.core, self.seq)

    def greet(self):
        barrier = pltpu.get_barrier_semaphore()
        others = [self.sibling, self.across_x, self.across_y] + [self.along_z(hop) for hop in (1, 2, 3)]
        for other in others:
            pl.semaphore_signal(barrier, inc=1, device_id=other, device_id_type=MESH)
        pl.semaphore_wait(barrier, len(others))


def send(source, target, send_sem, recv_sem, device):
    return pltpu.make_async_remote_copy(
        src_ref=source, dst_ref=target, send_sem=send_sem, recv_sem=recv_sem,
        device_id=device, device_id_type=MESH,
    )


class SmallReducer:
    def __init__(self, place, sums, recv, line, send_sem, recv_sem):
        self.place, self.sums, self.recv, self.line = place, sums, recv, line
        self.send_sem, self.recv_sem = send_sem, recv_sem

    def copies(self, phase):
        place = self.place
        if phase < 3:
            other = (place.sibling, place.across_x, place.across_y)[phase]
            return [send(self.sums.at[phase], self.recv.at[phase], self.send_sem.at[phase], self.recv_sem.at[phase], other)]
        return [
            send(self.sums.at[3], self.line.at[place.z], self.send_sem.at[2 + hop], self.recv_sem.at[2 + hop], place.along_z(hop))
            for hop in (1, 2, 3)
        ]

    def step(self, phase):
        if phase > 0:
            for copy in self.copies(phase - 1):
                copy.wait()
        if 0 < phase < 4:
            self.sums[phase] = self.sums[phase - 1] + self.recv[phase - 1]
        if phase < 4:
            for copy in self.copies(phase):
                copy.start()
        if phase == 3:
            self.line[self.place.z] = self.sums[3]

    def total(self):
        return (self.line[0] + self.line[1]) + (self.line[2] + self.line[3])


def dot_nn(left, right):
    return lax.dot_general(left, right, (((1,), (0,)), ((), ())), preferred_element_type=F32)


def dot_nt(left, right):
    return lax.dot_general(left, right, (((1,), (1,)), ((), ())), preferred_element_type=F32)


def dot_tn(left, right):
    return lax.dot_general(left, right, (((0,), (0,)), ((), ())), preferred_element_type=F32)


def row_mean(values):
    return jnp.mean(values, axis=-1, keepdims=True)


def normalise(values):
    center = values - row_mean(values)
    inverse = lax.rsqrt(row_mean(center * center) + norm_eps)
    return center * inverse, inverse


def fill_bias(lens_ref, row, bias_ref, block):
    tokens = bias_ref.shape[0]
    ends, total = [], jnp.int32(0)
    for j in range(lens_ref.shape[1]):
        total = total + lens_ref[row, j]
        ends.append(total)
    query_pos = lax.broadcasted_iota(jnp.int32, (1, tokens), 1)
    query_seg = jnp.zeros((1, tokens), jnp.int32)
    for end in ends:
        query_seg = query_seg + (query_pos >= end).astype(jnp.int32)

    def one(i, carry):
        start = pl.multiple_of(i * block, block)
        key_pos = start + lax.broadcasted_iota(jnp.int32, (block, 1), 0)
        key_seg = jnp.zeros((block, 1), jnp.int32)
        for end in ends:
            key_seg = key_seg + (key_pos >= end).astype(jnp.int32)
        allowed = (key_pos <= query_pos) & (key_seg == query_seg)
        bias_ref[pl.ds(start, block), :] = jnp.where(allowed, 0.0, masked_value)
        return carry

    lax.fori_loop(0, tokens // block, one, 0)


def keep_column(lens_ref, row, start, block):
    total = jnp.int32(0)
    for j in range(lens_ref.shape[1]):
        total = total + lens_ref[row, j]
    pos = start + lax.broadcasted_iota(jnp.int32, (block, 1), 0)
    return (pos < total).astype(F32)


def head_row(h, value):
    lane = lax.broadcasted_iota(jnp.int32, (1, 2 * HEAD), 1)
    low = h % 2 * HEAD
    return jnp.where((lane >= low) & (lane < low + HEAD), value, 0.0).astype(BF16)


def front_kernel(
    lens_ref, tokens_ref, cot_in_ref, gain_ref, shift_ref, qv_bias_ref, wq_ref, wk_ref, wv_ref,
    q_ref, k_ref, v_ref, o_ref, lse_ref, x_ref, cot_ref,
    arrived, normed, bias, value_t, out_t, vectors, send_sem, recv_sem, copy_sem,
):
    tokens, width = x_ref.shape
    lanes = wq_ref.shape[1]
    block = tokens_ref.shape[1]
    blocks = tokens // block
    place = Place()
    mine = pl.ds(place.seq, 1)
    sources, targets = (tokens_ref, cot_in_ref), (arrived, cot_ref)

    def outgoing(which, hop):
        other, row = place.in_plane(hop)
        return row, send(
            sources[which].at[jnp.minimum(row, 2)], targets[which].at[place.seq],
            send_sem.at[which, hop - 1], recv_sem.at[which, hop - 1], other,
        )

    def local(which):
        return pltpu.make_async_copy(
            sources[which].at[place.my_row], targets[which].at[place.seq], copy_sem.at[which]
        )

    def start(which):
        for hop in (1, 2, 3):
            row, copy = outgoing(which, hop)
            pl.when(row < 3)(copy.start)
        pl.when(place.active)(local(which).start)

    def finish(which):
        for hop in (1, 2, 3):
            row, copy = outgoing(which, hop)
            pl.when(row < 3)(copy.wait_send)
            pl.when(place.active)(copy.wait_recv)
        pl.when(place.active)(local(which).wait)

    @pl.when(pl.program_id(0) == 0)
    def _():
        place.greet_plane()
        start(0)
        vectors[0:1, :] = gain_ref[...].reshape(1, width)
        vectors[1:2, :] = shift_ref[...].reshape(1, width)
        for i in range(2):
            vectors[2 + i : 3 + i, :] = qv_bias_ref[i * width : (i + 1) * width].reshape(1, width)
        fill_bias(lens_ref, place.my_row, bias, block)

        @pl.when(jnp.logical_not(place.active))
        def _():
            arrived[...] = jnp.zeros_like(arrived)

        finish(0)
        start(1)

        def one(i, carry):
            rows = pl.ds(pl.multiple_of(i * block, block), block)
            x = arrived[i]
            x_ref[rows, :] = x
            unit, _ = normalise(x.astype(F32))
            normed[rows, :] = (unit * vectors[0:1, :] + vectors[1:2, :]).astype(BF16)
            return carry

        lax.fori_loop(0, blocks, one, 0)

    group = pl.ds(pl.multiple_of(pl.program_id(0) * lanes, lanes), lanes)

    def project(i, carry):
        rows = pl.ds(pl.multiple_of(i * block, block), block)
        h1 = normed[rows, :]
        q_ref[rows, :] = (dot_nn(h1, wq_ref[...]) + vectors[2:3, group]).astype(BF16)
        k_ref[rows, :] = dot_nn(h1, wk_ref[...]).astype(BF16)
        values = dot_nn(h1, wv_ref[...]) + vectors[3:4, group]
        v_ref[rows, :] = values.astype(BF16)
        value_t[:, rows] = values.T.astype(BF16)
        return carry

    lax.fori_loop(0, blocks, project, 0)

    heads = lanes // HEAD
    turns = [(i, h) for i in range(blocks) for h in range(heads)]

    def score(i, h):
        rows, count = slice(i * block, (i + 1) * block), (i + 1) * block
        pair = slice(h // 2 * 2 * HEAD, (h // 2 + 1) * 2 * HEAD)
        queries = q_ref[rows, pair] * head_row(h, HEAD ** (-0.5))
        return dot_nt(k_ref[:count, pair], queries) + bias[:count, rows]

    def mix(i, h, probs, total):
        rows, count = slice(i * block, (i + 1) * block), (i + 1) * block
        own = slice(h * HEAD, (h + 1) * HEAD)
        out_t[own, :] = dot_nn(value_t[own, :count], probs) * (1.0 / total)
        if h == heads - 1:
            o_ref[rows, :] = out_t[...].T.astype(BF16)

    following, waiting = score(*turns[0]), None
    for turn, (i, h) in enumerate(turns):
        scores = following
        if turn + 1 < len(turns):
            following = score(*turns[turn + 1])
        if waiting is not None:
            mix(*waiting)
        top = jnp.max(scores, axis=0, keepdims=True)
        probs = jnp.exp(scores - top)
        total = jnp.sum(probs, axis=0, keepdims=True)
        lse_ref[0, h : h + 1, i * block : (i + 1) * block] = top + jnp.log(total)
        waiting = (i, h, probs.astype(BF16), total)
    mix(*waiting)

    @pl.when(pl.program_id(0) == pl.num_programs(0) - 1)
    def _():
        finish(1)

        @pl.when(jnp.logical_not(place.active))
        def _():
            copy = pltpu.make_async_copy(arrived, cot_ref, copy_sem.at[1])
            copy.start()
            copy.wait()


def front(lens, tokens_in, cotangent, gain, shift, qkv_weight, qv_bias):
    rows, span, width = tokens_in.shape
    spans = lax.axis_size("seq")
    tokens = spans * span
    lanes = width // 3
    groups = width // lanes
    heads = max(8, lanes // HEAD)
    whole = lambda shape: pl.BlockSpec(shape, lambda g: (0,) * len(shape))
    columns = lambda shape, first: pl.BlockSpec(shape, lambda g: (0, first + g))
    act = jax.ShapeDtypeStruct((tokens, width), BF16)
    sem = lambda *shape: pltpu.SemaphoreType.DMA(shape)
    return pl.pallas_call(
        front_kernel,
        grid=(groups,),
        out_shape=(
            act, act, act, act, jax.ShapeDtypeStruct((groups, heads, tokens), F32), act,
            jax.ShapeDtypeStruct((spans, span, width), BF16),
        ),
        in_specs=[
            pl.BlockSpec(memory_space=pltpu.SMEM),
            pl.BlockSpec(memory_space=pl.ANY),
            pl.BlockSpec(memory_space=pl.ANY),
            whole((width,)),
            whole((width,)),
            whole((2 * width,)),
            columns((width, lanes), 0),
            columns((width, lanes), groups),
            columns((width, lanes), 2 * groups),
        ],
        out_specs=[columns((tokens, lanes), 0)] * 4
        + [
            pl.BlockSpec((1, heads, tokens), lambda g: (g, 0, 0)),
            whole((tokens, width)),
            pl.BlockSpec(memory_space=pl.ANY),
        ],
        scratch_shapes=[
            pltpu.VMEM((spans, span, width), BF16),
            pltpu.VMEM((tokens, width), BF16),
            pltpu.VMEM((tokens, tokens), F32),
            pltpu.VMEM((lanes, tokens), BF16),
            pltpu.VMEM((lanes, span), F32),
            pltpu.VMEM((8, width), F32),
            sem(2, 3), sem(2, 3), sem(2),
        ],
        compiler_params=pltpu.CompilerParams(
            collective_id=1, has_side_effects=True, vmem_limit_bytes=VMEM_LIMIT
        ),
        name="front",
    )(lens, tokens_in, cotangent, gain, shift, qv_bias, qkv_weight, qkv_weight, qkv_weight)


class Units:
    slots = (0, 1, 2, 3, 6, 9, 10, 11)

    def __init__(self, place, fresh, out, recv0, recv1, recv2, recv3, part, send_sem, recv_sem, copy_sem):
        self.place, self.fresh, self.out, self.part = place, fresh, out, part
        self.recv = (recv0, recv1, recv2, recv3)
        self.send_sem, self.recv_sem, self.copy_sem = send_sem, recv_sem, copy_sem
        _, rows, columns = fresh.shape
        self.size = (rows // 2, rows // 4, rows // 8, rows // 16)
        self.wide = columns // 2
        bits = (place.core, place.first_bit, place.second_bit)
        self.own = [bit * size for bit, size in zip(bits, self.size)]
        self.away = [(1 - bit) * size for bit, size in zip(bits, self.size)]

    @staticmethod
    def scratch(count, n, rows, columns):
        vmem = lambda *shape: pltpu.VMEM(shape, BF16)
        sem = lambda *shape: pltpu.SemaphoreType.DMA(shape)
        return [
            vmem(count, n, rows // 2, columns), vmem(count, n, rows // 4, columns), vmem(count, n, rows // 8, columns),
            vmem(count, 3, n, rows // 16, columns // 2), vmem(count, n, rows // 16, columns // 2),
            sem(count, 12), sem(count, 12), sem(count),
        ]

    def rows(self, start, count):
        return pl.ds(pl.multiple_of(start, self.size[3]), count)

    def piece(self, start, z):
        columns = pl.ds(pl.multiple_of(lax.rem(z, 2) * self.wide, self.wide), self.wide)
        return self.rows(start + lax.div(z, 2) * self.size[3], self.size[3]), columns

    def copies(self, phase, u):
        place, out, size, own = self.place, self.out, self.size, self.own
        first = self.slots[phase]
        sems = lambda i: (self.send_sem.at[u, first + i], self.recv_sem.at[u, first + i])
        hops = (1, 2, 3)
        if phase == 0:
            return [send(self.fresh.at[:, self.rows(self.away[0], size[0])], self.recv[0].at[u], *sems(0), place.sibling)]
        if phase < 3:
            source = self.recv[phase - 1].at[u, :, self.rows(self.away[phase], size[phase])]
            return [send(source, self.recv[phase].at[u], *sems(0), (place.first, place.second)[phase - 1])]
        if phase == 3:
            return [
                send(
                    self.recv[2].at[u, :, *self.piece(0, lax.rem(place.z + hop, 4))], self.recv[3].at[u, hop - 1],
                    *sems(hop - 1), place.along_z(hop),
                )
                for hop in hops
            ]
        if phase == 4:
            where = out.at[u, :, *self.piece(own[0] + own[1] + own[2], place.z)]
            return [send(self.part.at[u], where, *sems(hop - 1), place.along_z(hop)) for hop in hops]
        start, count, other = {
            5: (own[0] + own[1] + own[2], size[2], place.second),
            6: (own[0] + own[1], size[1], place.first),
            7: (own[0], size[0], place.sibling),
        }[phase]
        where = out.at[u, :, self.rows(start, count)]
        return [send(where, where, *sems(0), other)]

    def local(self, u):
        where = self.out.at[u, :, *self.piece(self.own[0] + self.own[1] + self.own[2], self.place.z)]
        return pltpu.make_async_copy(self.part.at[u], where, self.copy_sem.at[u])

    def add(self, phase, u):
        step = self.size[3]
        if phase == 3:
            rows, columns = self.piece(0, self.place.z)
            total = self.recv[2][u, :, rows, columns].astype(F32)
            for hop in range(3):
                total = total + self.recv[3][u, hop].astype(F32)
            self.part[u] = total.astype(BF16)
            return
        source = self.fresh if phase == 0 else self.recv[phase - 1].at[u]
        target = self.recv[phase].at[u]

        def one(i, carry):
            here = self.rows(i * step, step)
            there = self.rows(self.own[phase] + i * step, step)
            for panel in range(self.fresh.shape[0]):
                total = source[panel, there, :].astype(F32) + target[panel, here, :].astype(F32)
                target[panel, here, :] = total.astype(BF16)
            return carry

        lax.fori_loop(0, self.size[phase] // step, one, 0)

    def step(self, phase, u):
        if phase > 0:
            for copy in self.copies(phase - 1, u):
                copy.wait()
            if phase == 5:
                self.local(u).wait()
        if 0 < phase < 5:
            self.add(phase - 1, u)
        if phase < 8:
            for copy in self.copies(phase, u):
                copy.start()
        if phase == 4:
            self.local(u).start()


class Exchange:
    def __init__(self, place, source, target, send_sem, recv_sem, copy_sem):
        self.place, self.source, self.target = place, source, target
        self.send_sem, self.recv_sem, self.copy_sem = send_sem, recv_sem, copy_sem
        self.span = target.shape[1]

    def block(self, seq):
        return self.source.at[pl.ds(pl.multiple_of(seq * self.span, self.span), self.span)]

    def outgoing(self, hop):
        other, row = self.place.in_plane(hop)
        return row, send(
            self.block(other[1]), self.target.at[self.place.my_row],
            self.send_sem.at[hop - 1], self.recv_sem.at[hop - 1], other,
        )

    def local(self):
        return pltpu.make_async_copy(self.block(self.place.seq), self.target.at[self.place.my_row], self.copy_sem)

    def start(self):
        for hop in (3, 1, 2):
            pl.when(self.place.active)(self.outgoing(hop)[1].start)
        pl.when(self.place.active)(self.local().start)

    def finish(self):
        for hop in (1, 2, 3):
            row, copy = self.outgoing(hop)
            pl.when(self.place.active)(copy.wait_send)
            pl.when(row < 3)(copy.wait_recv)
        pl.when(self.place.active)(self.local().wait)


def plan(hooks, sizes, made):
    free = {"core": 0.0, "plane": 0.0, "line": 0.0}
    delay = {"core": 1.5, "plane": 3.5, "line": 3.0}
    now, flight, plans = 0.0, {}, {}

    def go(unit, phase):
        nonlocal now
        now += 0.3
        if phase == 8:
            flight[unit] = (8, 1e9)
            return
        kind = ("core", "plane", "plane", "line")[min(phase, 7 - phase)]
        time = sizes[unit] * (0.5 / 0.6, 0.25 / 0.094, 0.125 / 0.094, 0.25 / 0.094)[min(phase, 7 - phase)]
        begin = max(now, free[kind])
        free[kind] = begin + time
        flight[unit] = (phase, begin + time + delay[kind])

    for name, compute in hooks:
        now += compute
        plans[name] = []
        for unit in sorted(flight, key=lambda u: flight[u][1]):
            phase, end = flight[unit]
            if end <= now + 0.5:
                plans[name].append((unit, phase + 1))
                go(unit, phase + 1)
        for unit, hook in made.items():
            if hook == name:
                plans[name].append((unit, 0))
                go(unit, 0)
        if name in ("lo", "dx"):
            free["plane"] = max(now, free["plane"]) + 16.0
    return plans, {unit: phase + 1 for unit, (phase, _) in flight.items()}, now


def timetable(steps, groups):
    hooks = []
    for s in range(steps):
        hooks += [(("early", s), 14.0 if s == 0 else 3.0), (("late", s), 3.0), (("fed", s), 2.6)]
    hooks += [("lo", 7.0), ("proj", 1.5), ("turn", 3.0)]
    for s in range(steps, steps + groups):
        hooks += [(("low", s), 5.0), (("high", s), 3.5), (("made", s), 2.5)]
    hooks.append(("dx", 3.0))
    made = {s: ("fed", s) for s in range(steps)}
    made[steps] = "proj"
    made.update({steps + 1 + g: ("made", steps + g) for g in range(groups)})
    return hooks, made


def body_kernel(
    steps, groups,
    lens_ref, o_ref, x_ref, cot_ref, wp_ref, bp_ref, gain2_ref, shift2_ref, wf_ref, bf_ref, wo_ref, bo_ref,
    gain1_ref, shift1_ref, q_ref, k_ref, v_ref, lse_ref, wq_ref, wk_ref, wv_ref,
    lo_out, dx_out, feed_out, rest_out, small_out,
    middle, normed, normed_t, cot_low, out_acc, back_acc, hidden, back_low, bias, key_t, grad_q_t, delta, vectors,
    fresh_feed, fresh_rest, sums, small_recv, line_sums,
    small_send, small_recv_sem, out_send, out_recv, out_copy, *unit_scratch,
):
    tokens, width = x_ref.shape
    lanes = wq_ref.shape[1]
    span = lo_out.shape[1]
    blocks = tokens // span
    step = pl.program_id(0)
    place = Place()
    acc = sums.at[0]

    fed = Units(place, fresh_feed, feed_out, *unit_scratch[:8])
    rest = Units(place, fresh_rest, rest_out, *unit_scratch[8:])
    small = SmallReducer(place, sums, small_recv, line_sums, small_send, small_recv_sem)
    lo_back = Exchange(place, normed, lo_out, out_send.at[0], out_recv.at[0], out_copy.at[0])
    dx_back = Exchange(place, cot_low, dx_out, out_send.at[1], out_recv.at[1], out_copy.at[1])

    hooks, made = timetable(steps, groups)
    panel = width * width * 2e-6
    count = steps + 1 + groups
    plans, left, _ = plan(hooks, [2 * panel] * steps + [panel] * (1 + groups), made)
    order = [name for name, _ in hooks]
    freed = {u: order.index(name) for name, actions in plans.items() for u, phase in actions if phase == 1}
    for u in [*range(steps - 1), *range(steps, steps + groups)]:
        assert freed[u] < order.index(made[u + 1])

    def chosen(pairs, index):
        value, found = jnp.int32(0), jnp.int32(0)
        for key, item in pairs:
            hit = (index == key).astype(jnp.int32)
            value, found = value + hit * item, found + hit
        return value, found > 0

    def hook(name):
        if name in plans:
            for u, phase in plans[name]:
                units, index = (fed, u) if u < steps else (rest, u - steps)
                units.step(phase, index)
            return
        seen, bodies = {}, {}
        for s in range(steps + groups):
            for place_in_list, (u, phase) in enumerate(plans.get((name, s), [])):
                kind = (u < steps, phase)
                turn = seen[kind, s] = seen.get((kind, s), -1) + 1
                bodies.setdefault((*kind, turn), []).append((s, u if u < steps else u - steps))
        for (is_fed, phase, _), pairs in sorted(bodies.items(), key=lambda item: -item[0][1]):
            index, found = chosen(pairs, step)
            pl.when(found)(functools.partial((fed if is_fed else rest).step, phase, index))

    def each(body, first=0, last=blocks):
        def run(i, carry):
            start = pl.multiple_of(i * span, span)
            body(start, pl.ds(start, span))
            return carry

        lax.fori_loop(first, last, run, 0)

    def column_sum(values):
        return jnp.sum(values, axis=0, keepdims=True)

    @pl.when(step == 0)
    def _():
        place.greet()
        acc[...] = jnp.zeros_like(acc)
        for i, ref in enumerate((bp_ref, gain2_ref, shift2_ref, bo_ref, gain1_ref, shift1_ref)):
            vectors[i : i + 1, :] = ref[...].reshape(1, width)
        for f in range(steps):
            vectors[8 + f : 9 + f, :] = bf_ref[f * width : (f + 1) * width].reshape(1, width)

        def begin(start, rows):
            attn = dot_nn(o_ref[rows, :], wp_ref[...]) + vectors[0:1, :]
            mid = x_ref[rows, :].astype(F32) + branch_scale * attn
            middle[rows, :] = mid
            unit, _ = normalise(mid)
            h2 = unit * vectors[1:2, :] + vectors[2:3, :]
            normed[rows, :] = h2.astype(BF16)
            normed_t[:, rows] = h2.T.astype(BF16)
            keep = keep_column(lens_ref, place.my_row, start, span)
            low = (branch_scale * (keep * cot_ref[rows, :].astype(F32))).astype(BF16)
            cot_low[rows, :] = low
            acc[4:5, :] += column_sum(low.astype(F32))
            out_acc[rows, :] = jnp.zeros((span, width), F32)
            back_acc[rows, :] = jnp.zeros((span, width), F32)

        each(begin)

    @pl.when(step < steps)
    def _():
        def chunk(start, rows):
            pre = dot_nn(normed[rows, :], wf_ref[...]) + vectors[pl.ds(8 + step, 1), :]
            back = dot_nt(cot_low[rows, :], wo_ref[...])
            square = pre * pre
            root = (2.0 / jnp.pi) ** 0.5
            bend = jnp.tanh(pre * (root + (root * 0.044715) * square))
            half = 0.5 * pre
            hid = (half + half * bend).astype(BF16)
            slope = (0.5 + 0.5 * bend) + half * (1.0 - bend * bend) * (root + (3.0 * root * 0.044715) * square)
            grad = (back * slope).astype(BF16)
            hidden[rows, :] = hid
            back_low[rows, :] = grad
            acc[pl.ds(8 + step, 1), :] += column_sum(grad.astype(F32))
            out_acc[rows, :] += dot_nn(hid, wo_ref[...])
            back_acc[rows, :] += dot_nt(grad, wf_ref[...])

        each(chunk, 0, blocks // 2)
        hook("early")
        each(chunk, blocks // 2, blocks)
        hook("late")
        fresh_feed[0] = dot_tn(hidden[...], cot_low[...]).astype(BF16)
        fresh_feed[1] = dot_nn(normed_t[...], back_low[...]).astype(BF16)
        hook("fed")

    @pl.when(step == steps - 1)
    def _():
        def end(start, rows):
            keep = keep_column(lens_ref, place.my_row, start, span)
            mid = middle[rows, :]
            normed[rows, :] = (
                keep * (mid + branch_scale * (out_acc[rows, :] + vectors[3:4, :]))
            ).astype(BF16)
            unit, inverse = normalise(mid)
            back = back_acc[rows, :]
            back_acc[rows, :] = jnp.zeros((span, width), F32)
            acc[5:6, :] += column_sum(back * unit)
            acc[6:7, :] += column_sum(back)
            scaled = back * vectors[1:2, :]
            grad = keep * cot_ref[rows, :].astype(F32) + inverse * (
                scaled - row_mean(scaled) - unit * row_mean(scaled * unit)
            )
            middle[rows, :] = grad
            low = (branch_scale * grad).astype(BF16)
            hidden[rows, :] = low
            acc[7:8, :] += column_sum(low.astype(F32))
            back_low[rows, :] = dot_nt(low, wp_ref[...]).astype(BF16)

        each(end)
        hook("lo")
        lo_back.start()
        fresh_rest[0] = dot_tn(o_ref[...], hidden[...]).astype(BF16)
        hook("proj")

    @pl.when(step == steps)
    def _():
        fill_bias(lens_ref, place.my_row, bias, span)

        def turn(start, rows):
            unit, _ = normalise(x_ref[rows, :].astype(F32))
            normed_t[:, rows] = (unit * vectors[4:5, :] + vectors[5:6, :]).T.astype(BF16)

        each(turn)
        hook("turn")

    @pl.when(step >= steps)
    def _():
        group = pl.ds(pl.multiple_of((step - steps) * lanes, lanes), lanes)
        grad_k, grad_v = out_acc.at[:, :lanes], out_acc.at[:, lanes : 2 * lanes]
        grad_q, d_out = hidden.at[:, :lanes], hidden.at[:, lanes : 2 * lanes]
        grad_k[...] = jnp.zeros_like(grad_k)
        grad_v[...] = jnp.zeros_like(grad_v)
        grad_q_t[...] = jnp.zeros_like(grad_q_t)
        key_t[...] = k_ref[...].astype(F32).T.astype(BF16)
        head_id = lax.broadcasted_iota(jnp.int32, (8, lanes), 0)
        lane_id = lax.broadcasted_iota(jnp.int32, (8, lanes), 1)
        member = ((lane_id >= head_id * HEAD) & (lane_id < (head_id + 1) * HEAD)).astype(F32)

        def prepare(start, rows):
            grads = back_low[rows, group]
            d_out[rows, :] = grads
            product = grads.astype(F32) * o_ref[rows, group].astype(F32)
            delta[:, rows] = lax.dot_general(
                member, product, (((1,), (1,)), ((), ())),
                precision=lax.Precision.HIGHEST, preferred_element_type=F32,
            )

        each(prepare)
        heads = lanes // HEAD

        def tile(t, carry):
            i = sum((t >= b * (b + 1) // 2).astype(jnp.int32) for b in range(1, blocks))
            first = pl.multiple_of(i * span, span)
            key_first = pl.multiple_of((t - lax.div(i * (i + 1), 2)) * span, span)
            rows, keys = pl.ds(first, span), pl.ds(key_first, span)
            mask = bias[keys, rows]

            def start(h):
                pair = slice(h // 2 * 2 * HEAD, (h // 2 + 1) * 2 * HEAD)
                queries = q_ref[rows, pair] * head_row(h, HEAD ** (-0.5))
                grads = d_out[rows, pair] * head_row(h, 1.0)
                return queries, grads, dot_nt(k_ref[keys, pair], queries) + mask, dot_nt(v_ref[keys, pair], grads)

            following = start(0)
            for h in range(heads):
                pair = slice(h // 2 * 2 * HEAD, (h // 2 + 1) * 2 * HEAD)
                own = slice(h * HEAD, (h + 1) * HEAD)
                queries, grads, scores, grad_probs = following
                if h + 1 < heads:
                    following = start(h + 1)
                probs = jnp.exp(scores - lse_ref[0, h : h + 1, rows])
                grad_scores = (probs * (grad_probs - delta[h : h + 1, rows])).astype(BF16)
                grad_v[keys, pair] += dot_nn(probs.astype(BF16), grads)
                grad_k[keys, pair] += dot_nn(grad_scores, queries)
                grad_q_t[own, rows] += dot_nn(key_t[own, keys], grad_scores)
            return carry

        tiles = blocks * (blocks + 1) // 2
        lax.fori_loop(0, tiles - blocks, tile, 0)
        hook("low")
        lax.fori_loop(tiles - blocks, tiles, tile, 0)
        hook("high")

        def close(start, rows):
            dq = (grad_q_t[:, rows].T * HEAD ** (-0.5)).astype(BF16)
            grad_q[rows, :] = dq
            dk = grad_k[rows, :].astype(BF16)
            dv = grad_v[rows, :].astype(BF16)
            acc[2:3, group] += column_sum(dq.astype(F32))
            acc[3:4, group] += column_sum(dv.astype(F32))
            back_acc[rows, :] += dot_nt(dq, wq_ref[...]) + dot_nt(dk, wk_ref[...]) + dot_nt(dv, wv_ref[...])

        each(close)
        for p, grad in enumerate((grad_q, grad_k, grad_v)):
            fresh_rest[0, :, p * lanes : (p + 1) * lanes] = dot_nn(normed_t[...], grad[...].astype(BF16)).astype(BF16)
        hook("made")

    @pl.when(step == steps + groups - 1)
    def _():
        def last(start, rows):
            unit, inverse = normalise(x_ref[rows, :].astype(F32))
            back = back_acc[rows, :]
            acc[0:1, :] += column_sum(back * unit)
            acc[1:2, :] += column_sum(back)
            scaled = back * vectors[4:5, :]
            grad = middle[rows, :] + inverse * (
                scaled - row_mean(scaled) - unit * row_mean(scaled * unit)
            )
            cot_low[rows, :] = grad.astype(BF16)

        each(last)
        dx_back.start()
        hook("dx")
        small.step(0)

        def round_of(turn, carry):
            for units, first, number in ((fed, 0, steps), (rest, steps, 1 + groups)):
                def unit(u, carry):
                    phase, _ = chosen([(w, left[first + w]) for w in range(number)], u)
                    for p in range(1, 9):
                        pl.when(phase + turn == p)(functools.partial(units.step, p, u))
                    return carry

                lax.fori_loop(0, number, unit, 0)
            for p in range(1, 5):
                pl.when(turn == p - 1)(functools.partial(small.step, p))
            return carry

        lax.fori_loop(0, max(4, 9 - min(left.values())), round_of, 0)
        small_out[...] = small.total()
        lo_back.finish()
        dx_back.finish()


def body(
    lens, o, x, cot, q, k, v, lse, rows, span,
    ln1_gain, ln1_bias, qkv_weight, proj_weight, proj_bias, ln2_gain, ln2_bias, fc_weight, fc_bias, out_weight, out_bias,
):
    tokens, width = x.shape
    groups, heads, _ = lse.shape
    lanes = width // groups
    steps = fc_weight.shape[1] // width
    shape = jax.ShapeDtypeStruct
    once = pl.Buffered(1)
    whole = lambda *dims: pl.BlockSpec(dims, lambda s: (0,) * len(dims), pipeline_mode=once)
    act, vec, mat = whole(tokens, width), whole(width), whole(width, width)
    feed_step = lambda s: jnp.minimum(s, steps - 1)
    back_step = lambda s: jnp.maximum(s - steps, 0)
    columns = lambda dims, first: pl.BlockSpec(dims, lambda s: (0, first + back_step(s)))
    anywhere = pl.BlockSpec(memory_space=pl.ANY)
    f32 = lambda *dims: pltpu.VMEM(dims, F32)
    bf16 = lambda *dims: pltpu.VMEM(dims, BF16)
    sem = lambda *dims: pltpu.SemaphoreType.DMA(dims)
    return pl.pallas_call(
        functools.partial(body_kernel, steps, groups),
        grid=(steps + groups,),
        out_shape=(
            shape((rows, span, width), BF16),
            shape((rows, span, width), BF16),
            shape((steps, 2, width, width), BF16),
            shape((1 + groups, 1, width, width), BF16),
            shape((16, width), F32),
        ),
        in_specs=[
            pl.BlockSpec(memory_space=pltpu.SMEM),
            act, act, act, mat, vec, vec, vec,
            pl.BlockSpec((width, width), lambda s: (0, feed_step(s))),
            whole(steps * width),
            pl.BlockSpec((width, width), lambda s: (feed_step(s), 0)),
            vec, vec, vec,
            columns((tokens, lanes), 0), columns((tokens, lanes), 0), columns((tokens, lanes), 0),
            pl.BlockSpec((1, heads, tokens), lambda s: (back_step(s), 0, 0)),
            columns((width, lanes), 0), columns((width, lanes), groups), columns((width, lanes), 2 * groups),
        ],
        out_specs=[anywhere] * 4 + [pl.BlockSpec((16, width), lambda s: (0, 0))],
        scratch_shapes=[
            f32(tokens, width), bf16(tokens, width), bf16(width, tokens), bf16(tokens, width),
            f32(tokens, width), f32(tokens, width), bf16(tokens, width), bf16(tokens, width),
            f32(tokens, tokens), bf16(lanes, tokens), f32(lanes, tokens), f32(8, tokens), f32(16, width),
            bf16(2, width, width), bf16(1, width, width), f32(4, 16, width), f32(3, 16, width), f32(4, 16, width),
            sem(6), sem(6), sem(2, 3), sem(2, 3), sem(2),
            *Units.scratch(steps, 2, width, width), *Units.scratch(1 + groups, 1, width, width),
        ],
        compiler_params=pltpu.CompilerParams(
            collective_id=0, has_side_effects=True, vmem_limit_bytes=VMEM_LIMIT
        ),
        name="body",
    )(
        lens, o, x, cot, proj_weight, proj_bias, ln2_gain, ln2_bias, fc_weight, fc_bias, out_weight, out_bias,
        ln1_gain, ln1_bias, q, k, v, lse, qkv_weight, qkv_weight, qkv_weight,
    )


def finish_kernel(
    feed_ref, proj_ref, qkv_ref, small_ref, dx_ref,
    ln1_gain, ln1_bias, qkv_weight, qv_bias, proj_weight, proj_bias,
    ln2_gain, ln2_bias, fc_weight, fc_bias, out_weight, out_bias, input_grad,
):
    width = small_ref.shape[1]
    lanes = qkv_ref.shape[3]
    groups = width // lanes
    out_weight[...] = feed_ref[0, 0].astype(F32)
    fc_weight[...] = feed_ref[0, 1].astype(F32)
    for g in range(groups):
        qkv_weight[:, g * lanes : (g + 1) * lanes] = qkv_ref[1 + g, 0].astype(F32)
    proj_weight[...] = proj_ref[0, 0].astype(F32)
    input_grad[...] = dx_ref[...].astype(F32)

    @pl.when((pl.program_id(0) == 0) & (pl.program_id(1) == 0))
    def _():
        for ref, first in (
            (ln1_gain, 0), (ln1_bias, 1), (qv_bias, 2), (out_bias, 4),
            (ln2_gain, 5), (ln2_bias, 6), (proj_bias, 7), (fc_bias, 8),
        ):
            for i in range(ref.shape[0] // width):
                ref[i * width : (i + 1) * width] = small_ref[first + i]


def finish(feed_sums, rest_sums, small, dx):
    steps, _, width, _ = feed_sums.shape
    groups = rest_sums.shape[0] - 1
    lanes = width // groups
    rows, span, _ = dx.shape
    half = width // 2
    shape = lambda *dims: jax.ShapeDtypeStruct(dims, F32)
    flat = lambda n: pl.BlockSpec((n * width,), lambda f, r: (0,))
    third = lambda f: jnp.minimum(f, 2)
    row = pl.BlockSpec((1, span // 2, width), lambda f, r: (jnp.minimum(f, rows - 1), jnp.where(f > rows - 1, 1, r), 0))
    return pl.pallas_call(
        finish_kernel,
        grid=(steps, 2),
        out_shape=(
            shape(width), shape(width), shape(width, 3 * width), shape(2 * width),
            shape(width, width), shape(width), shape(width), shape(width),
            shape(width, steps * width), shape(steps * width), shape(steps * width, width), shape(width),
            shape(rows, span, width),
        ),
        in_specs=[
            pl.BlockSpec((1, 2, half, width), lambda f, r: (f, 0, r, 0)),
            pl.BlockSpec((1, 1, half, width), lambda f, r: (0, 0, jnp.where(f == steps - 1, r, 0), 0)),
            pl.BlockSpec((1 + groups, 1, half, lanes), lambda f, r: (0, 0, jnp.where(f > 2, 1, r), third(f))),
            pl.BlockSpec((16, width), lambda f, r: (0, 0)),
            row,
        ],
        out_specs=[
            flat(1), flat(1),
            pl.BlockSpec((half, width), lambda f, r: (jnp.where(f > 2, 1, r), third(f))),
            flat(2),
            pl.BlockSpec((half, width), lambda f, r: (jnp.where(f == steps - 1, r, 0), 0)),
            flat(1), flat(1), flat(1),
            pl.BlockSpec((half, width), lambda f, r: (r, f)),
            flat(steps),
            pl.BlockSpec((half, width), lambda f, r: (2 * f + r, 0)),
            flat(1),
            row,
        ],
        compiler_params=pltpu.CompilerParams(vmem_limit_bytes=VMEM_LIMIT),
        name="finish",
    )(feed_sums, rest_sums, rest_sums, small, dx)


def by_rows(
    tokens_in, lengths, ln1_gain, ln1_bias, qkv_weight, qv_bias, proj_weight, proj_bias,
    ln2_gain, ln2_bias, fc_weight, fc_bias, out_weight, out_bias, cotangent,
):
    rows, span, width = tokens_in.shape
    q, k, v, o, lse, x, cot = front(
        lengths, tokens_in, cotangent, ln1_gain, ln1_bias, qkv_weight, qv_bias
    )
    layer_out, dx, feed_sums, rest_sums, small = body(
        lengths, o, x, cot.reshape(x.shape), q, k, v, lse, rows, span,
        ln1_gain, ln1_bias, qkv_weight, proj_weight, proj_bias, ln2_gain, ln2_bias,
        fc_weight, fc_bias, out_weight, out_bias,
    )
    *grads, input_grad = finish(feed_sums, rest_sums, small, dx)
    return (layer_out, input_grad, *grads)


def layer_norm(values, gain, shift):
    center = values - jnp.mean(values, axis=-1, keepdims=True)
    spread = jnp.mean(center * center, axis=-1, keepdims=True)
    return center * lax.rsqrt(spread + norm_eps) * gain + shift


def gelu_tanh(values):
    return jax.nn.gelu(values, approximate=True)


def left_dot(left, right):
    return lax.dot_general(
        left, right, (((0,), (0,)), ((), ())), preferred_element_type=jnp.float32
    )


def right_dot(left, right):
    return lax.dot_general(
        left, right, (((1,), (1,)), ((), ())), preferred_element_type=jnp.float32
    )


def allowed_mask(query_pos, query_seg, key_pos, key_seg):
    return (key_pos[None, None, :] <= query_pos[None, :, None]) & (
        key_seg[:, None, :] == query_seg[:, :, None]
    )


def local(
    tokens_in,
    lengths,
    ln1_gain,
    ln1_bias,
    qkv_weight,
    qv_bias,
    proj_weight,
    proj_bias,
    ln2_gain,
    ln2_bias,
    fc_weight,
    fc_bias,
    out_weight,
    out_bias,
    cotangent,
):
    row_count, span_len, model_width = tokens_in.shape
    head_count = model_width // HEAD
    scale = HEAD ** (-0.5)
    seq_parts = lax.axis_size("seq")
    row_len = span_len * seq_parts
    first_pos = lax.axis_index("seq") * span_len
    doc_count = lengths.shape[1]
    positions = jnp.arange(row_len, dtype=jnp.int32)
    ends = jnp.cumsum(lengths, axis=1)
    segments = jnp.sum((positions[None, :, None] >= ends[:, None, :]).astype(jnp.int32), axis=2)
    my_segs = lax.dynamic_slice_in_dim(segments, first_pos, span_len, 1)
    my_pos = first_pos + jnp.arange(span_len, dtype=jnp.int32)
    token_count = row_count * span_len
    keep_flat = (my_segs < doc_count).astype(jnp.float32).reshape(token_count, 1)
    inputs = tokens_in.astype(jnp.float32).reshape(token_count, model_width)
    normed = layer_norm(inputs, ln1_gain, ln1_bias)
    normed_low = normed.astype(jnp.bfloat16)
    bias_full = jnp.concatenate(
        [qv_bias[:model_width], jnp.zeros((model_width,), jnp.float32), qv_bias[model_width:]]
    )
    projected = (
        jnp.dot(normed_low, qkv_weight, preferred_element_type=jnp.float32) + bias_full
    ).astype(jnp.bfloat16)
    projected = projected.reshape(row_count, span_len, 3 * model_width)
    queries = projected[..., :model_width]
    keys = projected[..., model_width : 2 * model_width]
    values = projected[..., 2 * model_width :]
    query_heads = queries.reshape(row_count, span_len, head_count, HEAD)
    key_heads = keys.reshape(row_count, span_len, head_count, HEAD)
    value_heads = values.reshape(row_count, span_len, head_count, HEAD)
    last_pos = first_pos + span_len - 1
    start_state = (
        jnp.full((row_count, head_count, span_len), masked_value, jnp.float32),
        jnp.zeros((row_count, head_count, span_len), jnp.float32),
        jnp.zeros((row_count, span_len, model_width), jnp.float32),
    )
    key_piece = lax.all_gather(keys, "seq", axis=1, tiled=True)
    value_piece = lax.all_gather(values, "seq", axis=1, tiled=True)
    count = key_piece.shape[1]

    def forward_update(state):
        top, total, accum = state
        piece_keys = key_piece.reshape(row_count, count, head_count, HEAD)
        piece_values = value_piece.reshape(row_count, count, head_count, HEAD)
        scores = (
            jnp.einsum(
                "rqhd,rkhd->rhqk", query_heads, piece_keys, preferred_element_type=jnp.float32
            )
            * scale
        )
        key_pos = jnp.arange(count, dtype=jnp.int32)
        allowed = allowed_mask(my_pos, my_segs, key_pos, segments)[:, None]
        scores = jnp.where(allowed, scores, masked_value)
        new_top = jnp.maximum(top, jnp.max(scores, axis=-1))
        weights = jnp.where(allowed, jnp.exp(scores - new_top[..., None]), 0.0)
        total = jnp.sum(weights, axis=-1)
        added = jnp.einsum(
            "rhqk,rkhd->rqhd",
            weights.astype(jnp.bfloat16),
            piece_values,
            preferred_element_type=jnp.float32,
        )
        accum = added.reshape(row_count, span_len, model_width)
        return (new_top, total, accum)

    top, total, accum = lax.cond(
        jnp.int32(0) > last_pos, lambda state: state, forward_update, start_state
    )
    log_total = top + jnp.log(total)
    attended_heads = (
        accum.reshape(row_count, span_len, head_count, HEAD) / total.transpose(0, 2, 1)[..., None]
    )
    attended = attended_heads.reshape(token_count, model_width)
    attended_low = attended.astype(jnp.bfloat16)
    attn_out = jnp.dot(attended_low, proj_weight, preferred_element_type=jnp.float32) + proj_bias
    middle = inputs + branch_scale * attn_out
    normed_two = layer_norm(middle, ln2_gain, ln2_bias)
    normed_two_low = normed_two.astype(jnp.bfloat16)
    hidden_pre = jnp.dot(normed_two_low, fc_weight, preferred_element_type=jnp.float32) + fc_bias
    hidden_low = gelu_tanh(hidden_pre).astype(jnp.bfloat16)
    branch_out = jnp.dot(hidden_low, out_weight, preferred_element_type=jnp.float32) + out_bias
    layer_out = (
        ((middle + branch_scale * branch_out) * keep_flat)
        .astype(jnp.bfloat16)
        .reshape(row_count, span_len, model_width)
    )
    grad_final = keep_flat * cotangent.astype(jnp.float32).reshape(token_count, model_width)
    grad_branch = (branch_scale * grad_final).astype(jnp.bfloat16)
    grad_out_weight = left_dot(hidden_low, grad_branch)
    grad_out_bias = jnp.sum(grad_branch.astype(jnp.float32), axis=0)
    grad_hidden = right_dot(grad_branch, out_weight)
    gelu_value, gelu_pull = jax.vjp(gelu_tanh, hidden_pre)
    grad_pre = gelu_pull(grad_hidden)[0].astype(jnp.bfloat16)
    grad_fc_weight = left_dot(normed_two_low, grad_pre)
    grad_fc_bias = jnp.sum(grad_pre.astype(jnp.float32), axis=0)
    grad_normed_two = right_dot(grad_pre, fc_weight)
    norm_value, norm_pull = jax.vjp(layer_norm, middle, ln2_gain, ln2_bias)
    grad_mid_norm, grad_ln2_gain, grad_ln2_bias = norm_pull(grad_normed_two)
    grad_middle = grad_final + grad_mid_norm
    grad_attn = (branch_scale * grad_middle).astype(jnp.bfloat16)
    grad_proj_weight = left_dot(attended_low, grad_attn)
    grad_proj_bias = jnp.sum(grad_attn.astype(jnp.float32), axis=0)
    grad_attended = (
        right_dot(grad_attn, proj_weight)
        .astype(jnp.bfloat16)
        .reshape(row_count, span_len, model_width)
    )
    grad_att_heads = grad_attended.reshape(row_count, span_len, head_count, HEAD)
    delta = jnp.sum(grad_att_heads.astype(jnp.float32) * attended_heads, axis=-1)
    delta_t = delta.transpose(0, 2, 1)
    zero_grad = jnp.zeros((row_count, span_len, model_width), jnp.float32)
    query_key_piece = lax.all_gather(keys, "seq", axis=1, tiled=True)
    query_value_piece = lax.all_gather(values, "seq", axis=1, tiled=True)
    query_count = query_key_piece.shape[1]

    def query_update(carry):
        piece_keys = query_key_piece.reshape(row_count, query_count, head_count, HEAD)
        piece_values = query_value_piece.reshape(row_count, query_count, head_count, HEAD)
        scores = (
            jnp.einsum(
                "rqhd,rkhd->rhqk", query_heads, piece_keys, preferred_element_type=jnp.float32
            )
            * scale
        )
        key_pos = jnp.arange(query_count, dtype=jnp.int32)
        allowed = allowed_mask(my_pos, my_segs, key_pos, segments)[:, None]
        probs = jnp.where(allowed, jnp.exp(scores - log_total[..., None]), 0.0)
        grad_probs = jnp.einsum(
            "rqhd,rkhd->rhqk", grad_att_heads, piece_values, preferred_element_type=jnp.float32
        )
        grad_scores = (probs * (grad_probs - delta_t[..., None])).astype(jnp.bfloat16)
        added = jnp.einsum(
            "rhqk,rkhd->rqhd", grad_scores, piece_keys, preferred_element_type=jnp.float32
        )
        return scale * added.reshape(row_count, span_len, model_width)

    grad_queries = lax.cond(jnp.int32(0) > last_pos, lambda carry: carry, query_update, zero_grad)
    stats_lse, stats_delta = (
        lax.all_gather(
            log_total.transpose(0, 2, 1).astype(jnp.bfloat16), "seq", axis=1, tiled=True
        ).astype(jnp.float32),
        lax.all_gather(delta.astype(jnp.bfloat16), "seq", axis=1, tiled=True).astype(delta.dtype),
    )
    query_piece_in = lax.all_gather(queries, "seq", axis=1, tiled=True)
    grad_piece_in = lax.all_gather(grad_attended, "seq", axis=1, tiled=True)
    key_count = query_piece_in.shape[1]

    def key_update(state):
        piece_queries = query_piece_in.reshape(row_count, key_count, head_count, HEAD)
        piece_grads = grad_piece_in.reshape(row_count, key_count, head_count, HEAD)
        scores = (
            jnp.einsum(
                "rqhd,rkhd->rhqk", piece_queries, key_heads, preferred_element_type=jnp.float32
            )
            * scale
        )
        query_pos = jnp.arange(key_count, dtype=jnp.int32)
        allowed = allowed_mask(query_pos, segments, my_pos, my_segs)[:, None]
        piece_lse = stats_lse.transpose(0, 2, 1)
        piece_delta = stats_delta.transpose(0, 2, 1)
        probs = jnp.where(allowed, jnp.exp(scores - piece_lse[..., None]), 0.0)
        add_v = jnp.einsum(
            "rhqk,rqhd->rkhd",
            probs.astype(jnp.bfloat16),
            piece_grads,
            preferred_element_type=jnp.float32,
        )
        grad_probs = jnp.einsum(
            "rqhd,rkhd->rhqk", piece_grads, value_heads, preferred_element_type=jnp.float32
        )
        grad_scores = (probs * (grad_probs - piece_delta[..., None])).astype(jnp.bfloat16)
        add_k = jnp.einsum(
            "rhqk,rqhd->rkhd", grad_scores, piece_queries, preferred_element_type=jnp.float32
        )
        return (
            scale * add_k.reshape(row_count, span_len, model_width),
            add_v.reshape(row_count, span_len, model_width),
        )

    grad_keys, grad_values = lax.cond(
        jnp.int32(0) + key_count <= first_pos,
        lambda state: state,
        key_update,
        (zero_grad, zero_grad),
    )
    grad_projected = (
        jnp.concatenate([grad_queries, grad_keys, grad_values], axis=-1)
        .astype(jnp.bfloat16)
        .reshape(token_count, 3 * model_width)
    )
    grad_qkv_weight = left_dot(normed_low, grad_projected)
    column_sums = jnp.sum(grad_projected.astype(jnp.float32), axis=0)
    grad_qv_bias = jnp.concatenate([column_sums[:model_width], column_sums[2 * model_width :]])
    grad_normed = right_dot(grad_projected, qkv_weight)
    first_value, first_pull = jax.vjp(layer_norm, inputs, ln1_gain, ln1_bias)
    grad_in_norm, grad_ln1_gain, grad_ln1_bias = first_pull(grad_normed)
    input_grad = (grad_middle + grad_in_norm).reshape(row_count, span_len, model_width)
    local_grads = (
        grad_ln1_gain,
        grad_ln1_bias,
        grad_qkv_weight,
        grad_qv_bias,
        grad_proj_weight,
        grad_proj_bias,
        grad_ln2_gain,
        grad_ln2_bias,
        grad_fc_weight,
        grad_fc_bias,
        grad_out_weight,
        grad_out_bias,
    )
    shares = (
        lax.psum_scatter(
            local_grads[0].astype(jnp.bfloat16), "row", scatter_dimension=0, tiled=True
        ).astype(jnp.float32),
        lax.psum_scatter(
            local_grads[1].astype(jnp.bfloat16), "row", scatter_dimension=0, tiled=True
        ).astype(jnp.float32),
        lax.psum_scatter(
            local_grads[2].astype(jnp.bfloat16), "row", scatter_dimension=0, tiled=True
        ).astype(jnp.float32),
        lax.psum_scatter(
            local_grads[3].astype(jnp.bfloat16), "row", scatter_dimension=0, tiled=True
        ).astype(jnp.float32),
        lax.psum_scatter(
            local_grads[4].astype(jnp.bfloat16), "row", scatter_dimension=0, tiled=True
        ).astype(jnp.float32),
        lax.psum_scatter(
            local_grads[5].astype(jnp.bfloat16), "row", scatter_dimension=0, tiled=True
        ).astype(jnp.float32),
        lax.psum_scatter(
            local_grads[6].astype(jnp.bfloat16), "row", scatter_dimension=0, tiled=True
        ).astype(jnp.float32),
        lax.psum_scatter(
            local_grads[7].astype(jnp.bfloat16), "row", scatter_dimension=0, tiled=True
        ).astype(jnp.float32),
        lax.psum_scatter(
            local_grads[8].astype(jnp.bfloat16), "row", scatter_dimension=0, tiled=True
        ).astype(jnp.float32),
        lax.psum_scatter(
            local_grads[9].astype(jnp.bfloat16), "row", scatter_dimension=0, tiled=True
        ).astype(jnp.float32),
        lax.psum_scatter(
            local_grads[10].astype(jnp.bfloat16), "row", scatter_dimension=0, tiled=True
        ).astype(jnp.float32),
        lax.psum_scatter(
            local_grads[11].astype(jnp.bfloat16), "row", scatter_dimension=0, tiled=True
        ).astype(jnp.float32),
    )
    totals = (
        lax.psum(shares[0].astype(jnp.bfloat16), "seq").astype(jnp.float32),
        lax.psum(shares[1].astype(jnp.bfloat16), "seq").astype(jnp.float32),
        lax.psum(shares[2].astype(jnp.bfloat16), "seq").astype(jnp.float32),
        lax.psum(shares[3].astype(jnp.bfloat16), "seq").astype(jnp.float32),
        lax.psum(shares[4].astype(jnp.bfloat16), "seq").astype(jnp.float32),
        lax.psum(shares[5].astype(jnp.bfloat16), "seq").astype(jnp.float32),
        lax.psum(shares[6].astype(jnp.bfloat16), "seq").astype(jnp.float32),
        lax.psum(shares[7].astype(jnp.bfloat16), "seq").astype(jnp.float32),
        lax.psum(shares[8].astype(jnp.bfloat16), "seq").astype(jnp.float32),
        lax.psum(shares[9].astype(jnp.bfloat16), "seq").astype(jnp.float32),
        lax.psum(shares[10].astype(jnp.bfloat16), "seq").astype(jnp.float32),
        lax.psum(shares[11].astype(jnp.bfloat16), "seq").astype(jnp.float32),
    )
    summed = (
        lax.all_gather(totals[0].astype(jnp.bfloat16), "row", axis=0, tiled=True).astype(
            jnp.float32
        ),
        lax.all_gather(totals[1].astype(jnp.bfloat16), "row", axis=0, tiled=True).astype(
            jnp.float32
        ),
        lax.all_gather(totals[2].astype(jnp.bfloat16), "row", axis=0, tiled=True).astype(
            jnp.float32
        ),
        lax.all_gather(totals[3].astype(jnp.bfloat16), "row", axis=0, tiled=True).astype(
            jnp.float32
        ),
        lax.all_gather(totals[4].astype(jnp.bfloat16), "row", axis=0, tiled=True).astype(
            jnp.float32
        ),
        lax.all_gather(totals[5].astype(jnp.bfloat16), "row", axis=0, tiled=True).astype(
            jnp.float32
        ),
        lax.all_gather(totals[6].astype(jnp.bfloat16), "row", axis=0, tiled=True).astype(
            jnp.float32
        ),
        lax.all_gather(totals[7].astype(jnp.bfloat16), "row", axis=0, tiled=True).astype(
            jnp.float32
        ),
        lax.all_gather(totals[8].astype(jnp.bfloat16), "row", axis=0, tiled=True).astype(
            jnp.float32
        ),
        lax.all_gather(totals[9].astype(jnp.bfloat16), "row", axis=0, tiled=True).astype(
            jnp.float32
        ),
        lax.all_gather(totals[10].astype(jnp.bfloat16), "row", axis=0, tiled=True).astype(
            jnp.float32
        ),
        lax.all_gather(totals[11].astype(jnp.bfloat16), "row", axis=0, tiled=True).astype(
            jnp.float32
        ),
    )
    return (
        layer_out,
        input_grad,
        summed[0],
        summed[1],
        summed[2],
        summed[3],
        summed[4],
        summed[5],
        summed[6],
        summed[7],
        summed[8],
        summed[9],
        summed[10],
        summed[11],
    )


def solution(mesh):
    in_specs = (
        P("row", "seq", None),
        P("row", None),
        P(),
        P(),
        P(),
        P(),
        P(),
        P(),
        P(),
        P(),
        P(),
        P(),
        P(),
        P(),
        P("row", "seq", None),
    )
    out_specs = (
        P("row", "seq", None),
        P("row", "seq", None),
        P(),
        P(),
        P(),
        P(),
        P(),
        P(),
        P(),
        P(),
        P(),
        P(),
        P(),
        P(),
    )
    own_rows = mesh.shape["row"] == 8 and mesh.shape["seq"] == 4
    return jax.shard_map(by_rows if own_rows else local, mesh=mesh, in_specs=in_specs, out_specs=out_specs, check_vma=False)
```

```python
import functools

import jax
import jax.numpy as jnp
from jax import lax
from jax.experimental import pallas as pl
from jax.experimental.pallas import tpu as pltpu
from jax.sharding import PartitionSpec as P

HEAD = 64
branch_scale = 12.0 ** (-0.5)
masked_value = -1e30
norm_eps = 1e-05
F32, BF16 = jnp.float32, jnp.bfloat16
VMEM_LIMIT = 60 * 1024 * 1024


MESH = pl.DeviceIdType.MESH


class Place:
    def __init__(self):
        row, seq = lax.axis_index("row"), lax.axis_index("seq")
        self.row, self.seq = row, seq
        self.core, self.z = lax.rem(row, 2), lax.div(row, 2)
        self.x, self.y = lax.rem(seq, 2), lax.div(seq, 2)
        self.sibling = (row + 1 - 2 * self.core, seq)
        self.across_x = (row, seq + 1 - 2 * self.x)
        self.across_y = (row, seq + 2 - 4 * self.y)
        step_x, step_y = 1 - 2 * self.x, 2 - 4 * self.y
        self.first_bit = self.x + self.core * (self.y - self.x)
        self.second_bit = self.y + self.core * (self.x - self.y)
        self.first = (row, seq + step_x + self.core * (step_y - step_x))
        self.second = (row, seq + step_y + self.core * (step_x - step_y))

        self.next_z = (row + 2 - 4 * lax.rem(self.z, 2), seq)
        self.far_z = (row + 4 - 8 * lax.div(self.z, 2), seq)
        own = seq + self.core * (3 - 2 * seq)
        self.active = own < 3
        self.my_row = jnp.minimum(own, 2)

    def in_plane(self, hop):
        across_x, across_y = hop % 2, hop // 2
        x = self.x + across_x * (1 - 2 * self.x)
        y = self.y + across_y * (1 - 2 * self.y)
        seq = 2 * y + x
        return (self.row, seq), seq + self.core * (3 - 2 * seq)

    def greet_plane(self):
        barrier = pltpu.get_barrier_semaphore()
        for hop in (1, 2, 3):
            pl.semaphore_signal(barrier, inc=1, device_id=self.in_plane(hop)[0], device_id_type=MESH)
        pl.semaphore_wait(barrier, 3)

    def along_z(self, hop):
        return (2 * lax.rem(self.z + hop, 4) + self.core, self.seq)

    def greet(self):
        barrier = pltpu.get_barrier_semaphore()
        others = [self.sibling, self.across_x, self.across_y] + [self.along_z(hop) for hop in (1, 2, 3)]
        for other in others:
            pl.semaphore_signal(barrier, inc=1, device_id=other, device_id_type=MESH)
        pl.semaphore_wait(barrier, len(others))


def send(source, target, send_sem, recv_sem, device):
    return pltpu.make_async_remote_copy(
        src_ref=source, dst_ref=target, send_sem=send_sem, recv_sem=recv_sem,
        device_id=device, device_id_type=MESH,
    )


class SmallReducer:
    def __init__(self, place, sums, recv, line, send_sem, recv_sem):
        self.place, self.sums, self.recv, self.line = place, sums, recv, line
        self.send_sem, self.recv_sem = send_sem, recv_sem

    def copies(self, phase):
        place = self.place
        if phase < 3:
            other = (place.sibling, place.across_x, place.across_y)[phase]
            return [send(self.sums.at[phase], self.recv.at[phase], self.send_sem.at[phase], self.recv_sem.at[phase], other)]
        return [
            send(self.sums.at[3], self.line.at[place.z], self.send_sem.at[2 + hop], self.recv_sem.at[2 + hop], place.along_z(hop))
            for hop in (1, 2, 3)
        ]

    def step(self, phase):
        if phase > 0:
            for copy in self.copies(phase - 1):
                copy.wait()
        if 0 < phase < 4:
            self.sums[phase] = self.sums[phase - 1] + self.recv[phase - 1]
        if phase < 4:
            for copy in self.copies(phase):
                copy.start()
        if phase == 3:
            self.line[self.place.z] = self.sums[3]

    def total(self):
        return (self.line[0] + self.line[1]) + (self.line[2] + self.line[3])


def dot_nn(left, right):
    return lax.dot_general(left, right, (((1,), (0,)), ((), ())), preferred_element_type=F32)


def dot_nt(left, right):
    return lax.dot_general(left, right, (((1,), (1,)), ((), ())), preferred_element_type=F32)


def dot_tn(left, right):
    return lax.dot_general(left, right, (((0,), (0,)), ((), ())), preferred_element_type=F32)


def row_mean(values):
    return jnp.mean(values, axis=-1, keepdims=True)


def normalise(values):
    center = values - row_mean(values)
    inverse = lax.rsqrt(row_mean(center * center) + norm_eps)
    return center * inverse, inverse


def fill_bias(lens_ref, row, bias_ref, block):
    tokens = bias_ref.shape[0]
    ends, total = [], jnp.int32(0)
    for j in range(lens_ref.shape[1]):
        total = total + lens_ref[row, j]
        ends.append(total)
    query_pos = lax.broadcasted_iota(jnp.int32, (1, tokens), 1)
    query_seg = jnp.zeros((1, tokens), jnp.int32)
    for end in ends:
        query_seg = query_seg + (query_pos >= end).astype(jnp.int32)

    def one(i, carry):
        start = pl.multiple_of(i * block, block)
        key_pos = start + lax.broadcasted_iota(jnp.int32, (block, 1), 0)
        key_seg = jnp.zeros((block, 1), jnp.int32)
        for end in ends:
            key_seg = key_seg + (key_pos >= end).astype(jnp.int32)
        allowed = (key_pos <= query_pos) & (key_seg == query_seg)
        bias_ref[pl.ds(start, block), :] = jnp.where(allowed, 0.0, masked_value)
        return carry

    lax.fori_loop(0, tokens // block, one, 0)


def keep_column(lens_ref, row, start, block):
    total = jnp.int32(0)
    for j in range(lens_ref.shape[1]):
        total = total + lens_ref[row, j]
    pos = start + lax.broadcasted_iota(jnp.int32, (block, 1), 0)
    return (pos < total).astype(F32)


def head_row(h, value):
    lane = lax.broadcasted_iota(jnp.int32, (1, 2 * HEAD), 1)
    low = h % 2 * HEAD
    return jnp.where((lane >= low) & (lane < low + HEAD), value, 0.0).astype(BF16)


def front_kernel(
    lens_ref, tokens_ref, cot_in_ref, gain_ref, shift_ref, qv_bias_ref, wq_ref, wk_ref, wv_ref,
    q_ref, k_ref, v_ref, o_ref, lse_ref, x_ref, cot_ref,
    arrived, normed, bias, value_t, out_t, vectors, send_sem, recv_sem, copy_sem,
):
    tokens, width = x_ref.shape
    lanes = wq_ref.shape[1]
    block = tokens_ref.shape[1]
    blocks = tokens // block
    place = Place()
    mine = pl.ds(place.seq, 1)
    sources, targets = (tokens_ref, cot_in_ref), (arrived, cot_ref)

    def outgoing(which, hop):
        other, row = place.in_plane(hop)
        return row, send(
            sources[which].at[jnp.minimum(row, 2)], targets[which].at[place.seq],
            send_sem.at[which, hop - 1], recv_sem.at[which, hop - 1], other,
        )

    def local(which):
        return pltpu.make_async_copy(
            sources[which].at[place.my_row], targets[which].at[place.seq], copy_sem.at[which]
        )

    def start(which):
        for hop in (1, 2, 3):
            row, copy = outgoing(which, hop)
            pl.when(row < 3)(copy.start)
        pl.when(place.active)(local(which).start)

    def arrive(which, hop):
        if hop == 0:
            pl.when(place.active)(local(which).wait)
        else:
            pl.when(place.active)(outgoing(which, hop)[1].wait_recv)

    def leave(which):
        for hop in (1, 2, 3):
            row, copy = outgoing(which, hop)
            pl.when(row < 3)(copy.wait_send)

    @pl.when(pl.program_id(0) == 0)
    def _():
        place.greet_plane()
        start(0)
        vectors[0:1, :] = gain_ref[...].reshape(1, width)
        vectors[1:2, :] = shift_ref[...].reshape(1, width)
        for i in range(2):
            vectors[2 + i : 3 + i, :] = qv_bias_ref[i * width : (i + 1) * width].reshape(1, width)
        fill_bias(lens_ref, place.my_row, bias, block)

        @pl.when(jnp.logical_not(place.active))
        def _():
            arrived[...] = jnp.zeros_like(arrived)

        for hop in range(4):
            arrive(0, hop)
            if hop == 3:
                start(1)
            i = place.in_plane(hop)[0][1]
            rows = pl.ds(pl.multiple_of(i * block, block), block)
            x = arrived[i]
            x_ref[rows, :] = x
            unit, _ = normalise(x.astype(F32))
            normed[rows, :] = (unit * vectors[0:1, :] + vectors[1:2, :]).astype(BF16)
        leave(0)

    group = pl.ds(pl.multiple_of(pl.program_id(0) * lanes, lanes), lanes)

    def project(i, carry):
        rows = pl.ds(pl.multiple_of(i * block, block), block)
        h1 = normed[rows, :]
        q_ref[rows, :] = (dot_nn(h1, wq_ref[...]) + vectors[2:3, group]).astype(BF16)
        k_ref[rows, :] = dot_nn(h1, wk_ref[...]).astype(BF16)
        values = dot_nn(h1, wv_ref[...]) + vectors[3:4, group]
        v_ref[rows, :] = values.astype(BF16)
        value_t[:, rows] = values.T.astype(BF16)
        return carry

    lax.fori_loop(0, blocks, project, 0)

    heads = lanes // HEAD
    turns = [(i, h) for i in range(blocks) for h in range(heads)]

    def score(i, h):
        rows, count = slice(i * block, (i + 1) * block), (i + 1) * block
        pair = slice(h // 2 * 2 * HEAD, (h // 2 + 1) * 2 * HEAD)
        queries = q_ref[rows, pair] * head_row(h, HEAD ** (-0.5))
        return dot_nt(k_ref[:count, pair], queries) + bias[:count, rows]

    def mix(i, h, probs, total):
        rows, count = slice(i * block, (i + 1) * block), (i + 1) * block
        own = slice(h * HEAD, (h + 1) * HEAD)
        out_t[own, :] = dot_nn(value_t[own, :count], probs) * (1.0 / total)
        if h == heads - 1:
            o_ref[rows, :] = out_t[...].T.astype(BF16)

    following, waiting = score(*turns[0]), None
    for turn, (i, h) in enumerate(turns):
        scores = following
        if turn + 1 < len(turns):
            following = score(*turns[turn + 1])
        if waiting is not None:
            mix(*waiting)
        top = jnp.max(scores, axis=0, keepdims=True)
        probs = jnp.exp(scores - top)
        total = jnp.sum(probs, axis=0, keepdims=True)
        lse_ref[0, h : h + 1, i * block : (i + 1) * block] = top + jnp.log(total)
        waiting = (i, h, probs.astype(BF16), total)
    mix(*waiting)

    @pl.when(pl.program_id(0) == pl.num_programs(0) - 1)
    def _():
        for hop in range(4):
            arrive(1, hop)
        leave(1)

        @pl.when(jnp.logical_not(place.active))
        def _():
            copy = pltpu.make_async_copy(arrived, cot_ref, copy_sem.at[1])
            copy.start()
            copy.wait()


def front(lens, tokens_in, cotangent, gain, shift, qkv_weight, qv_bias):
    rows, span, width = tokens_in.shape
    spans = lax.axis_size("seq")
    tokens = spans * span
    lanes = width // 3
    groups = width // lanes
    heads = max(8, lanes // HEAD)
    whole = lambda shape: pl.BlockSpec(shape, lambda g: (0,) * len(shape))
    columns = lambda shape, first: pl.BlockSpec(shape, lambda g: (0, first + g))
    act = jax.ShapeDtypeStruct((tokens, width), BF16)
    sem = lambda *shape: pltpu.SemaphoreType.DMA(shape)
    return pl.pallas_call(
        front_kernel,
        grid=(groups,),
        out_shape=(
            act, act, act, act, jax.ShapeDtypeStruct((groups, heads, tokens), F32), act,
            jax.ShapeDtypeStruct((spans, span, width), BF16),
        ),
        in_specs=[
            pl.BlockSpec(memory_space=pltpu.SMEM),
            pl.BlockSpec(memory_space=pl.ANY),
            pl.BlockSpec(memory_space=pl.ANY),
            whole((width,)),
            whole((width,)),
            whole((2 * width,)),
            columns((width, lanes), 0),
            columns((width, lanes), groups),
            columns((width, lanes), 2 * groups),
        ],
        out_specs=[columns((tokens, lanes), 0)] * 4
        + [
            pl.BlockSpec((1, heads, tokens), lambda g: (g, 0, 0)),
            whole((tokens, width)),
            pl.BlockSpec(memory_space=pl.ANY),
        ],
        scratch_shapes=[
            pltpu.VMEM((spans, span, width), BF16),
            pltpu.VMEM((tokens, width), BF16),
            pltpu.VMEM((tokens, tokens), F32),
            pltpu.VMEM((lanes, tokens), BF16),
            pltpu.VMEM((lanes, span), F32),
            pltpu.VMEM((8, width), F32),
            sem(2, 3), sem(2, 3), sem(2),
        ],
        compiler_params=pltpu.CompilerParams(
            collective_id=1, has_side_effects=True, vmem_limit_bytes=VMEM_LIMIT
        ),
        name="front",
    )(lens, tokens_in, cotangent, gain, shift, qv_bias, qkv_weight, qkv_weight, qkv_weight)


class Units:
    def __init__(self, place, fresh, out, recv0, recv1, recv2, recv3, recv4, part, send_sem, recv_sem, copy_sem):
        self.place, self.fresh, self.out, self.part = place, fresh, out, part
        self.recv = (recv0, recv1, recv2, recv3, recv4)
        self.send_sem, self.recv_sem, self.copy_sem = send_sem, recv_sem, copy_sem
        _, rows, columns = fresh.shape
        self.size = (rows // 2, rows // 4, rows // 8, rows // 16)
        self.wide = columns // 2
        self.bits = (place.core, place.first_bit, lax.rem(place.z, 2), lax.div(place.z, 2), place.second_bit)
        self.partners = (place.sibling, place.first, place.next_z, place.far_z, place.second)

    @staticmethod
    def scratch(count, n, rows, columns):
        vmem = lambda *shape: pltpu.VMEM((count, n, *shape), BF16)
        sem = pltpu.SemaphoreType.DMA
        return [vmem(rows // 2 ** k, columns) for k in range(1, 5)] + [
            vmem(rows // 16, columns // 2), vmem(rows // 16, columns // 2),
            sem((count, 10)), sem((count, 10)), sem((count,)),
        ]

    def part_of(self, stage, bit):
        if stage == 4:
            return slice(None), pl.ds(pl.multiple_of(bit * self.wide, self.wide), self.wide)
        size = self.size[stage]
        return pl.ds(pl.multiple_of(bit * size, size), size), slice(None)

    def region(self, stage):
        start = sum(bit * size for bit, size in zip(self.bits[: min(stage, 3) + 1], self.size))
        size = self.size[min(stage, 3)]
        rows = pl.ds(pl.multiple_of(start, size), size)
        return rows, self.part_of(4, self.bits[4])[1] if stage == 4 else slice(None)

    def copy(self, phase, u):
        sems = self.send_sem.at[u, phase], self.recv_sem.at[u, phase]
        if phase < 5:
            source = self.fresh if phase == 0 else self.recv[phase - 1].at[u]
            source = source.at[:, *self.part_of(phase, 1 - self.bits[phase])]
            return send(source, self.recv[phase].at[u], *sems, self.partners[phase])
        where = self.out.at[u, :, *self.region(9 - phase)]
        return send(self.part.at[u] if phase == 5 else where, where, *sems, self.partners[9 - phase])

    def local(self, u):
        return pltpu.make_async_copy(self.part.at[u], self.out.at[u, :, *self.region(4)], self.copy_sem.at[u])

    def add(self, phase, u):
        source = self.fresh if phase == 0 else self.recv[phase - 1].at[u]
        target = self.recv[phase].at[u]
        step = self.size[3]
        if phase == 4:
            own = source[:, :, self.part_of(4, self.bits[4])[1]].astype(F32)
            self.part[u] = (own + target[...].astype(F32)).astype(BF16)
            return

        def one(i, carry):
            here = pl.ds(pl.multiple_of(i * step, step), step)
            there = pl.ds(pl.multiple_of(self.bits[phase] * self.size[phase] + i * step, step), step)
            for panel in range(self.fresh.shape[0]):
                total = source[panel, there, :].astype(F32) + target[panel, here, :].astype(F32)
                target[panel, here, :] = total.astype(BF16)
            return carry

        lax.fori_loop(0, self.size[phase] // step, one, 0)

    def step(self, phase, u):
        if phase > 0:
            self.copy(phase - 1, u).wait()
            if phase == 6:
                self.local(u).wait()
        if 0 < phase < 6:
            self.add(phase - 1, u)
        if phase < 10:
            self.copy(phase, u).start()
        if phase == 5:
            self.local(u).start()


class Exchange:
    def __init__(self, place, source, target, send_sem, recv_sem, copy_sem):
        self.place, self.source, self.target = place, source, target
        self.send_sem, self.recv_sem, self.copy_sem = send_sem, recv_sem, copy_sem
        self.span = target.shape[1]

    def block(self, seq):
        return self.source.at[pl.ds(pl.multiple_of(seq * self.span, self.span), self.span)]

    def outgoing(self, hop):
        other, row = self.place.in_plane(hop)
        return row, send(
            self.block(other[1]), self.target.at[self.place.my_row],
            self.send_sem.at[hop - 1], self.recv_sem.at[hop - 1], other,
        )

    def local(self):
        return pltpu.make_async_copy(self.block(self.place.seq), self.target.at[self.place.my_row], self.copy_sem)

    def start(self, hop):
        pl.when(self.place.active)(self.outgoing(hop)[1].start)
        if hop == 3:
            pl.when(self.place.active)(self.local().start)

    def finish(self):
        for hop in (1, 2, 3):
            row, copy = self.outgoing(hop)
            pl.when(self.place.active)(copy.wait_send)
            pl.when(row < 3)(copy.wait_recv)
        pl.when(self.place.active)(self.local().wait)


def plan(hooks, sizes, made):
    free = {"core": 0.0, "plane": 0.0, "near": 0.0, "far": 0.0}
    delay = {"core": 1.5, "plane": 3.5, "near": 3.0, "far": 3.5}
    now, flight, plans, spare = 0.0, {}, {}, []
    small = len(sizes)

    def go(unit, phase):
        nonlocal now
        now += 0.3
        if phase == (4 if unit == small else 10):
            del flight[unit]
            return
        if unit == small:
            kind, time = ("core", "plane", "plane", "far")[phase], 0.3
        else:
            stage = min(phase, 9 - phase)
            kind = ("core", "plane", "near", "far", "plane")[stage]
            time = sizes[unit] * (0.5 / 0.6, 0.25 / 0.094, 0.25 / 0.094, 0.25 / 0.094, 0.03125 / 0.094)[stage]
        begin = max(now, free[kind])
        free[kind] = begin + time
        if kind == "far":
            free["near"] = max(now, free["near"]) + time / 2
        flight[unit] = (phase, begin + time + delay[kind])

    def fill(items):
        if spare and free["plane"] <= now + 4.0:
            free["plane"] = now + 5.3
            items.append(spare.pop(0))

    for name, compute in hooks:
        now += compute
        items = plans[name] = []
        for unit in sorted(flight, key=lambda u: flight[u][1]):
            phase, end = flight[unit]
            if end <= now + 0.5:
                items.append((unit, phase + 1))
                go(unit, phase + 1)
        for unit, hook in made.items():
            if hook == name:
                items.append((unit, 0))
                go(unit, 0)
        if name in ("lo", "dx"):
            spare += [(name, hop) for hop in (3, 1, 2)]
        fill(items)
    tail = [(small, 0)]
    go(small, 0)
    while flight:
        unit = min(flight, key=lambda u: flight[u][1])
        phase, end = flight[unit]
        now = max(now, end)
        tail.append((unit, phase + 1))
        go(unit, phase + 1)
        fill(tail)
    return plans, tail + spare, max(now, free["plane"] + 3.5)


def timetable(steps, groups):
    hooks = []
    for s in range(steps):
        hooks += [(("early", s), 18.0 if s == 0 else 3.0), (("late", s), 3.0), (("fed", s), 2.6)]
    hooks += [("lo", 7.0), ("proj", 1.5), ("turn", 3.0)]
    for s in range(steps, steps + groups):
        hooks += [(("low", s), 6.0 + 1.2 * (s > steps)), (("high", s), 4.0), (("made", s), 1.8)]
    hooks.append(("dx", 4.2))
    made = {s: ("fed", s) for s in range(steps)}
    made[steps] = "proj"
    made.update({steps + 1 + g: ("made", steps + g) for g in range(groups)})
    return hooks, made


def body_kernel(
    steps, groups,
    lens_ref, o_ref, x_ref, cot_ref, wp_ref, bp_ref, gain2_ref, shift2_ref, wf_ref, bf_ref, wo_ref, bo_ref,
    gain1_ref, shift1_ref, q_ref, k_ref, v_ref, lse_ref, wq_ref, wk_ref, wv_ref,
    lo_out, dx_out, feed_out, rest_out, small_out,
    middle, normed, normed_t, cot_low, out_acc, back_acc, hidden, back_low, bias, key_t, grad_q_t, delta, vectors,
    fresh_feed, fresh_rest, sums, small_recv, line_sums,
    small_send, small_recv_sem, out_send, out_recv, out_copy, *unit_scratch,
):
    tokens, width = x_ref.shape
    lanes = wq_ref.shape[1]
    span = lo_out.shape[1]
    blocks = tokens // span
    step = pl.program_id(0)
    place = Place()
    acc = sums.at[0]

    sets = [
        Units(place, fresh_feed, feed_out, *unit_scratch[:9]), Units(place, fresh_rest, rest_out, *unit_scratch[9:])
    ]
    small = SmallReducer(place, sums, small_recv, line_sums, small_send, small_recv_sem)
    lo_back = Exchange(place, normed, lo_out, out_send.at[0], out_recv.at[0], out_copy.at[0])
    dx_back = Exchange(place, cot_low, dx_out, out_send.at[1], out_recv.at[1], out_copy.at[1])
    exchanges = {"lo": lo_back, "dx": dx_back}

    hooks, made = timetable(steps, groups)
    panel = width * width * 2e-6
    count = steps + 1 + groups
    plans, tail, _ = plan(hooks, [2 * panel] * steps + [panel] * (1 + groups), made)
    order = [name for name, _ in hooks]
    freed = {u: order.index(name) for name, items in plans.items() for u, phase in items if phase == 1}
    for u in [*range(steps - 1), *range(steps, steps + groups)]:
        assert freed[u] < order.index(made[u + 1])

    def chosen(pairs, index):
        value, found = jnp.int32(0), jnp.int32(0)
        for key, item in pairs:
            hit = (index == key).astype(jnp.int32)
            value, found = value + hit * item, found + hit
        return value, found > 0

    def start(item, index=None):
        u, phase = item
        if u in exchanges:
            return functools.partial(exchanges[u].start, phase)
        if u == count:
            return functools.partial(small.step, phase)
        return functools.partial(sets[u >= steps].step, phase, number(item) if index is None else index)

    def kind(item):
        u, phase = item
        return (u if u in exchanges or u == count else int(u >= steps)), phase

    def number(item):
        u = item[0]
        return 0 if u in exchanges or u == count else u - steps * (u >= steps)

    def hook(name):
        if name in plans:
            for item in plans[name]:
                start(item)()
            return
        bodies = {}
        for s in range(steps + groups):
            seen = {}
            for item in plans.get((name, s), []):
                turn = seen[kind(item)] = seen.get(kind(item), -1) + 1
                bodies.setdefault((kind(item), turn), []).append((s, item))
        for _, pairs in sorted(bodies.items(), key=lambda body: -body[0][0][1]):
            index, found = chosen([(s, number(item)) for s, item in pairs], step)
            pl.when(found)(start(pairs[0][1], index))

    def each(body, first=0, last=blocks):
        def run(i, carry):
            start = pl.multiple_of(i * span, span)
            body(start, pl.ds(start, span))
            return carry

        lax.fori_loop(first, last, run, 0)

    def column_sum(values):
        return jnp.sum(values, axis=0, keepdims=True)

    @pl.when(step == 0)
    def _():
        place.greet()
        acc[...] = jnp.zeros_like(acc)
        for i, ref in enumerate((bp_ref, gain2_ref, shift2_ref, bo_ref, gain1_ref, shift1_ref)):
            vectors[i : i + 1, :] = ref[...].reshape(1, width)
        for f in range(steps):
            vectors[8 + f : 9 + f, :] = bf_ref[f * width : (f + 1) * width].reshape(1, width)

        def begin(start, rows):
            attn = dot_nn(o_ref[rows, :], wp_ref[...]) + vectors[0:1, :]
            mid = x_ref[rows, :].astype(F32) + branch_scale * attn
            middle[rows, :] = mid
            unit, _ = normalise(mid)
            h2 = unit * vectors[1:2, :] + vectors[2:3, :]
            normed[rows, :] = h2.astype(BF16)
            keep = keep_column(lens_ref, place.my_row, start, span)
            low = (branch_scale * (keep * cot_ref[rows, :].astype(F32))).astype(BF16)
            cot_low[rows, :] = low
            acc[4:5, :] += column_sum(low.astype(F32))
            out_acc[rows, :] = jnp.zeros((span, width), F32)
            back_acc[rows, :] = jnp.zeros((span, width), F32)

        each(begin)

    @pl.when(step < steps)
    def _():
        def chunk(start, rows):
            pre = dot_nn(normed[rows, :], wf_ref[...]) + vectors[pl.ds(8 + step, 1), :]
            back = dot_nt(cot_low[rows, :], wo_ref[...])
            square = pre * pre
            root = (2.0 / jnp.pi) ** 0.5
            bend = jnp.tanh(pre * (root + (root * 0.044715) * square))
            half = 0.5 * pre
            hid = (half + half * bend).astype(BF16)
            slope = (0.5 + 0.5 * bend) + half * (1.0 - bend * bend) * (root + (3.0 * root * 0.044715) * square)
            grad = (back * slope).astype(BF16)
            hidden[rows, :] = hid
            back_low[rows, :] = grad
            acc[pl.ds(8 + step, 1), :] += column_sum(grad.astype(F32))
            out_acc[rows, :] += dot_nn(hid, wo_ref[...])
            back_acc[rows, :] += dot_nt(grad, wf_ref[...])

        each(chunk, 0, blocks // 2)
        hook("early")
        each(chunk, blocks // 2, blocks)
        hook("late")
        fresh_feed[0] = dot_tn(hidden[...], cot_low[...]).astype(BF16)
        fresh_feed[1] = dot_tn(normed[...], back_low[...]).astype(BF16)
        hook("fed")

    @pl.when(step == steps - 1)
    def _():
        def end(start, rows):
            keep = keep_column(lens_ref, place.my_row, start, span)
            mid = middle[rows, :]
            normed[rows, :] = (
                keep * (mid + branch_scale * (out_acc[rows, :] + vectors[3:4, :]))
            ).astype(BF16)
            unit, inverse = normalise(mid)
            back = back_acc[rows, :]
            back_acc[rows, :] = jnp.zeros((span, width), F32)
            acc[5:6, :] += column_sum(back * unit)
            acc[6:7, :] += column_sum(back)
            scaled = back * vectors[1:2, :]
            grad = keep * cot_ref[rows, :].astype(F32) + inverse * (
                scaled - row_mean(scaled) - unit * row_mean(scaled * unit)
            )
            middle[rows, :] = grad
            low = (branch_scale * grad).astype(BF16)
            hidden[rows, :] = low
            acc[7:8, :] += column_sum(low.astype(F32))
            back_low[rows, :] = dot_nt(low, wp_ref[...]).astype(BF16)

        each(end)
        hook("lo")
        fresh_rest[0] = dot_tn(o_ref[...], hidden[...]).astype(BF16)
        hook("proj")

    @pl.when(step == steps)
    def _():
        fill_bias(lens_ref, place.my_row, bias, span)

        def turn(start, rows):
            unit, _ = normalise(x_ref[rows, :].astype(F32))
            normed_t[:, rows] = (unit * vectors[4:5, :] + vectors[5:6, :]).T.astype(BF16)

        each(turn)
        hook("turn")

    @pl.when(step >= steps)
    def _():
        group = pl.ds(pl.multiple_of((step - steps) * lanes, lanes), lanes)
        grad_k, grad_v = out_acc.at[:, :lanes], out_acc.at[:, lanes : 2 * lanes]
        grad_q, d_out = hidden.at[:, :lanes], hidden.at[:, lanes : 2 * lanes]
        grad_k[...] = jnp.zeros_like(grad_k)
        grad_v[...] = jnp.zeros_like(grad_v)
        grad_q_t[...] = jnp.zeros_like(grad_q_t)
        key_t[...] = k_ref[...].astype(F32).T.astype(BF16)
        head_id = lax.broadcasted_iota(jnp.int32, (8, lanes), 0)
        lane_id = lax.broadcasted_iota(jnp.int32, (8, lanes), 1)
        member = ((lane_id >= head_id * HEAD) & (lane_id < (head_id + 1) * HEAD)).astype(F32)

        def prepare(start, rows):
            grads = back_low[rows, group]
            d_out[rows, :] = grads
            product = grads.astype(F32) * o_ref[rows, group].astype(F32)
            delta[:, rows] = lax.dot_general(
                member, product, (((1,), (1,)), ((), ())),
                precision=lax.Precision.HIGHEST, preferred_element_type=F32,
            )

        each(prepare)
        heads = lanes // HEAD

        def tile(t, carry):
            i = sum((t >= b * (b + 1) // 2).astype(jnp.int32) for b in range(1, blocks))
            first = pl.multiple_of(i * span, span)
            key_first = pl.multiple_of((t - lax.div(i * (i + 1), 2)) * span, span)
            rows, keys = pl.ds(first, span), pl.ds(key_first, span)
            mask = bias[keys, rows]

            def start(h):
                pair = slice(h // 2 * 2 * HEAD, (h // 2 + 1) * 2 * HEAD)
                queries = q_ref[rows, pair] * head_row(h, HEAD ** (-0.5))
                grads = d_out[rows, pair] * head_row(h, 1.0)
                return queries, grads, dot_nt(k_ref[keys, pair], queries) + mask, dot_nt(v_ref[keys, pair], grads)

            following = start(0)
            for h in range(heads):
                pair = slice(h // 2 * 2 * HEAD, (h // 2 + 1) * 2 * HEAD)
                own = slice(h * HEAD, (h + 1) * HEAD)
                queries, grads, scores, grad_probs = following
                if h + 1 < heads:
                    following = start(h + 1)
                probs = jnp.exp(scores - lse_ref[0, h : h + 1, rows])
                grad_scores = (probs * (grad_probs - delta[h : h + 1, rows])).astype(BF16)
                grad_v[keys, pair] += dot_nn(probs.astype(BF16), grads)
                grad_k[keys, pair] += dot_nn(grad_scores, queries)
                grad_q_t[own, rows] += dot_nn(key_t[own, keys], grad_scores)
            return carry

        tiles = blocks * (blocks + 1) // 2
        lax.fori_loop(0, tiles - blocks, tile, 0)
        hook("low")
        lax.fori_loop(tiles - blocks, tiles, tile, 0)
        hook("high")

        def close(start, rows):
            dq = (grad_q_t[:, rows].T * HEAD ** (-0.5)).astype(BF16)
            grad_q[rows, :] = dq
            acc[2:3, group] += column_sum(dq.astype(F32))
            acc[3:4, group] += column_sum(grad_v[rows, :].astype(BF16).astype(F32))

        each(close)
        for p, grad in enumerate((grad_q, grad_k, grad_v)):
            fresh_rest[0, :, p * lanes : (p + 1) * lanes] = dot_nn(normed_t[...], grad[...].astype(BF16)).astype(BF16)
        hook("made")

        def pull(start, rows):
            back_acc[rows, :] += (
                dot_nt(grad_q[rows, :], wq_ref[...])
                + dot_nt(grad_k[rows, :].astype(BF16), wk_ref[...])
                + dot_nt(grad_v[rows, :].astype(BF16), wv_ref[...])
            )

        each(pull)

    @pl.when(step == steps + groups - 1)
    def _():
        def last(start, rows):
            unit, inverse = normalise(x_ref[rows, :].astype(F32))
            back = back_acc[rows, :]
            acc[0:1, :] += column_sum(back * unit)
            acc[1:2, :] += column_sum(back)
            scaled = back * vectors[4:5, :]
            grad = middle[rows, :] + inverse * (
                scaled - row_mean(scaled) - unit * row_mean(scaled * unit)
            )
            cot_low[rows, :] = grad.astype(BF16)

        each(last)
        hook("dx")
        kinds = sorted({kind(item) for item in tail}, key=str)
        codes = [(t, kinds.index(kind(item)) * count + number(item)) for t, item in enumerate(tail)]

        def turn(t, carry):
            code, _ = chosen(codes, t)
            which, index = lax.div(code, count), lax.rem(code, count)
            for k, this in enumerate(kinds):
                item = next(item for item in tail if kind(item) == this)
                pl.when(which == k)(start(item, index))
            return carry

        lax.fori_loop(0, len(tail), turn, 0)
        small_out[...] = small.total()
        lo_back.finish()
        dx_back.finish()


def body(
    lens, o, x, cot, q, k, v, lse, rows, span,
    ln1_gain, ln1_bias, qkv_weight, proj_weight, proj_bias, ln2_gain, ln2_bias, fc_weight, fc_bias, out_weight, out_bias,
):
    tokens, width = x.shape
    groups, heads, _ = lse.shape
    lanes = width // groups
    steps = fc_weight.shape[1] // width
    shape = jax.ShapeDtypeStruct
    once = pl.Buffered(1)
    whole = lambda *dims: pl.BlockSpec(dims, lambda s: (0,) * len(dims), pipeline_mode=once)
    act, vec, mat = whole(tokens, width), whole(width), whole(width, width)
    feed_step = lambda s: jnp.minimum(s, steps - 1)
    back_step = lambda s: jnp.maximum(s - steps, 0)
    columns = lambda dims, first: pl.BlockSpec(dims, lambda s: (0, first + back_step(s)))
    anywhere = pl.BlockSpec(memory_space=pl.ANY)
    f32 = lambda *dims: pltpu.VMEM(dims, F32)
    bf16 = lambda *dims: pltpu.VMEM(dims, BF16)
    sem = lambda *dims: pltpu.SemaphoreType.DMA(dims)
    return pl.pallas_call(
        functools.partial(body_kernel, steps, groups),
        grid=(steps + groups,),
        out_shape=(
            shape((rows, span, width), BF16),
            shape((rows, span, width), BF16),
            shape((steps, 2, width, width), BF16),
            shape((1 + groups, 1, width, width), BF16),
            shape((16, width), F32),
        ),
        in_specs=[
            pl.BlockSpec(memory_space=pltpu.SMEM),
            act, act, act, mat, vec, vec, vec,
            pl.BlockSpec((width, width), lambda s: (0, feed_step(s))),
            whole(steps * width),
            pl.BlockSpec((width, width), lambda s: (feed_step(s), 0)),
            vec, vec, vec,
            columns((tokens, lanes), 0), columns((tokens, lanes), 0), columns((tokens, lanes), 0),
            pl.BlockSpec((1, heads, tokens), lambda s: (back_step(s), 0, 0)),
            columns((width, lanes), 0), columns((width, lanes), groups), columns((width, lanes), 2 * groups),
        ],
        out_specs=[anywhere] * 4 + [pl.BlockSpec((16, width), lambda s: (0, 0))],
        scratch_shapes=[
            f32(tokens, width), bf16(tokens, width), bf16(width, tokens), bf16(tokens, width),
            f32(tokens, width), f32(tokens, width), bf16(tokens, width), bf16(tokens, width),
            f32(tokens, tokens), bf16(lanes, tokens), f32(lanes, tokens), f32(8, tokens), f32(16, width),
            bf16(2, width, width), bf16(1, width, width), f32(4, 16, width), f32(3, 16, width), f32(4, 16, width),
            sem(6), sem(6), sem(2, 3), sem(2, 3), sem(2),
            *Units.scratch(steps, 2, width, width), *Units.scratch(1 + groups, 1, width, width),
        ],
        compiler_params=pltpu.CompilerParams(
            collective_id=0, has_side_effects=True, vmem_limit_bytes=VMEM_LIMIT
        ),
        name="body",
    )(
        lens, o, x, cot, proj_weight, proj_bias, ln2_gain, ln2_bias, fc_weight, fc_bias, out_weight, out_bias,
        ln1_gain, ln1_bias, q, k, v, lse, qkv_weight, qkv_weight, qkv_weight,
    )


def finish_kernel(
    feed_ref, proj_ref, qkv_ref, small_ref, dx_ref,
    ln1_gain, ln1_bias, qkv_weight, qv_bias, proj_weight, proj_bias,
    ln2_gain, ln2_bias, fc_weight, fc_bias, out_weight, out_bias, input_grad,
):
    width = small_ref.shape[1]
    lanes = qkv_ref.shape[3]
    groups = width // lanes
    out_weight[...] = feed_ref[0, 0].astype(F32)
    fc_weight[...] = feed_ref[0, 1].astype(F32)
    for g in range(groups):
        qkv_weight[:, g * lanes : (g + 1) * lanes] = qkv_ref[1 + g, 0].astype(F32)
    proj_weight[...] = proj_ref[0, 0].astype(F32)
    input_grad[...] = dx_ref[...].astype(F32)

    @pl.when((pl.program_id(0) == 0) & (pl.program_id(1) == 0))
    def _():
        for ref, first in (
            (ln1_gain, 0), (ln1_bias, 1), (qv_bias, 2), (out_bias, 4),
            (ln2_gain, 5), (ln2_bias, 6), (proj_bias, 7), (fc_bias, 8),
        ):
            for i in range(ref.shape[0] // width):
                ref[i * width : (i + 1) * width] = small_ref[first + i]


def finish(feed_sums, rest_sums, small, dx):
    steps, _, width, _ = feed_sums.shape
    groups = rest_sums.shape[0] - 1
    lanes = width // groups
    rows, span, _ = dx.shape
    cuts = 1
    half = width // cuts
    shape = lambda *dims: jax.ShapeDtypeStruct(dims, F32)
    flat = lambda n: pl.BlockSpec((n * width,), lambda f, r: (0,))
    third = lambda f: jnp.minimum(f, 2)
    row = pl.BlockSpec((1, span // cuts, width), lambda f, r: (jnp.minimum(f, rows - 1), jnp.where(f > rows - 1, cuts - 1, r), 0))
    return pl.pallas_call(
        finish_kernel,
        grid=(steps, cuts),
        out_shape=(
            shape(width), shape(width), shape(width, 3 * width), shape(2 * width),
            shape(width, width), shape(width), shape(width), shape(width),
            shape(width, steps * width), shape(steps * width), shape(steps * width, width), shape(width),
            shape(rows, span, width),
        ),
        in_specs=[
            pl.BlockSpec((1, 2, half, width), lambda f, r: (f, 0, r, 0)),
            pl.BlockSpec((1, 1, half, width), lambda f, r: (0, 0, jnp.where(f == steps - 1, r, 0), 0)),
            pl.BlockSpec((1 + groups, 1, half, lanes), lambda f, r: (0, 0, jnp.where(f > 2, cuts - 1, r), third(f))),
            pl.BlockSpec((16, width), lambda f, r: (0, 0)),
            row,
        ],
        out_specs=[
            flat(1), flat(1),
            pl.BlockSpec((half, width), lambda f, r: (jnp.where(f > 2, cuts - 1, r), third(f))),
            flat(2),
            pl.BlockSpec((half, width), lambda f, r: (jnp.where(f == steps - 1, r, 0), 0)),
            flat(1), flat(1), flat(1),
            pl.BlockSpec((half, width), lambda f, r: (r, f)),
            flat(steps),
            pl.BlockSpec((half, width), lambda f, r: (cuts * f + r, 0)),
            flat(1),
            row,
        ],
        compiler_params=pltpu.CompilerParams(vmem_limit_bytes=VMEM_LIMIT),
        name="finish",
    )(feed_sums, rest_sums, rest_sums, small, dx)


def by_rows(
    tokens_in, lengths, ln1_gain, ln1_bias, qkv_weight, qv_bias, proj_weight, proj_bias,
    ln2_gain, ln2_bias, fc_weight, fc_bias, out_weight, out_bias, cotangent,
):
    rows, span, width = tokens_in.shape
    q, k, v, o, lse, x, cot = front(
        lengths, tokens_in, cotangent, ln1_gain, ln1_bias, qkv_weight, qv_bias
    )
    layer_out, dx, feed_sums, rest_sums, small = body(
        lengths, o, x, cot.reshape(x.shape), q, k, v, lse, rows, span,
        ln1_gain, ln1_bias, qkv_weight, proj_weight, proj_bias, ln2_gain, ln2_bias,
        fc_weight, fc_bias, out_weight, out_bias,
    )
    *grads, input_grad = finish(feed_sums, rest_sums, small, dx)
    return (layer_out, input_grad, *grads)


def layer_norm(values, gain, shift):
    center = values - jnp.mean(values, axis=-1, keepdims=True)
    spread = jnp.mean(center * center, axis=-1, keepdims=True)
    return center * lax.rsqrt(spread + norm_eps) * gain + shift


def gelu_tanh(values):
    return jax.nn.gelu(values, approximate=True)


def left_dot(left, right):
    return lax.dot_general(
        left, right, (((0,), (0,)), ((), ())), preferred_element_type=jnp.float32
    )


def right_dot(left, right):
    return lax.dot_general(
        left, right, (((1,), (1,)), ((), ())), preferred_element_type=jnp.float32
    )


def allowed_mask(query_pos, query_seg, key_pos, key_seg):
    return (key_pos[None, None, :] <= query_pos[None, :, None]) & (
        key_seg[:, None, :] == query_seg[:, :, None]
    )


def local(
    tokens_in,
    lengths,
    ln1_gain,
    ln1_bias,
    qkv_weight,
    qv_bias,
    proj_weight,
    proj_bias,
    ln2_gain,
    ln2_bias,
    fc_weight,
    fc_bias,
    out_weight,
    out_bias,
    cotangent,
):
    row_count, span_len, model_width = tokens_in.shape
    head_count = model_width // HEAD
    scale = HEAD ** (-0.5)
    seq_parts = lax.axis_size("seq")
    row_len = span_len * seq_parts
    first_pos = lax.axis_index("seq") * span_len
    doc_count = lengths.shape[1]
    positions = jnp.arange(row_len, dtype=jnp.int32)
    ends = jnp.cumsum(lengths, axis=1)
    segments = jnp.sum((positions[None, :, None] >= ends[:, None, :]).astype(jnp.int32), axis=2)
    my_segs = lax.dynamic_slice_in_dim(segments, first_pos, span_len, 1)
    my_pos = first_pos + jnp.arange(span_len, dtype=jnp.int32)
    token_count = row_count * span_len
    keep_flat = (my_segs < doc_count).astype(jnp.float32).reshape(token_count, 1)
    inputs = tokens_in.astype(jnp.float32).reshape(token_count, model_width)
    normed = layer_norm(inputs, ln1_gain, ln1_bias)
    normed_low = normed.astype(jnp.bfloat16)
    bias_full = jnp.concatenate(
        [qv_bias[:model_width], jnp.zeros((model_width,), jnp.float32), qv_bias[model_width:]]
    )
    projected = (
        jnp.dot(normed_low, qkv_weight, preferred_element_type=jnp.float32) + bias_full
    ).astype(jnp.bfloat16)
    projected = projected.reshape(row_count, span_len, 3 * model_width)
    queries = projected[..., :model_width]
    keys = projected[..., model_width : 2 * model_width]
    values = projected[..., 2 * model_width :]
    query_heads = queries.reshape(row_count, span_len, head_count, HEAD)
    key_heads = keys.reshape(row_count, span_len, head_count, HEAD)
    value_heads = values.reshape(row_count, span_len, head_count, HEAD)
    last_pos = first_pos + span_len - 1
    start_state = (
        jnp.full((row_count, head_count, span_len), masked_value, jnp.float32),
        jnp.zeros((row_count, head_count, span_len), jnp.float32),
        jnp.zeros((row_count, span_len, model_width), jnp.float32),
    )
    key_piece = lax.all_gather(keys, "seq", axis=1, tiled=True)
    value_piece = lax.all_gather(values, "seq", axis=1, tiled=True)
    count = key_piece.shape[1]

    def forward_update(state):
        top, total, accum = state
        piece_keys = key_piece.reshape(row_count, count, head_count, HEAD)
        piece_values = value_piece.reshape(row_count, count, head_count, HEAD)
        scores = (
            jnp.einsum(
                "rqhd,rkhd->rhqk", query_heads, piece_keys, preferred_element_type=jnp.float32
            )
            * scale
        )
        key_pos = jnp.arange(count, dtype=jnp.int32)
        allowed = allowed_mask(my_pos, my_segs, key_pos, segments)[:, None]
        scores = jnp.where(allowed, scores, masked_value)
        new_top = jnp.maximum(top, jnp.max(scores, axis=-1))
        weights = jnp.where(allowed, jnp.exp(scores - new_top[..., None]), 0.0)
        total = jnp.sum(weights, axis=-1)
        added = jnp.einsum(
            "rhqk,rkhd->rqhd",
            weights.astype(jnp.bfloat16),
            piece_values,
            preferred_element_type=jnp.float32,
        )
        accum = added.reshape(row_count, span_len, model_width)
        return (new_top, total, accum)

    top, total, accum = lax.cond(
        jnp.int32(0) > last_pos, lambda state: state, forward_update, start_state
    )
    log_total = top + jnp.log(total)
    attended_heads = (
        accum.reshape(row_count, span_len, head_count, HEAD) / total.transpose(0, 2, 1)[..., None]
    )
    attended = attended_heads.reshape(token_count, model_width)
    attended_low = attended.astype(jnp.bfloat16)
    attn_out = jnp.dot(attended_low, proj_weight, preferred_element_type=jnp.float32) + proj_bias
    middle = inputs + branch_scale * attn_out
    normed_two = layer_norm(middle, ln2_gain, ln2_bias)
    normed_two_low = normed_two.astype(jnp.bfloat16)
    hidden_pre = jnp.dot(normed_two_low, fc_weight, preferred_element_type=jnp.float32) + fc_bias
    hidden_low = gelu_tanh(hidden_pre).astype(jnp.bfloat16)
    branch_out = jnp.dot(hidden_low, out_weight, preferred_element_type=jnp.float32) + out_bias
    layer_out = (
        ((middle + branch_scale * branch_out) * keep_flat)
        .astype(jnp.bfloat16)
        .reshape(row_count, span_len, model_width)
    )
    grad_final = keep_flat * cotangent.astype(jnp.float32).reshape(token_count, model_width)
    grad_branch = (branch_scale * grad_final).astype(jnp.bfloat16)
    grad_out_weight = left_dot(hidden_low, grad_branch)
    grad_out_bias = jnp.sum(grad_branch.astype(jnp.float32), axis=0)
    grad_hidden = right_dot(grad_branch, out_weight)
    gelu_value, gelu_pull = jax.vjp(gelu_tanh, hidden_pre)
    grad_pre = gelu_pull(grad_hidden)[0].astype(jnp.bfloat16)
    grad_fc_weight = left_dot(normed_two_low, grad_pre)
    grad_fc_bias = jnp.sum(grad_pre.astype(jnp.float32), axis=0)
    grad_normed_two = right_dot(grad_pre, fc_weight)
    norm_value, norm_pull = jax.vjp(layer_norm, middle, ln2_gain, ln2_bias)
    grad_mid_norm, grad_ln2_gain, grad_ln2_bias = norm_pull(grad_normed_two)
    grad_middle = grad_final + grad_mid_norm
    grad_attn = (branch_scale * grad_middle).astype(jnp.bfloat16)
    grad_proj_weight = left_dot(attended_low, grad_attn)
    grad_proj_bias = jnp.sum(grad_attn.astype(jnp.float32), axis=0)
    grad_attended = (
        right_dot(grad_attn, proj_weight)
        .astype(jnp.bfloat16)
        .reshape(row_count, span_len, model_width)
    )
    grad_att_heads = grad_attended.reshape(row_count, span_len, head_count, HEAD)
    delta = jnp.sum(grad_att_heads.astype(jnp.float32) * attended_heads, axis=-1)
    delta_t = delta.transpose(0, 2, 1)
    zero_grad = jnp.zeros((row_count, span_len, model_width), jnp.float32)
    query_key_piece = lax.all_gather(keys, "seq", axis=1, tiled=True)
    query_value_piece = lax.all_gather(values, "seq", axis=1, tiled=True)
    query_count = query_key_piece.shape[1]

    def query_update(carry):
        piece_keys = query_key_piece.reshape(row_count, query_count, head_count, HEAD)
        piece_values = query_value_piece.reshape(row_count, query_count, head_count, HEAD)
        scores = (
            jnp.einsum(
                "rqhd,rkhd->rhqk", query_heads, piece_keys, preferred_element_type=jnp.float32
            )
            * scale
        )
        key_pos = jnp.arange(query_count, dtype=jnp.int32)
        allowed = allowed_mask(my_pos, my_segs, key_pos, segments)[:, None]
        probs = jnp.where(allowed, jnp.exp(scores - log_total[..., None]), 0.0)
        grad_probs = jnp.einsum(
            "rqhd,rkhd->rhqk", grad_att_heads, piece_values, preferred_element_type=jnp.float32
        )
        grad_scores = (probs * (grad_probs - delta_t[..., None])).astype(jnp.bfloat16)
        added = jnp.einsum(
            "rhqk,rkhd->rqhd", grad_scores, piece_keys, preferred_element_type=jnp.float32
        )
        return scale * added.reshape(row_count, span_len, model_width)

    grad_queries = lax.cond(jnp.int32(0) > last_pos, lambda carry: carry, query_update, zero_grad)
    stats_lse, stats_delta = (
        lax.all_gather(
            log_total.transpose(0, 2, 1).astype(jnp.bfloat16), "seq", axis=1, tiled=True
        ).astype(jnp.float32),
        lax.all_gather(delta.astype(jnp.bfloat16), "seq", axis=1, tiled=True).astype(delta.dtype),
    )
    query_piece_in = lax.all_gather(queries, "seq", axis=1, tiled=True)
    grad_piece_in = lax.all_gather(grad_attended, "seq", axis=1, tiled=True)
    key_count = query_piece_in.shape[1]

    def key_update(state):
        piece_queries = query_piece_in.reshape(row_count, key_count, head_count, HEAD)
        piece_grads = grad_piece_in.reshape(row_count, key_count, head_count, HEAD)
        scores = (
            jnp.einsum(
                "rqhd,rkhd->rhqk", piece_queries, key_heads, preferred_element_type=jnp.float32
            )
            * scale
        )
        query_pos = jnp.arange(key_count, dtype=jnp.int32)
        allowed = allowed_mask(query_pos, segments, my_pos, my_segs)[:, None]
        piece_lse = stats_lse.transpose(0, 2, 1)
        piece_delta = stats_delta.transpose(0, 2, 1)
        probs = jnp.where(allowed, jnp.exp(scores - piece_lse[..., None]), 0.0)
        add_v = jnp.einsum(
            "rhqk,rqhd->rkhd",
            probs.astype(jnp.bfloat16),
            piece_grads,
            preferred_element_type=jnp.float32,
        )
        grad_probs = jnp.einsum(
            "rqhd,rkhd->rhqk", piece_grads, value_heads, preferred_element_type=jnp.float32
        )
        grad_scores = (probs * (grad_probs - piece_delta[..., None])).astype(jnp.bfloat16)
        add_k = jnp.einsum(
            "rhqk,rqhd->rkhd", grad_scores, piece_queries, preferred_element_type=jnp.float32
        )
        return (
            scale * add_k.reshape(row_count, span_len, model_width),
            add_v.reshape(row_count, span_len, model_width),
        )

    grad_keys, grad_values = lax.cond(
        jnp.int32(0) + key_count <= first_pos,
        lambda state: state,
        key_update,
        (zero_grad, zero_grad),
    )
    grad_projected = (
        jnp.concatenate([grad_queries, grad_keys, grad_values], axis=-1)
        .astype(jnp.bfloat16)
        .reshape(token_count, 3 * model_width)
    )
    grad_qkv_weight = left_dot(normed_low, grad_projected)
    column_sums = jnp.sum(grad_projected.astype(jnp.float32), axis=0)
    grad_qv_bias = jnp.concatenate([column_sums[:model_width], column_sums[2 * model_width :]])
    grad_normed = right_dot(grad_projected, qkv_weight)
    first_value, first_pull = jax.vjp(layer_norm, inputs, ln1_gain, ln1_bias)
    grad_in_norm, grad_ln1_gain, grad_ln1_bias = first_pull(grad_normed)
    input_grad = (grad_middle + grad_in_norm).reshape(row_count, span_len, model_width)
    local_grads = (
        grad_ln1_gain,
        grad_ln1_bias,
        grad_qkv_weight,
        grad_qv_bias,
        grad_proj_weight,
        grad_proj_bias,
        grad_ln2_gain,
        grad_ln2_bias,
        grad_fc_weight,
        grad_fc_bias,
        grad_out_weight,
        grad_out_bias,
    )
    shares = (
        lax.psum_scatter(
            local_grads[0].astype(jnp.bfloat16), "row", scatter_dimension=0, tiled=True
        ).astype(jnp.float32),
        lax.psum_scatter(
            local_grads[1].astype(jnp.bfloat16), "row", scatter_dimension=0, tiled=True
        ).astype(jnp.float32),
        lax.psum_scatter(
            local_grads[2].astype(jnp.bfloat16), "row", scatter_dimension=0, tiled=True
        ).astype(jnp.float32),
        lax.psum_scatter(
            local_grads[3].astype(jnp.bfloat16), "row", scatter_dimension=0, tiled=True
        ).astype(jnp.float32),
        lax.psum_scatter(
            local_grads[4].astype(jnp.bfloat16), "row", scatter_dimension=0, tiled=True
        ).astype(jnp.float32),
        lax.psum_scatter(
            local_grads[5].astype(jnp.bfloat16), "row", scatter_dimension=0, tiled=True
        ).astype(jnp.float32),
        lax.psum_scatter(
            local_grads[6].astype(jnp.bfloat16), "row", scatter_dimension=0, tiled=True
        ).astype(jnp.float32),
        lax.psum_scatter(
            local_grads[7].astype(jnp.bfloat16), "row", scatter_dimension=0, tiled=True
        ).astype(jnp.float32),
        lax.psum_scatter(
            local_grads[8].astype(jnp.bfloat16), "row", scatter_dimension=0, tiled=True
        ).astype(jnp.float32),
        lax.psum_scatter(
            local_grads[9].astype(jnp.bfloat16), "row", scatter_dimension=0, tiled=True
        ).astype(jnp.float32),
        lax.psum_scatter(
            local_grads[10].astype(jnp.bfloat16), "row", scatter_dimension=0, tiled=True
        ).astype(jnp.float32),
        lax.psum_scatter(
            local_grads[11].astype(jnp.bfloat16), "row", scatter_dimension=0, tiled=True
        ).astype(jnp.float32),
    )
    totals = (
        lax.psum(shares[0].astype(jnp.bfloat16), "seq").astype(jnp.float32),
        lax.psum(shares[1].astype(jnp.bfloat16), "seq").astype(jnp.float32),
        lax.psum(shares[2].astype(jnp.bfloat16), "seq").astype(jnp.float32),
        lax.psum(shares[3].astype(jnp.bfloat16), "seq").astype(jnp.float32),
        lax.psum(shares[4].astype(jnp.bfloat16), "seq").astype(jnp.float32),
        lax.psum(shares[5].astype(jnp.bfloat16), "seq").astype(jnp.float32),
        lax.psum(shares[6].astype(jnp.bfloat16), "seq").astype(jnp.float32),
        lax.psum(shares[7].astype(jnp.bfloat16), "seq").astype(jnp.float32),
        lax.psum(shares[8].astype(jnp.bfloat16), "seq").astype(jnp.float32),
        lax.psum(shares[9].astype(jnp.bfloat16), "seq").astype(jnp.float32),
        lax.psum(shares[10].astype(jnp.bfloat16), "seq").astype(jnp.float32),
        lax.psum(shares[11].astype(jnp.bfloat16), "seq").astype(jnp.float32),
    )
    summed = (
        lax.all_gather(totals[0].astype(jnp.bfloat16), "row", axis=0, tiled=True).astype(
            jnp.float32
        ),
        lax.all_gather(totals[1].astype(jnp.bfloat16), "row", axis=0, tiled=True).astype(
            jnp.float32
        ),
        lax.all_gather(totals[2].astype(jnp.bfloat16), "row", axis=0, tiled=True).astype(
            jnp.float32
        ),
        lax.all_gather(totals[3].astype(jnp.bfloat16), "row", axis=0, tiled=True).astype(
            jnp.float32
        ),
        lax.all_gather(totals[4].astype(jnp.bfloat16), "row", axis=0, tiled=True).astype(
            jnp.float32
        ),
        lax.all_gather(totals[5].astype(jnp.bfloat16), "row", axis=0, tiled=True).astype(
            jnp.float32
        ),
        lax.all_gather(totals[6].astype(jnp.bfloat16), "row", axis=0, tiled=True).astype(
            jnp.float32
        ),
        lax.all_gather(totals[7].astype(jnp.bfloat16), "row", axis=0, tiled=True).astype(
            jnp.float32
        ),
        lax.all_gather(totals[8].astype(jnp.bfloat16), "row", axis=0, tiled=True).astype(
            jnp.float32
        ),
        lax.all_gather(totals[9].astype(jnp.bfloat16), "row", axis=0, tiled=True).astype(
            jnp.float32
        ),
        lax.all_gather(totals[10].astype(jnp.bfloat16), "row", axis=0, tiled=True).astype(
            jnp.float32
        ),
        lax.all_gather(totals[11].astype(jnp.bfloat16), "row", axis=0, tiled=True).astype(
            jnp.float32
        ),
    )
    return (
        layer_out,
        input_grad,
        summed[0],
        summed[1],
        summed[2],
        summed[3],
        summed[4],
        summed[5],
        summed[6],
        summed[7],
        summed[8],
        summed[9],
        summed[10],
        summed[11],
    )


def solution(mesh):
    in_specs = (
        P("row", "seq", None),
        P("row", None),
        P(),
        P(),
        P(),
        P(),
        P(),
        P(),
        P(),
        P(),
        P(),
        P(),
        P(),
        P(),
        P("row", "seq", None),
    )
    out_specs = (
        P("row", "seq", None),
        P("row", "seq", None),
        P(),
        P(),
        P(),
        P(),
        P(),
        P(),
        P(),
        P(),
        P(),
        P(),
        P(),
        P(),
    )
    own_rows = mesh.shape["row"] == 8 and mesh.shape["seq"] == 4
    return jax.shard_map(by_rows if own_rows else local, mesh=mesh, in_specs=in_specs, out_specs=out_specs, check_vma=False)
```

```python
import functools

import jax
import jax.numpy as jnp
from jax import lax
from jax.experimental import pallas as pl
from jax.experimental.pallas import tpu as pltpu
from jax.sharding import PartitionSpec as P

HEAD = 64
branch_scale = 12.0 ** (-0.5)
masked_value = -1e30
norm_eps = 1e-05
F32, BF16 = jnp.float32, jnp.bfloat16
VMEM_LIMIT = 60 * 1024 * 1024


MESH = pl.DeviceIdType.MESH


class Place:
    def __init__(self):
        row, seq = lax.axis_index("row"), lax.axis_index("seq")
        self.row, self.seq = row, seq
        self.core, self.z = lax.rem(row, 2), lax.div(row, 2)
        self.x, self.y = lax.rem(seq, 2), lax.div(seq, 2)
        self.sibling = (row + 1 - 2 * self.core, seq)
        self.across_x = (row, seq + 1 - 2 * self.x)
        self.across_y = (row, seq + 2 - 4 * self.y)
        step_x, step_y = 1 - 2 * self.x, 2 - 4 * self.y
        self.first_bit = self.x + self.core * (self.y - self.x)
        self.second_bit = self.y + self.core * (self.x - self.y)
        self.first = (row, seq + step_x + self.core * (step_y - step_x))
        self.second = (row, seq + step_y + self.core * (step_x - step_y))

        self.next_z = (row + 2 - 4 * lax.rem(self.z, 2), seq)
        self.far_z = (row + 4 - 8 * lax.div(self.z, 2), seq)
        own = seq + self.core * (3 - 2 * seq)
        self.active = own < 3
        self.my_row = jnp.minimum(own, 2)

    def in_plane(self, hop):
        across_x, across_y = hop % 2, hop // 2
        x = self.x + across_x * (1 - 2 * self.x)
        y = self.y + across_y * (1 - 2 * self.y)
        seq = 2 * y + x
        return (self.row, seq), seq + self.core * (3 - 2 * seq)

    def greet_plane(self):
        barrier = pltpu.get_barrier_semaphore()
        for hop in (1, 2, 3):
            pl.semaphore_signal(barrier, inc=1, device_id=self.in_plane(hop)[0], device_id_type=MESH)
        pl.semaphore_wait(barrier, 3)

    def along_z(self, hop):
        return (2 * lax.rem(self.z + hop, 4) + self.core, self.seq)

    def greet(self):
        barrier = pltpu.get_barrier_semaphore()
        others = [self.sibling, self.across_x, self.across_y] + [self.along_z(hop) for hop in (1, 2, 3)]
        for other in others:
            pl.semaphore_signal(barrier, inc=1, device_id=other, device_id_type=MESH)
        pl.semaphore_wait(barrier, len(others))


def send(source, target, send_sem, recv_sem, device):
    return pltpu.make_async_remote_copy(
        src_ref=source, dst_ref=target, send_sem=send_sem, recv_sem=recv_sem,
        device_id=device, device_id_type=MESH,
    )


class SmallReducer:
    def __init__(self, place, sums, recv, line, send_sem, recv_sem):
        self.place, self.sums, self.recv, self.line = place, sums, recv, line
        self.send_sem, self.recv_sem = send_sem, recv_sem

    def copies(self, phase):
        place = self.place
        if phase < 3:
            other = (place.sibling, place.across_x, place.across_y)[phase]
            return [send(self.sums.at[phase], self.recv.at[phase], self.send_sem.at[phase], self.recv_sem.at[phase], other)]
        return [
            send(self.sums.at[3], self.line.at[place.z], self.send_sem.at[2 + hop], self.recv_sem.at[2 + hop], place.along_z(hop))
            for hop in (1, 2, 3)
        ]

    def step(self, phase):
        if phase > 0:
            for copy in self.copies(phase - 1):
                copy.wait()
        if 0 < phase < 4:
            self.sums[phase] = self.sums[phase - 1] + self.recv[phase - 1]
        if phase < 4:
            for copy in self.copies(phase):
                copy.start()
        if phase == 3:
            self.line[self.place.z] = self.sums[3]

    def total(self):
        return (self.line[0] + self.line[1]) + (self.line[2] + self.line[3])


def dot_nn(left, right):
    return lax.dot_general(left, right, (((1,), (0,)), ((), ())), preferred_element_type=F32)


def dot_nt(left, right):
    return lax.dot_general(left, right, (((1,), (1,)), ((), ())), preferred_element_type=F32)


def dot_tn(left, right):
    return lax.dot_general(left, right, (((0,), (0,)), ((), ())), preferred_element_type=F32)


def row_mean(values):
    return jnp.mean(values, axis=-1, keepdims=True)


def normalise(values):
    center = values - row_mean(values)
    inverse = lax.rsqrt(row_mean(center * center) + norm_eps)
    return center * inverse, inverse


def fill_bias(lens_ref, row, bias_ref, block):
    tokens = bias_ref.shape[0]
    ends, total = [], jnp.int32(0)
    for j in range(lens_ref.shape[1]):
        total = total + lens_ref[row, j]
        ends.append(total)
    query_pos = lax.broadcasted_iota(jnp.int32, (1, tokens), 1)
    query_seg = jnp.zeros((1, tokens), jnp.int32)
    for end in ends:
        query_seg = query_seg + (query_pos >= end).astype(jnp.int32)

    def one(i, carry):
        start = pl.multiple_of(i * block, block)
        key_pos = start + lax.broadcasted_iota(jnp.int32, (block, 1), 0)
        key_seg = jnp.zeros((block, 1), jnp.int32)
        for end in ends:
            key_seg = key_seg + (key_pos >= end).astype(jnp.int32)
        allowed = (key_pos <= query_pos) & (key_seg == query_seg)
        bias_ref[pl.ds(start, block), :] = jnp.where(allowed, 0.0, masked_value)
        return carry

    lax.fori_loop(0, tokens // block, one, 0)


def keep_column(lens_ref, row, start, block):
    total = jnp.int32(0)
    for j in range(lens_ref.shape[1]):
        total = total + lens_ref[row, j]
    pos = start + lax.broadcasted_iota(jnp.int32, (block, 1), 0)
    return (pos < total).astype(F32)


def head_row(h, value):
    lane = lax.broadcasted_iota(jnp.int32, (1, 2 * HEAD), 1)
    low = h % 2 * HEAD
    return jnp.where((lane >= low) & (lane < low + HEAD), value, 0.0).astype(BF16)


def front_kernel(
    lens_ref, tokens_ref, cot_in_ref, gain_ref, shift_ref, qv_bias_ref, wq_ref, wk_ref, wv_ref,
    q_ref, k_ref, v_ref, o_ref, lse_ref, x_ref, cot_ref,
    arrived, normed, bias, value_t, out_t, vectors, send_sem, recv_sem, copy_sem,
):
    tokens, width = x_ref.shape
    lanes = wq_ref.shape[1]
    block = tokens_ref.shape[1]
    blocks = tokens // block
    place = Place()
    mine = pl.ds(place.seq, 1)
    sources, targets = (tokens_ref, cot_in_ref), (arrived, cot_ref)

    def outgoing(which, hop):
        other, row = place.in_plane(hop)
        return row, send(
            sources[which].at[jnp.minimum(row, 2)], targets[which].at[place.seq],
            send_sem.at[which, hop - 1], recv_sem.at[which, hop - 1], other,
        )

    def local(which):
        return pltpu.make_async_copy(
            sources[which].at[place.my_row], targets[which].at[place.seq], copy_sem.at[which]
        )

    def start(which):
        for hop in (1, 2, 3):
            row, copy = outgoing(which, hop)
            pl.when(row < 3)(copy.start)
        pl.when(place.active)(local(which).start)

    def arrive(which, hop):
        if hop == 0:
            pl.when(place.active)(local(which).wait)
        else:
            pl.when(place.active)(outgoing(which, hop)[1].wait_recv)

    def leave(which):
        for hop in (1, 2, 3):
            row, copy = outgoing(which, hop)
            pl.when(row < 3)(copy.wait_send)

    @pl.when(pl.program_id(0) == 0)
    def _():
        place.greet_plane()
        start(0)
        vectors[0:1, :] = gain_ref[...].reshape(1, width)
        vectors[1:2, :] = shift_ref[...].reshape(1, width)
        for i in range(2):
            vectors[2 + i : 3 + i, :] = qv_bias_ref[i * width : (i + 1) * width].reshape(1, width)
        fill_bias(lens_ref, place.my_row, bias, block)

        @pl.when(jnp.logical_not(place.active))
        def _():
            arrived[...] = jnp.zeros_like(arrived)

        for hop in range(4):
            arrive(0, hop)
            if hop == 3:
                start(1)
            i = place.in_plane(hop)[0][1]
            rows = pl.ds(pl.multiple_of(i * block, block), block)
            x = arrived[i]
            x_ref[rows, :] = x
            unit, _ = normalise(x.astype(F32))
            normed[rows, :] = (unit * vectors[0:1, :] + vectors[1:2, :]).astype(BF16)
        leave(0)

    group = pl.ds(pl.multiple_of(pl.program_id(0) * lanes, lanes), lanes)

    def project(i, carry):
        rows = pl.ds(pl.multiple_of(i * block, block), block)
        h1 = normed[rows, :]
        q_ref[rows, :] = (dot_nn(h1, wq_ref[...]) + vectors[2:3, group]).astype(BF16)
        k_ref[rows, :] = dot_nn(h1, wk_ref[...]).astype(BF16)
        values = dot_nn(h1, wv_ref[...]) + vectors[3:4, group]
        v_ref[rows, :] = values.astype(BF16)
        value_t[:, rows] = values.T.astype(BF16)
        return carry

    lax.fori_loop(0, blocks, project, 0)

    heads = lanes // HEAD
    turns = [(i, h) for i in range(blocks) for h in range(heads)]

    def score(i, h):
        rows, count = slice(i * block, (i + 1) * block), (i + 1) * block
        pair = slice(h // 2 * 2 * HEAD, (h // 2 + 1) * 2 * HEAD)
        queries = q_ref[rows, pair] * head_row(h, HEAD ** (-0.5))
        return dot_nt(k_ref[:count, pair], queries) + bias[:count, rows]

    def mix(i, h, probs, total):
        rows, count = slice(i * block, (i + 1) * block), (i + 1) * block
        own = slice(h * HEAD, (h + 1) * HEAD)
        out_t[own, :] = dot_nn(value_t[own, :count], probs) * (1.0 / total)
        if h == heads - 1:
            o_ref[rows, :] = out_t[...].T.astype(BF16)

    following, waiting = score(*turns[0]), None
    for turn, (i, h) in enumerate(turns):
        scores = following
        if turn + 1 < len(turns):
            following = score(*turns[turn + 1])
        if waiting is not None:
            mix(*waiting)
        top = jnp.max(scores, axis=0, keepdims=True)
        probs = jnp.exp(scores - top)
        total = jnp.sum(probs, axis=0, keepdims=True)
        lse_ref[0, h : h + 1, i * block : (i + 1) * block] = top + jnp.log(total)
        waiting = (i, h, probs.astype(BF16), total)
    mix(*waiting)

    @pl.when(pl.program_id(0) == pl.num_programs(0) - 1)
    def _():
        for hop in range(4):
            arrive(1, hop)
        leave(1)

        @pl.when(jnp.logical_not(place.active))
        def _():
            copy = pltpu.make_async_copy(arrived, cot_ref, copy_sem.at[1])
            copy.start()
            copy.wait()


def front(lens, tokens_in, cotangent, gain, shift, qkv_weight, qv_bias):
    rows, span, width = tokens_in.shape
    spans = lax.axis_size("seq")
    tokens = spans * span
    lanes = width // 3
    groups = width // lanes
    heads = max(8, lanes // HEAD)
    whole = lambda shape: pl.BlockSpec(shape, lambda g: (0,) * len(shape))
    columns = lambda shape, first: pl.BlockSpec(shape, lambda g: (0, first + g))
    act = jax.ShapeDtypeStruct((tokens, width), BF16)
    sem = lambda *shape: pltpu.SemaphoreType.DMA(shape)
    return pl.pallas_call(
        front_kernel,
        grid=(groups,),
        out_shape=(
            act, act, act, act, jax.ShapeDtypeStruct((groups, heads, tokens), F32), act,
            jax.ShapeDtypeStruct((spans, span, width), BF16),
        ),
        in_specs=[
            pl.BlockSpec(memory_space=pltpu.SMEM),
            pl.BlockSpec(memory_space=pl.ANY),
            pl.BlockSpec(memory_space=pl.ANY),
            whole((width,)),
            whole((width,)),
            whole((2 * width,)),
            columns((width, lanes), 0),
            columns((width, lanes), groups),
            columns((width, lanes), 2 * groups),
        ],
        out_specs=[columns((tokens, lanes), 0)] * 4
        + [
            pl.BlockSpec((1, heads, tokens), lambda g: (g, 0, 0)),
            whole((tokens, width)),
            pl.BlockSpec(memory_space=pl.ANY),
        ],
        scratch_shapes=[
            pltpu.VMEM((spans, span, width), BF16),
            pltpu.VMEM((tokens, width), BF16),
            pltpu.VMEM((tokens, tokens), F32),
            pltpu.VMEM((lanes, tokens), BF16),
            pltpu.VMEM((lanes, span), F32),
            pltpu.VMEM((8, width), F32),
            sem(2, 3), sem(2, 3), sem(2),
        ],
        compiler_params=pltpu.CompilerParams(
            collective_id=1, has_side_effects=True, vmem_limit_bytes=VMEM_LIMIT
        ),
        name="front",
    )(lens, tokens_in, cotangent, gain, shift, qv_bias, qkv_weight, qkv_weight, qkv_weight)


class Units:
    def __init__(self, place, fresh, out, recv0, recv1, recv2, recv3, recv4, part, send_sem, recv_sem, copy_sem):
        self.place, self.fresh, self.out, self.part = place, fresh, out, part
        self.recv = (recv0, recv1, recv2, recv3, recv4)
        self.send_sem, self.recv_sem, self.copy_sem = send_sem, recv_sem, copy_sem
        _, rows, columns = fresh.shape
        self.size = (rows // 2, rows // 4, rows // 8, rows // 16)
        self.wide = columns // 2
        self.bits = (place.core, place.first_bit, lax.rem(place.z, 2), lax.div(place.z, 2), place.second_bit)
        self.partners = (place.sibling, place.first, place.next_z, place.far_z, place.second)

    @staticmethod
    def scratch(count, n, rows, columns):
        vmem = lambda *shape: pltpu.VMEM((count, n, *shape), BF16)
        sem = pltpu.SemaphoreType.DMA
        return [vmem(rows // 2 ** k, columns) for k in range(1, 5)] + [
            vmem(rows // 16, columns // 2), vmem(rows // 16, columns // 2),
            sem((count, 10)), sem((count, 10)), sem((count,)),
        ]

    def part_of(self, stage, bit):
        if stage == 4:
            return slice(None), pl.ds(pl.multiple_of(bit * self.wide, self.wide), self.wide)
        size = self.size[stage]
        return pl.ds(pl.multiple_of(bit * size, size), size), slice(None)

    def region(self, stage):
        start = sum(bit * size for bit, size in zip(self.bits[: min(stage, 3) + 1], self.size))
        size = self.size[min(stage, 3)]
        rows = pl.ds(pl.multiple_of(start, size), size)
        return rows, self.part_of(4, self.bits[4])[1] if stage == 4 else slice(None)

    def copy(self, phase, u):
        sems = self.send_sem.at[u, phase], self.recv_sem.at[u, phase]
        if phase < 5:
            source = self.fresh if phase == 0 else self.recv[phase - 1].at[u]
            source = source.at[:, *self.part_of(phase, 1 - self.bits[phase])]
            return send(source, self.recv[phase].at[u], *sems, self.partners[phase])
        where = self.out.at[u, :, *self.region(9 - phase)]
        return send(self.part.at[u] if phase == 5 else where, where, *sems, self.partners[9 - phase])

    def local(self, u):
        return pltpu.make_async_copy(self.part.at[u], self.out.at[u, :, *self.region(4)], self.copy_sem.at[u])

    def add(self, phase, u):
        source = self.fresh if phase == 0 else self.recv[phase - 1].at[u]
        target = self.recv[phase].at[u]
        step = self.size[3]
        if phase == 4:
            own = source[:, :, self.part_of(4, self.bits[4])[1]].astype(F32)
            self.part[u] = (own + target[...].astype(F32)).astype(BF16)
            return

        def one(i, carry):
            here = pl.ds(pl.multiple_of(i * step, step), step)
            there = pl.ds(pl.multiple_of(self.bits[phase] * self.size[phase] + i * step, step), step)
            for panel in range(self.fresh.shape[0]):
                total = source[panel, there, :].astype(F32) + target[panel, here, :].astype(F32)
                target[panel, here, :] = total.astype(BF16)
            return carry

        lax.fori_loop(0, self.size[phase] // step, one, 0)

    def step(self, phase, u):
        if phase > 0:
            self.copy(phase - 1, u).wait()
            if phase == 6:
                self.local(u).wait()
        if 0 < phase < 6:
            self.add(phase - 1, u)
        if phase < 10:
            self.copy(phase, u).start()
        if phase == 5:
            self.local(u).start()


class Exchange:
    def __init__(self, place, source, target, send_sem, recv_sem, copy_sem):
        self.place, self.source, self.target = place, source, target
        self.send_sem, self.recv_sem, self.copy_sem = send_sem, recv_sem, copy_sem
        self.span = target.shape[1]

    def block(self, seq):
        return self.source.at[pl.ds(pl.multiple_of(seq * self.span, self.span), self.span)]

    def outgoing(self, hop):
        other, row = self.place.in_plane(hop)
        return row, send(
            self.block(other[1]), self.target.at[self.place.my_row],
            self.send_sem.at[hop - 1], self.recv_sem.at[hop - 1], other,
        )

    def local(self):
        return pltpu.make_async_copy(self.block(self.place.seq), self.target.at[self.place.my_row], self.copy_sem)

    def start(self, hop):
        pl.when(self.place.active)(self.outgoing(hop)[1].start)
        if hop == 3:
            pl.when(self.place.active)(self.local().start)

    def finish(self):
        for hop in (1, 2, 3):
            row, copy = self.outgoing(hop)
            pl.when(self.place.active)(copy.wait_send)
            pl.when(row < 3)(copy.wait_recv)
        pl.when(self.place.active)(self.local().wait)


def plan(hooks, sizes, made):
    free = {"core": 0.0, "plane": 0.0, "near": 0.0, "far": 0.0}
    delay = {"core": 1.5, "plane": 3.5, "near": 3.0, "far": 3.5}
    now, flight, plans, spare = 0.0, {}, {}, []
    small = len(sizes)

    def go(unit, phase):
        nonlocal now
        now += 0.3
        if phase == (4 if unit == small else 10):
            del flight[unit]
            return
        if unit == small:
            kind, time = ("core", "plane", "plane", "far")[phase], 0.3
        else:
            stage = min(phase, 9 - phase)
            kind = ("core", "plane", "near", "far", "plane")[stage]
            time = sizes[unit] * (0.5 / 0.6, 0.25 / 0.094, 0.25 / 0.094, 0.25 / 0.094, 0.03125 / 0.094)[stage]
        begin = max(now, free[kind])
        free[kind] = begin + time
        if kind == "far":
            free["near"] = max(now, free["near"]) + time / 2
        flight[unit] = (phase, begin + time + delay[kind])

    def fill(items):
        if spare and free["plane"] <= now + 4.0:
            free["plane"] = now + 5.3
            items.append(spare.pop(0))

    for name, compute in hooks:
        now += compute
        items = plans[name] = []
        for unit in sorted(flight, key=lambda u: flight[u][1]):
            phase, end = flight[unit]
            if end <= now + 0.5:
                items.append((unit, phase + 1))
                go(unit, phase + 1)
        for unit, hook in made.items():
            if hook == name:
                items.append((unit, 0))
                go(unit, 0)
        if name in ("lo", "dx"):
            spare += [(name, hop) for hop in (3, 2, 1)]
        fill(items)
    tail = [(small, 0)]
    go(small, 0)
    while flight:
        unit = min(flight, key=lambda u: flight[u][1])
        phase, end = flight[unit]
        now = max(now, end)
        tail.append((unit, phase + 1))
        go(unit, phase + 1)
        fill(tail)
    return plans, tail + spare, max(now, free["plane"] + 3.5)


def timetable(steps, groups):
    hooks = []
    for s in range(steps):
        hooks += [(("early", s), 18.0 if s == 0 else 3.0), (("late", s), 3.0), (("fed", s), 2.6)]
    hooks += [("lo", 7.0), ("proj", 1.5), ("turn", 3.0)]
    for s in range(steps, steps + groups):
        hooks += [(("low", s), 6.0 + 1.2 * (s > steps)), (("high", s), 4.0), (("made", s), 1.8)]
    hooks.append(("dx", 4.2))
    made = {s: ("fed", s) for s in range(steps)}
    made[steps] = "proj"
    made.update({steps + 1 + g: ("made", steps + g) for g in range(groups)})
    return hooks, made


def body_kernel(
    steps, groups,
    lens_ref, o_ref, x_ref, cot_ref, wp_ref, bp_ref, gain2_ref, shift2_ref, wf_ref, bf_ref, wo_ref, bo_ref,
    gain1_ref, shift1_ref, q_ref, k_ref, v_ref, lse_ref, wq_ref, wk_ref, wv_ref,
    lo_out, dx_out, feed_out, rest_out, small_out,
    middle, normed, normed_t, cot_low, out_acc, back_acc, hidden, back_low, bias, key_t, grad_q_t, delta, vectors,
    fresh_feed, fresh_rest, sums, small_recv, line_sums,
    small_send, small_recv_sem, out_send, out_recv, out_copy, *unit_scratch,
):
    tokens, width = x_ref.shape
    lanes = wq_ref.shape[1]
    span = lo_out.shape[1]
    blocks = tokens // span
    step = pl.program_id(0)
    place = Place()
    acc = sums.at[0]

    sets = [
        Units(place, fresh_feed, feed_out, *unit_scratch[:9]), Units(place, fresh_rest, rest_out, *unit_scratch[9:])
    ]
    small = SmallReducer(place, sums, small_recv, line_sums, small_send, small_recv_sem)
    lo_back = Exchange(place, normed, lo_out, out_send.at[0], out_recv.at[0], out_copy.at[0])
    dx_back = Exchange(place, cot_low, dx_out, out_send.at[1], out_recv.at[1], out_copy.at[1])
    exchanges = {"lo": lo_back, "dx": dx_back}

    hooks, made = timetable(steps, groups)
    panel = width * width * 2e-6
    count = steps + 1 + groups
    plans, tail, _ = plan(hooks, [2 * panel] * steps + [panel] * (1 + groups), made)
    order = [name for name, _ in hooks]
    freed = {u: order.index(name) for name, items in plans.items() for u, phase in items if phase == 1}
    for u in [*range(steps - 1), *range(steps, steps + groups)]:
        assert freed[u] < order.index(made[u + 1])

    def chosen(pairs, index):
        value, found = jnp.int32(0), jnp.int32(0)
        for key, item in pairs:
            hit = (index == key).astype(jnp.int32)
            value, found = value + hit * item, found + hit
        return value, found > 0

    def start(item, index=None):
        u, phase = item
        if u in exchanges:
            return functools.partial(exchanges[u].start, phase)
        if u == count:
            return functools.partial(small.step, phase)
        return functools.partial(sets[u >= steps].step, phase, number(item) if index is None else index)

    def kind(item):
        u, phase = item
        return (u if u in exchanges or u == count else int(u >= steps)), phase

    def number(item):
        u = item[0]
        return 0 if u in exchanges or u == count else u - steps * (u >= steps)

    def hook(name):
        if name in plans:
            for item in plans[name]:
                start(item)()
            return
        bodies = {}
        for s in range(steps + groups):
            seen = {}
            for item in plans.get((name, s), []):
                turn = seen[kind(item)] = seen.get(kind(item), -1) + 1
                bodies.setdefault((kind(item), turn), []).append((s, item))
        for _, pairs in sorted(bodies.items(), key=lambda body: -body[0][0][1]):
            index, found = chosen([(s, number(item)) for s, item in pairs], step)
            pl.when(found)(start(pairs[0][1], index))

    def each(body, first=0, last=blocks):
        def run(i, carry):
            start = pl.multiple_of(i * span, span)
            body(start, pl.ds(start, span))
            return carry

        lax.fori_loop(first, last, run, 0)

    def column_sum(values):
        return jnp.sum(values, axis=0, keepdims=True)

    @pl.when(step == 0)
    def _():
        place.greet()
        acc[...] = jnp.zeros_like(acc)
        for i, ref in enumerate((bp_ref, gain2_ref, shift2_ref, bo_ref, gain1_ref, shift1_ref)):
            vectors[i : i + 1, :] = ref[...].reshape(1, width)
        for f in range(steps):
            vectors[8 + f : 9 + f, :] = bf_ref[f * width : (f + 1) * width].reshape(1, width)

        def begin(start, rows):
            attn = dot_nn(o_ref[rows, :], wp_ref[...]) + vectors[0:1, :]
            mid = x_ref[rows, :].astype(F32) + branch_scale * attn
            middle[rows, :] = mid
            unit, _ = normalise(mid)
            h2 = unit * vectors[1:2, :] + vectors[2:3, :]
            normed[rows, :] = h2.astype(BF16)
            keep = keep_column(lens_ref, place.my_row, start, span)
            low = (branch_scale * (keep * cot_ref[rows, :].astype(F32))).astype(BF16)
            cot_low[rows, :] = low
            acc[4:5, :] += column_sum(low.astype(F32))
            out_acc[rows, :] = jnp.zeros((span, width), F32)
            back_acc[rows, :] = jnp.zeros((span, width), F32)

        each(begin)

    @pl.when(step < steps)
    def _():
        def chunk(start, rows):
            pre = dot_nn(normed[rows, :], wf_ref[...]) + vectors[pl.ds(8 + step, 1), :]
            back = dot_nt(cot_low[rows, :], wo_ref[...])
            square = pre * pre
            root = (2.0 / jnp.pi) ** 0.5
            bend = jnp.tanh(pre * (root + (root * 0.044715) * square))
            half = 0.5 * pre
            hid = (half + half * bend).astype(BF16)
            slope = (0.5 + 0.5 * bend) + half * (1.0 - bend * bend) * (root + (3.0 * root * 0.044715) * square)
            grad = (back * slope).astype(BF16)
            hidden[rows, :] = hid
            back_low[rows, :] = grad
            acc[pl.ds(8 + step, 1), :] += column_sum(grad.astype(F32))
            out_acc[rows, :] += dot_nn(hid, wo_ref[...])
            back_acc[rows, :] += dot_nt(grad, wf_ref[...])

        each(chunk, 0, blocks // 2)
        hook("early")
        each(chunk, blocks // 2, blocks)
        hook("late")
        fresh_feed[0] = dot_tn(hidden[...], cot_low[...]).astype(BF16)
        fresh_feed[1] = dot_tn(normed[...], back_low[...]).astype(BF16)
        hook("fed")

    @pl.when(step == steps - 1)
    def _():
        def end(start, rows):
            keep = keep_column(lens_ref, place.my_row, start, span)
            mid = middle[rows, :]
            normed[rows, :] = (
                keep * (mid + branch_scale * (out_acc[rows, :] + vectors[3:4, :]))
            ).astype(BF16)
            unit, inverse = normalise(mid)
            back = back_acc[rows, :]
            back_acc[rows, :] = jnp.zeros((span, width), F32)
            acc[5:6, :] += column_sum(back * unit)
            acc[6:7, :] += column_sum(back)
            scaled = back * vectors[1:2, :]
            grad = keep * cot_ref[rows, :].astype(F32) + inverse * (
                scaled - row_mean(scaled) - unit * row_mean(scaled * unit)
            )
            middle[rows, :] = grad
            low = (branch_scale * grad).astype(BF16)
            hidden[rows, :] = low
            acc[7:8, :] += column_sum(low.astype(F32))
            back_low[rows, :] = dot_nt(low, wp_ref[...]).astype(BF16)

        each(end)
        hook("lo")
        fresh_rest[0] = dot_tn(o_ref[...], hidden[...]).astype(BF16)
        hook("proj")

    @pl.when(step == steps)
    def _():
        fill_bias(lens_ref, place.my_row, bias, span)

        def turn(start, rows):
            unit, _ = normalise(x_ref[rows, :].astype(F32))
            normed_t[:, rows] = (unit * vectors[4:5, :] + vectors[5:6, :]).T.astype(BF16)

        each(turn)
        hook("turn")

    @pl.when(step >= steps)
    def _():
        group = pl.ds(pl.multiple_of((step - steps) * lanes, lanes), lanes)
        grad_k, grad_v = out_acc.at[:, :lanes], out_acc.at[:, lanes : 2 * lanes]
        grad_q, d_out = hidden.at[:, :lanes], hidden.at[:, lanes : 2 * lanes]
        grad_k[...] = jnp.zeros_like(grad_k)
        grad_v[...] = jnp.zeros_like(grad_v)
        grad_q_t[...] = jnp.zeros_like(grad_q_t)
        key_t[...] = k_ref[...].astype(F32).T.astype(BF16)
        head_id = lax.broadcasted_iota(jnp.int32, (8, lanes), 0)
        lane_id = lax.broadcasted_iota(jnp.int32, (8, lanes), 1)
        member = ((lane_id >= head_id * HEAD) & (lane_id < (head_id + 1) * HEAD)).astype(F32)

        def prepare(start, rows):
            grads = back_low[rows, group]
            d_out[rows, :] = grads
            product = grads.astype(F32) * o_ref[rows, group].astype(F32)
            delta[:, rows] = lax.dot_general(
                member, product, (((1,), (1,)), ((), ())),
                precision=lax.Precision.HIGHEST, preferred_element_type=F32,
            )

        each(prepare)
        heads = lanes // HEAD

        def tile(t, carry):
            i = sum((t >= b * (b + 1) // 2).astype(jnp.int32) for b in range(1, blocks))
            first = pl.multiple_of(i * span, span)
            key_first = pl.multiple_of((t - lax.div(i * (i + 1), 2)) * span, span)
            rows, keys = pl.ds(first, span), pl.ds(key_first, span)
            mask = bias[keys, rows]

            def start(h):
                pair = slice(h // 2 * 2 * HEAD, (h // 2 + 1) * 2 * HEAD)
                queries = q_ref[rows, pair] * head_row(h, HEAD ** (-0.5))
                grads = d_out[rows, pair] * head_row(h, 1.0)
                return queries, grads, dot_nt(k_ref[keys, pair], queries) + mask, dot_nt(v_ref[keys, pair], grads)

            following = start(0)
            for h in range(heads):
                pair = slice(h // 2 * 2 * HEAD, (h // 2 + 1) * 2 * HEAD)
                own = slice(h * HEAD, (h + 1) * HEAD)
                queries, grads, scores, grad_probs = following
                if h + 1 < heads:
                    following = start(h + 1)
                probs = jnp.exp(scores - lse_ref[0, h : h + 1, rows])
                grad_scores = (probs * (grad_probs - delta[h : h + 1, rows])).astype(BF16)
                grad_v[keys, pair] += dot_nn(probs.astype(BF16), grads)
                grad_k[keys, pair] += dot_nn(grad_scores, queries)
                grad_q_t[own, rows] += dot_nn(key_t[own, keys], grad_scores)
            return carry

        tiles = blocks * (blocks + 1) // 2
        lax.fori_loop(0, tiles - blocks, tile, 0)
        hook("low")
        lax.fori_loop(tiles - blocks, tiles, tile, 0)
        hook("high")

        def close(start, rows):
            dq = (grad_q_t[:, rows].T * HEAD ** (-0.5)).astype(BF16)
            grad_q[rows, :] = dq
            acc[2:3, group] += column_sum(dq.astype(F32))
            acc[3:4, group] += column_sum(grad_v[rows, :].astype(BF16).astype(F32))

        each(close)
        for p, grad in enumerate((grad_q, grad_k, grad_v)):
            fresh_rest[0, :, p * lanes : (p + 1) * lanes] = dot_nn(normed_t[...], grad[...].astype(BF16)).astype(BF16)
        hook("made")

        def pull(start, rows):
            back_acc[rows, :] += (
                dot_nt(grad_q[rows, :], wq_ref[...])
                + dot_nt(grad_k[rows, :].astype(BF16), wk_ref[...])
                + dot_nt(grad_v[rows, :].astype(BF16), wv_ref[...])
            )

        each(pull)

    @pl.when(step == steps + groups - 1)
    def _():
        def last(start, rows):
            unit, inverse = normalise(x_ref[rows, :].astype(F32))
            back = back_acc[rows, :]
            acc[0:1, :] += column_sum(back * unit)
            acc[1:2, :] += column_sum(back)
            scaled = back * vectors[4:5, :]
            grad = middle[rows, :] + inverse * (
                scaled - row_mean(scaled) - unit * row_mean(scaled * unit)
            )
            cot_low[rows, :] = grad.astype(BF16)

        each(last)
        hook("dx")
        kinds = sorted({kind(item) for item in tail}, key=str)
        codes = [(t, kinds.index(kind(item)) * count + number(item)) for t, item in enumerate(tail)]

        def turn(t, carry):
            code, _ = chosen(codes, t)
            which, index = lax.div(code, count), lax.rem(code, count)
            for k, this in enumerate(kinds):
                item = next(item for item in tail if kind(item) == this)
                pl.when(which == k)(start(item, index))
            return carry

        lax.fori_loop(0, len(tail), turn, 0)
        small_out[...] = small.total()
        lo_back.finish()
        dx_back.finish()


def body(
    lens, o, x, cot, q, k, v, lse, rows, span,
    ln1_gain, ln1_bias, qkv_weight, proj_weight, proj_bias, ln2_gain, ln2_bias, fc_weight, fc_bias, out_weight, out_bias,
):
    tokens, width = x.shape
    groups, heads, _ = lse.shape
    lanes = width // groups
    steps = fc_weight.shape[1] // width
    shape = jax.ShapeDtypeStruct
    once = pl.Buffered(1)
    whole = lambda *dims: pl.BlockSpec(dims, lambda s: (0,) * len(dims), pipeline_mode=once)
    act, vec, mat = whole(tokens, width), whole(width), whole(width, width)
    feed_step = lambda s: jnp.minimum(s, steps - 1)
    back_step = lambda s: jnp.maximum(s - steps, 0)
    columns = lambda dims, first: pl.BlockSpec(dims, lambda s: (0, first + back_step(s)))
    anywhere = pl.BlockSpec(memory_space=pl.ANY)
    f32 = lambda *dims: pltpu.VMEM(dims, F32)
    bf16 = lambda *dims: pltpu.VMEM(dims, BF16)
    sem = lambda *dims: pltpu.SemaphoreType.DMA(dims)
    return pl.pallas_call(
        functools.partial(body_kernel, steps, groups),
        grid=(steps + groups,),
        out_shape=(
            shape((rows, span, width), BF16),
            shape((rows, span, width), BF16),
            shape((steps, 2, width, width), BF16),
            shape((1 + groups, 1, width, width), BF16),
            shape((16, width), F32),
        ),
        in_specs=[
            pl.BlockSpec(memory_space=pltpu.SMEM),
            act, act, act, mat, vec, vec, vec,
            pl.BlockSpec((width, width), lambda s: (0, feed_step(s))),
            whole(steps * width),
            pl.BlockSpec((width, width), lambda s: (feed_step(s), 0)),
            vec, vec, vec,
            columns((tokens, lanes), 0), columns((tokens, lanes), 0), columns((tokens, lanes), 0),
            pl.BlockSpec((1, heads, tokens), lambda s: (back_step(s), 0, 0)),
            columns((width, lanes), 0), columns((width, lanes), groups), columns((width, lanes), 2 * groups),
        ],
        out_specs=[anywhere] * 4 + [pl.BlockSpec((16, width), lambda s: (0, 0))],
        scratch_shapes=[
            f32(tokens, width), bf16(tokens, width), bf16(width, tokens), bf16(tokens, width),
            f32(tokens, width), f32(tokens, width), bf16(tokens, width), bf16(tokens, width),
            f32(tokens, tokens), bf16(lanes, tokens), f32(lanes, tokens), f32(8, tokens), f32(16, width),
            bf16(2, width, width), bf16(1, width, width), f32(4, 16, width), f32(3, 16, width), f32(4, 16, width),
            sem(6), sem(6), sem(2, 3), sem(2, 3), sem(2),
            *Units.scratch(steps, 2, width, width), *Units.scratch(1 + groups, 1, width, width),
        ],
        compiler_params=pltpu.CompilerParams(
            collective_id=0, has_side_effects=True, vmem_limit_bytes=VMEM_LIMIT
        ),
        name="body",
    )(
        lens, o, x, cot, proj_weight, proj_bias, ln2_gain, ln2_bias, fc_weight, fc_bias, out_weight, out_bias,
        ln1_gain, ln1_bias, q, k, v, lse, qkv_weight, qkv_weight, qkv_weight,
    )


def finish_kernel(
    feed_ref, proj_ref, qkv_ref, small_ref, dx_ref,
    ln1_gain, ln1_bias, qkv_weight, qv_bias, proj_weight, proj_bias,
    ln2_gain, ln2_bias, fc_weight, fc_bias, out_weight, out_bias, input_grad,
):
    width = small_ref.shape[1]
    lanes = qkv_ref.shape[3]
    groups = width // lanes
    out_weight[...] = feed_ref[0, 0].astype(F32)
    fc_weight[...] = feed_ref[0, 1].astype(F32)
    for g in range(groups):
        qkv_weight[:, g * lanes : (g + 1) * lanes] = qkv_ref[1 + g, 0].astype(F32)
    proj_weight[...] = proj_ref[0, 0].astype(F32)
    input_grad[...] = dx_ref[...].astype(F32)

    @pl.when((pl.program_id(0) == 0) & (pl.program_id(1) == 0))
    def _():
        for ref, first in (
            (ln1_gain, 0), (ln1_bias, 1), (qv_bias, 2), (out_bias, 4),
            (ln2_gain, 5), (ln2_bias, 6), (proj_bias, 7), (fc_bias, 8),
        ):
            for i in range(ref.shape[0] // width):
                ref[i * width : (i + 1) * width] = small_ref[first + i]


def finish(feed_sums, rest_sums, small, dx):
    steps, _, width, _ = feed_sums.shape
    groups = rest_sums.shape[0] - 1
    lanes = width // groups
    rows, span, _ = dx.shape
    cuts = 1
    half = width // cuts
    shape = lambda *dims: jax.ShapeDtypeStruct(dims, F32)
    flat = lambda n: pl.BlockSpec((n * width,), lambda f, r: (0,))
    third = lambda f: jnp.minimum(f, 2)
    row = pl.BlockSpec((1, span // cuts, width), lambda f, r: (jnp.minimum(f, rows - 1), jnp.where(f > rows - 1, cuts - 1, r), 0))
    return pl.pallas_call(
        finish_kernel,
        grid=(steps, cuts),
        out_shape=(
            shape(width), shape(width), shape(width, 3 * width), shape(2 * width),
            shape(width, width), shape(width), shape(width), shape(width),
            shape(width, steps * width), shape(steps * width), shape(steps * width, width), shape(width),
            shape(rows, span, width),
        ),
        in_specs=[
            pl.BlockSpec((1, 2, half, width), lambda f, r: (f, 0, r, 0)),
            pl.BlockSpec((1, 1, half, width), lambda f, r: (0, 0, jnp.where(f == steps - 1, r, 0), 0)),
            pl.BlockSpec((1 + groups, 1, half, lanes), lambda f, r: (0, 0, jnp.where(f > 2, cuts - 1, r), third(f))),
            pl.BlockSpec((16, width), lambda f, r: (0, 0)),
            row,
        ],
        out_specs=[
            flat(1), flat(1),
            pl.BlockSpec((half, width), lambda f, r: (jnp.where(f > 2, cuts - 1, r), third(f))),
            flat(2),
            pl.BlockSpec((half, width), lambda f, r: (jnp.where(f == steps - 1, r, 0), 0)),
            flat(1), flat(1), flat(1),
            pl.BlockSpec((half, width), lambda f, r: (r, f)),
            flat(steps),
            pl.BlockSpec((half, width), lambda f, r: (cuts * f + r, 0)),
            flat(1),
            row,
        ],
        compiler_params=pltpu.CompilerParams(vmem_limit_bytes=VMEM_LIMIT),
        name="finish",
    )(feed_sums, rest_sums, rest_sums, small, dx)


def by_rows(
    tokens_in, lengths, ln1_gain, ln1_bias, qkv_weight, qv_bias, proj_weight, proj_bias,
    ln2_gain, ln2_bias, fc_weight, fc_bias, out_weight, out_bias, cotangent,
):
    rows, span, width = tokens_in.shape
    q, k, v, o, lse, x, cot = front(
        lengths, tokens_in, cotangent, ln1_gain, ln1_bias, qkv_weight, qv_bias
    )
    layer_out, dx, feed_sums, rest_sums, small = body(
        lengths, o, x, cot.reshape(x.shape), q, k, v, lse, rows, span,
        ln1_gain, ln1_bias, qkv_weight, proj_weight, proj_bias, ln2_gain, ln2_bias,
        fc_weight, fc_bias, out_weight, out_bias,
    )
    *grads, input_grad = finish(feed_sums, rest_sums, small, dx)
    return (layer_out, input_grad, *grads)


def layer_norm(values, gain, shift):
    center = values - jnp.mean(values, axis=-1, keepdims=True)
    spread = jnp.mean(center * center, axis=-1, keepdims=True)
    return center * lax.rsqrt(spread + norm_eps) * gain + shift


def gelu_tanh(values):
    return jax.nn.gelu(values, approximate=True)


def left_dot(left, right):
    return lax.dot_general(
        left, right, (((0,), (0,)), ((), ())), preferred_element_type=jnp.float32
    )


def right_dot(left, right):
    return lax.dot_general(
        left, right, (((1,), (1,)), ((), ())), preferred_element_type=jnp.float32
    )


def allowed_mask(query_pos, query_seg, key_pos, key_seg):
    return (key_pos[None, None, :] <= query_pos[None, :, None]) & (
        key_seg[:, None, :] == query_seg[:, :, None]
    )


def local(
    tokens_in,
    lengths,
    ln1_gain,
    ln1_bias,
    qkv_weight,
    qv_bias,
    proj_weight,
    proj_bias,
    ln2_gain,
    ln2_bias,
    fc_weight,
    fc_bias,
    out_weight,
    out_bias,
    cotangent,
):
    row_count, span_len, model_width = tokens_in.shape
    head_count = model_width // HEAD
    scale = HEAD ** (-0.5)
    seq_parts = lax.axis_size("seq")
    row_len = span_len * seq_parts
    first_pos = lax.axis_index("seq") * span_len
    doc_count = lengths.shape[1]
    positions = jnp.arange(row_len, dtype=jnp.int32)
    ends = jnp.cumsum(lengths, axis=1)
    segments = jnp.sum((positions[None, :, None] >= ends[:, None, :]).astype(jnp.int32), axis=2)
    my_segs = lax.dynamic_slice_in_dim(segments, first_pos, span_len, 1)
    my_pos = first_pos + jnp.arange(span_len, dtype=jnp.int32)
    token_count = row_count * span_len
    keep_flat = (my_segs < doc_count).astype(jnp.float32).reshape(token_count, 1)
    inputs = tokens_in.astype(jnp.float32).reshape(token_count, model_width)
    normed = layer_norm(inputs, ln1_gain, ln1_bias)
    normed_low = normed.astype(jnp.bfloat16)
    bias_full = jnp.concatenate(
        [qv_bias[:model_width], jnp.zeros((model_width,), jnp.float32), qv_bias[model_width:]]
    )
    projected = (
        jnp.dot(normed_low, qkv_weight, preferred_element_type=jnp.float32) + bias_full
    ).astype(jnp.bfloat16)
    projected = projected.reshape(row_count, span_len, 3 * model_width)
    queries = projected[..., :model_width]
    keys = projected[..., model_width : 2 * model_width]
    values = projected[..., 2 * model_width :]
    query_heads = queries.reshape(row_count, span_len, head_count, HEAD)
    key_heads = keys.reshape(row_count, span_len, head_count, HEAD)
    value_heads = values.reshape(row_count, span_len, head_count, HEAD)
    last_pos = first_pos + span_len - 1
    start_state = (
        jnp.full((row_count, head_count, span_len), masked_value, jnp.float32),
        jnp.zeros((row_count, head_count, span_len), jnp.float32),
        jnp.zeros((row_count, span_len, model_width), jnp.float32),
    )
    key_piece = lax.all_gather(keys, "seq", axis=1, tiled=True)
    value_piece = lax.all_gather(values, "seq", axis=1, tiled=True)
    count = key_piece.shape[1]

    def forward_update(state):
        top, total, accum = state
        piece_keys = key_piece.reshape(row_count, count, head_count, HEAD)
        piece_values = value_piece.reshape(row_count, count, head_count, HEAD)
        scores = (
            jnp.einsum(
                "rqhd,rkhd->rhqk", query_heads, piece_keys, preferred_element_type=jnp.float32
            )
            * scale
        )
        key_pos = jnp.arange(count, dtype=jnp.int32)
        allowed = allowed_mask(my_pos, my_segs, key_pos, segments)[:, None]
        scores = jnp.where(allowed, scores, masked_value)
        new_top = jnp.maximum(top, jnp.max(scores, axis=-1))
        weights = jnp.where(allowed, jnp.exp(scores - new_top[..., None]), 0.0)
        total = jnp.sum(weights, axis=-1)
        added = jnp.einsum(
            "rhqk,rkhd->rqhd",
            weights.astype(jnp.bfloat16),
            piece_values,
            preferred_element_type=jnp.float32,
        )
        accum = added.reshape(row_count, span_len, model_width)
        return (new_top, total, accum)

    top, total, accum = lax.cond(
        jnp.int32(0) > last_pos, lambda state: state, forward_update, start_state
    )
    log_total = top + jnp.log(total)
    attended_heads = (
        accum.reshape(row_count, span_len, head_count, HEAD) / total.transpose(0, 2, 1)[..., None]
    )
    attended = attended_heads.reshape(token_count, model_width)
    attended_low = attended.astype(jnp.bfloat16)
    attn_out = jnp.dot(attended_low, proj_weight, preferred_element_type=jnp.float32) + proj_bias
    middle = inputs + branch_scale * attn_out
    normed_two = layer_norm(middle, ln2_gain, ln2_bias)
    normed_two_low = normed_two.astype(jnp.bfloat16)
    hidden_pre = jnp.dot(normed_two_low, fc_weight, preferred_element_type=jnp.float32) + fc_bias
    hidden_low = gelu_tanh(hidden_pre).astype(jnp.bfloat16)
    branch_out = jnp.dot(hidden_low, out_weight, preferred_element_type=jnp.float32) + out_bias
    layer_out = (
        ((middle + branch_scale * branch_out) * keep_flat)
        .astype(jnp.bfloat16)
        .reshape(row_count, span_len, model_width)
    )
    grad_final = keep_flat * cotangent.astype(jnp.float32).reshape(token_count, model_width)
    grad_branch = (branch_scale * grad_final).astype(jnp.bfloat16)
    grad_out_weight = left_dot(hidden_low, grad_branch)
    grad_out_bias = jnp.sum(grad_branch.astype(jnp.float32), axis=0)
    grad_hidden = right_dot(grad_branch, out_weight)
    gelu_value, gelu_pull = jax.vjp(gelu_tanh, hidden_pre)
    grad_pre = gelu_pull(grad_hidden)[0].astype(jnp.bfloat16)
    grad_fc_weight = left_dot(normed_two_low, grad_pre)
    grad_fc_bias = jnp.sum(grad_pre.astype(jnp.float32), axis=0)
    grad_normed_two = right_dot(grad_pre, fc_weight)
    norm_value, norm_pull = jax.vjp(layer_norm, middle, ln2_gain, ln2_bias)
    grad_mid_norm, grad_ln2_gain, grad_ln2_bias = norm_pull(grad_normed_two)
    grad_middle = grad_final + grad_mid_norm
    grad_attn = (branch_scale * grad_middle).astype(jnp.bfloat16)
    grad_proj_weight = left_dot(attended_low, grad_attn)
    grad_proj_bias = jnp.sum(grad_attn.astype(jnp.float32), axis=0)
    grad_attended = (
        right_dot(grad_attn, proj_weight)
        .astype(jnp.bfloat16)
        .reshape(row_count, span_len, model_width)
    )
    grad_att_heads = grad_attended.reshape(row_count, span_len, head_count, HEAD)
    delta = jnp.sum(grad_att_heads.astype(jnp.float32) * attended_heads, axis=-1)
    delta_t = delta.transpose(0, 2, 1)
    zero_grad = jnp.zeros((row_count, span_len, model_width), jnp.float32)
    query_key_piece = lax.all_gather(keys, "seq", axis=1, tiled=True)
    query_value_piece = lax.all_gather(values, "seq", axis=1, tiled=True)
    query_count = query_key_piece.shape[1]

    def query_update(carry):
        piece_keys = query_key_piece.reshape(row_count, query_count, head_count, HEAD)
        piece_values = query_value_piece.reshape(row_count, query_count, head_count, HEAD)
        scores = (
            jnp.einsum(
                "rqhd,rkhd->rhqk", query_heads, piece_keys, preferred_element_type=jnp.float32
            )
            * scale
        )
        key_pos = jnp.arange(query_count, dtype=jnp.int32)
        allowed = allowed_mask(my_pos, my_segs, key_pos, segments)[:, None]
        probs = jnp.where(allowed, jnp.exp(scores - log_total[..., None]), 0.0)
        grad_probs = jnp.einsum(
            "rqhd,rkhd->rhqk", grad_att_heads, piece_values, preferred_element_type=jnp.float32
        )
        grad_scores = (probs * (grad_probs - delta_t[..., None])).astype(jnp.bfloat16)
        added = jnp.einsum(
            "rhqk,rkhd->rqhd", grad_scores, piece_keys, preferred_element_type=jnp.float32
        )
        return scale * added.reshape(row_count, span_len, model_width)

    grad_queries = lax.cond(jnp.int32(0) > last_pos, lambda carry: carry, query_update, zero_grad)
    stats_lse, stats_delta = (
        lax.all_gather(
            log_total.transpose(0, 2, 1).astype(jnp.bfloat16), "seq", axis=1, tiled=True
        ).astype(jnp.float32),
        lax.all_gather(delta.astype(jnp.bfloat16), "seq", axis=1, tiled=True).astype(delta.dtype),
    )
    query_piece_in = lax.all_gather(queries, "seq", axis=1, tiled=True)
    grad_piece_in = lax.all_gather(grad_attended, "seq", axis=1, tiled=True)
    key_count = query_piece_in.shape[1]

    def key_update(state):
        piece_queries = query_piece_in.reshape(row_count, key_count, head_count, HEAD)
        piece_grads = grad_piece_in.reshape(row_count, key_count, head_count, HEAD)
        scores = (
            jnp.einsum(
                "rqhd,rkhd->rhqk", piece_queries, key_heads, preferred_element_type=jnp.float32
            )
            * scale
        )
        query_pos = jnp.arange(key_count, dtype=jnp.int32)
        allowed = allowed_mask(query_pos, segments, my_pos, my_segs)[:, None]
        piece_lse = stats_lse.transpose(0, 2, 1)
        piece_delta = stats_delta.transpose(0, 2, 1)
        probs = jnp.where(allowed, jnp.exp(scores - piece_lse[..., None]), 0.0)
        add_v = jnp.einsum(
            "rhqk,rqhd->rkhd",
            probs.astype(jnp.bfloat16),
            piece_grads,
            preferred_element_type=jnp.float32,
        )
        grad_probs = jnp.einsum(
            "rqhd,rkhd->rhqk", piece_grads, value_heads, preferred_element_type=jnp.float32
        )
        grad_scores = (probs * (grad_probs - piece_delta[..., None])).astype(jnp.bfloat16)
        add_k = jnp.einsum(
            "rhqk,rqhd->rkhd", grad_scores, piece_queries, preferred_element_type=jnp.float32
        )
        return (
            scale * add_k.reshape(row_count, span_len, model_width),
            add_v.reshape(row_count, span_len, model_width),
        )

    grad_keys, grad_values = lax.cond(
        jnp.int32(0) + key_count <= first_pos,
        lambda state: state,
        key_update,
        (zero_grad, zero_grad),
    )
    grad_projected = (
        jnp.concatenate([grad_queries, grad_keys, grad_values], axis=-1)
        .astype(jnp.bfloat16)
        .reshape(token_count, 3 * model_width)
    )
    grad_qkv_weight = left_dot(normed_low, grad_projected)
    column_sums = jnp.sum(grad_projected.astype(jnp.float32), axis=0)
    grad_qv_bias = jnp.concatenate([column_sums[:model_width], column_sums[2 * model_width :]])
    grad_normed = right_dot(grad_projected, qkv_weight)
    first_value, first_pull = jax.vjp(layer_norm, inputs, ln1_gain, ln1_bias)
    grad_in_norm, grad_ln1_gain, grad_ln1_bias = first_pull(grad_normed)
    input_grad = (grad_middle + grad_in_norm).reshape(row_count, span_len, model_width)
    local_grads = (
        grad_ln1_gain,
        grad_ln1_bias,
        grad_qkv_weight,
        grad_qv_bias,
        grad_proj_weight,
        grad_proj_bias,
        grad_ln2_gain,
        grad_ln2_bias,
        grad_fc_weight,
        grad_fc_bias,
        grad_out_weight,
        grad_out_bias,
    )
    shares = (
        lax.psum_scatter(
            local_grads[0].astype(jnp.bfloat16), "row", scatter_dimension=0, tiled=True
        ).astype(jnp.float32),
        lax.psum_scatter(
            local_grads[1].astype(jnp.bfloat16), "row", scatter_dimension=0, tiled=True
        ).astype(jnp.float32),
        lax.psum_scatter(
            local_grads[2].astype(jnp.bfloat16), "row", scatter_dimension=0, tiled=True
        ).astype(jnp.float32),
        lax.psum_scatter(
            local_grads[3].astype(jnp.bfloat16), "row", scatter_dimension=0, tiled=True
        ).astype(jnp.float32),
        lax.psum_scatter(
            local_grads[4].astype(jnp.bfloat16), "row", scatter_dimension=0, tiled=True
        ).astype(jnp.float32),
        lax.psum_scatter(
            local_grads[5].astype(jnp.bfloat16), "row", scatter_dimension=0, tiled=True
        ).astype(jnp.float32),
        lax.psum_scatter(
            local_grads[6].astype(jnp.bfloat16), "row", scatter_dimension=0, tiled=True
        ).astype(jnp.float32),
        lax.psum_scatter(
            local_grads[7].astype(jnp.bfloat16), "row", scatter_dimension=0, tiled=True
        ).astype(jnp.float32),
        lax.psum_scatter(
            local_grads[8].astype(jnp.bfloat16), "row", scatter_dimension=0, tiled=True
        ).astype(jnp.float32),
        lax.psum_scatter(
            local_grads[9].astype(jnp.bfloat16), "row", scatter_dimension=0, tiled=True
        ).astype(jnp.float32),
        lax.psum_scatter(
            local_grads[10].astype(jnp.bfloat16), "row", scatter_dimension=0, tiled=True
        ).astype(jnp.float32),
        lax.psum_scatter(
            local_grads[11].astype(jnp.bfloat16), "row", scatter_dimension=0, tiled=True
        ).astype(jnp.float32),
    )
    totals = (
        lax.psum(shares[0].astype(jnp.bfloat16), "seq").astype(jnp.float32),
        lax.psum(shares[1].astype(jnp.bfloat16), "seq").astype(jnp.float32),
        lax.psum(shares[2].astype(jnp.bfloat16), "seq").astype(jnp.float32),
        lax.psum(shares[3].astype(jnp.bfloat16), "seq").astype(jnp.float32),
        lax.psum(shares[4].astype(jnp.bfloat16), "seq").astype(jnp.float32),
        lax.psum(shares[5].astype(jnp.bfloat16), "seq").astype(jnp.float32),
        lax.psum(shares[6].astype(jnp.bfloat16), "seq").astype(jnp.float32),
        lax.psum(shares[7].astype(jnp.bfloat16), "seq").astype(jnp.float32),
        lax.psum(shares[8].astype(jnp.bfloat16), "seq").astype(jnp.float32),
        lax.psum(shares[9].astype(jnp.bfloat16), "seq").astype(jnp.float32),
        lax.psum(shares[10].astype(jnp.bfloat16), "seq").astype(jnp.float32),
        lax.psum(shares[11].astype(jnp.bfloat16), "seq").astype(jnp.float32),
    )
    summed = (
        lax.all_gather(totals[0].astype(jnp.bfloat16), "row", axis=0, tiled=True).astype(
            jnp.float32
        ),
        lax.all_gather(totals[1].astype(jnp.bfloat16), "row", axis=0, tiled=True).astype(
            jnp.float32
        ),
        lax.all_gather(totals[2].astype(jnp.bfloat16), "row", axis=0, tiled=True).astype(
            jnp.float32
        ),
        lax.all_gather(totals[3].astype(jnp.bfloat16), "row", axis=0, tiled=True).astype(
            jnp.float32
        ),
        lax.all_gather(totals[4].astype(jnp.bfloat16), "row", axis=0, tiled=True).astype(
            jnp.float32
        ),
        lax.all_gather(totals[5].astype(jnp.bfloat16), "row", axis=0, tiled=True).astype(
            jnp.float32
        ),
        lax.all_gather(totals[6].astype(jnp.bfloat16), "row", axis=0, tiled=True).astype(
            jnp.float32
        ),
        lax.all_gather(totals[7].astype(jnp.bfloat16), "row", axis=0, tiled=True).astype(
            jnp.float32
        ),
        lax.all_gather(totals[8].astype(jnp.bfloat16), "row", axis=0, tiled=True).astype(
            jnp.float32
        ),
        lax.all_gather(totals[9].astype(jnp.bfloat16), "row", axis=0, tiled=True).astype(
            jnp.float32
        ),
        lax.all_gather(totals[10].astype(jnp.bfloat16), "row", axis=0, tiled=True).astype(
            jnp.float32
        ),
        lax.all_gather(totals[11].astype(jnp.bfloat16), "row", axis=0, tiled=True).astype(
            jnp.float32
        ),
    )
    return (
        layer_out,
        input_grad,
        summed[0],
        summed[1],
        summed[2],
        summed[3],
        summed[4],
        summed[5],
        summed[6],
        summed[7],
        summed[8],
        summed[9],
        summed[10],
        summed[11],
    )


def solution(mesh):
    in_specs = (
        P("row", "seq", None),
        P("row", None),
        P(),
        P(),
        P(),
        P(),
        P(),
        P(),
        P(),
        P(),
        P(),
        P(),
        P(),
        P(),
        P("row", "seq", None),
    )
    out_specs = (
        P("row", "seq", None),
        P("row", "seq", None),
        P(),
        P(),
        P(),
        P(),
        P(),
        P(),
        P(),
        P(),
        P(),
        P(),
        P(),
        P(),
    )
    own_rows = mesh.shape["row"] == 8 and mesh.shape["seq"] == 4
    return jax.shard_map(by_rows if own_rows else local, mesh=mesh, in_specs=in_specs, out_specs=out_specs, check_vma=False)
```
